32 devices in a mesh: wide: 8 (over z, core), narrow: 4 (over y, x).
Axes of the slice: x: 2, y: 2, z: 4, core: 2. Of those that a mesh axis runs over, the one named last changes fastest.
Arguments:
- tokens: bfloat16 [8, 1024, 2048], P('narrow', 'wide'), may hold values from -6 to 6
- lengths: int32 [8], P('narrow'), may hold values from 128 to 1024, as said below
- cotangent: bfloat16 [8, 1024, 2048], P('narrow', 'wide'), may hold values from -6 to 6
- first_gain: float32 [2048], replicated, may hold values from 0.5 to 1.5
- proj_in: bfloat16 [2, 2048, 2560], P(None, 'narrow', 'wide'), may hold values from -0.125 to 0.125
- conv_weight: float32 [4, 2560], P(None, 'wide'), may hold values from -3 to 3
- conv_bias: float32 [2560], P('wide'), may hold values from -3 to 3
- rate_weight: bfloat16 [16, 160, 160], P('wide'), may hold values from -0.5 to 0.5
- rate_bias: float32 [2560], P('wide'), may hold values from -4 to 4
- input_weight: bfloat16 [16, 160, 160], P('wide'), may hold values from -0.5 to 0.5
- input_bias: float32 [2560], P('wide'), may hold values from -4 to 4
- decay_param: float32 [2560], P('wide'), may hold values from 4.3 to 9
- proj_out: bfloat16 [2560, 2048], P('wide', 'narrow'), may hold values from -0.3125 to 0.3125
- second_gain: float32 [2048], replicated, may hold values from 0.5 to 1.5
- mlp_in: bfloat16 [2, 2048, 6144], P(None, 'narrow', 'wide'), may hold values from -0.125 to 0.125
- mlp_down: bfloat16 [6144, 2048], P('wide', 'narrow'), may hold values from -0.109375 to 0.109375
Outputs:
- output: bfloat16 [8, 1024, 2048], P('narrow', 'wide')
- grad_tokens: bfloat16 [8, 1024, 2048], P('narrow', 'wide')
- final_state: float32 [8, 2560], P('narrow', 'wide')
- conv_state: float32 [8, 3, 2560], P('narrow', None, 'wide')
- grad_first_gain: float32 [2048], replicated
- grad_proj_in: float32 [2, 2048, 2560], P(None, 'narrow', 'wide')
- grad_conv_weight: float32 [4, 2560], P(None, 'wide')
- grad_conv_bias: float32 [2560], P('wide')
- grad_rate_weight: float32 [16, 160, 160], P('wide')
- grad_rate_bias: float32 [2560], P('wide')
- grad_input_weight: float32 [16, 160, 160], P('wide')
- grad_input_bias: float32 [2560], P('wide')
- grad_decay_param: float32 [2560], P('wide')
- grad_proj_out: float32 [2560, 2048], P('wide', 'narrow')
- grad_second_gain: float32 [2048], replicated
- grad_mlp_in: float32 [2, 2048, 6144], P(None, 'narrow', 'wide')
- grad_mlp_down: float32 [6144, 2048], P('wide', 'narrow')
The draws below stay inside these ranges and needn't reach their ends.
Inputs may be any that keep to these rules, and one draw needn't show every extreme that they name: `lengths`: in every aligned group of 2 consecutive sequences at least one has length 1024.
All inputs are finite; a program needn't handle non-finite values.
Results may differ from the reference program's by a relative error of at most 0.0086.
Values may be sent and summed in bfloat16 or wider, within the bound.
No kernel may reach another device: no remote copies, remote signals or barrier semaphores. Data moves between devices by JAX's collectives and lax.ppermute only.
A program may use at most 320 MiB of HBM per device.

```python
import jax
import jax.numpy as jnp
from jax import lax

D = 2048
R = 2560
FF = 6144
BLOCKS = 16
BW = 160
LEN = 1024
MIN_LEN = 128
SEQ_GRP = 2
SEQS = 8


def draw_lengths(key, part):
    key = jax.random.fold_in(key, 11)
    key_shift, key_len, key_pick = jax.random.split(key, 3)
    group_count = SEQS // SEQ_GRP
    shifts = jax.random.randint(key_shift, (group_count, SEQ_GRP), 0, 4)
    ceiling = jnp.maximum(LEN // jnp.left_shift(1, shifts), MIN_LEN)
    spread = jax.random.randint(key_len, (group_count, SEQ_GRP), 0, 1 << 20)
    drawn = MIN_LEN + spread % (ceiling - MIN_LEN + 1)
    chosen = jax.random.randint(key_pick, (group_count, 1), 0, SEQ_GRP)
    slots = jnp.arange(SEQ_GRP, dtype=jnp.int32)[None, :]
    return jnp.where(slots == chosen, LEN, drawn).astype(jnp.int32).reshape(SEQS)


def steps_of(stream_key, extent, cuts, smallest, high):
    gain, own = 1.0, jax.random.fold_in(stream_key, 6)
    for axis_at, blocks in cuts:
        draws = jnp.exp(jax.random.uniform(jax.random.fold_in(own, axis_at), (blocks,), jnp.float32, smallest / len(cuts), high / len(cuts)))
        gain = gain * jnp.repeat(draws, extent[axis_at] // blocks).reshape([-1 if axis == axis_at else 1 for axis in range(len(extent))])
    return gain


def centred(own_key, dims, scale, bound, cuts=(), kind=jnp.bfloat16):
    gain = steps_of(own_key, dims, cuts, -0.22, 0.18) if cuts else 1.0
    result = jax.random.normal(own_key, dims, jnp.float32) * scale * gain
    return jnp.minimum(jnp.maximum(result, -bound), bound).astype(kind)


def setup_inputs(seed: int = 0) -> dict:
    splits = jax.random.split(jax.random.key(seed), 17)
    tokens = centred(splits[0], (SEQS, LEN, D), 1.0, 6.0, ((0, 4), (1, 8)))
    lengths = draw_lengths(jax.random.fold_in(splits[16], 71), 0)
    cotangent = centred(splits[2], (SEQS, LEN, D), 1.0, 6.0, ((0, 4), (1, 8)))
    first_gain = jnp.clip(1.0 + 0.1 * jax.random.normal(splits[3], (D,), jnp.float32), 0.5, 1.5)
    proj_in = centred(splits[4], (2, D, R), D ** -0.5, 0.125, ((1, 4), (2, 8)))
    conv_weight = centred(splits[5], (4, R), 4 ** -0.5, 3.0, ((1, 8),), jnp.float32)
    conv_bias = centred(splits[6], (R,), 0.5, 3.0, ((0, 8),), jnp.float32)
    rate_weight = centred(splits[7], (BLOCKS, BW, BW), BW ** -0.5, 0.5, ((0, 8),))
    rate_bias = centred(splits[8], (R,), 1.0, 4.0, ((0, 8),), jnp.float32)
    input_weight = centred(splits[9], (BLOCKS, BW, BW), BW ** -0.5, 0.5, ((0, 8),))
    input_bias = centred(splits[10], (R,), 1.0, 4.0, ((0, 8),), jnp.float32)
    decay_param = jnp.clip(4.3 + 4.7 * jax.random.uniform(splits[11], (R,), jnp.float32) ** steps_of(splits[11], (R,), ((0, 8),), -0.2, 0.2), 4.3, 9.0)
    proj_out = centred(splits[12], (R, D), (R // 8) ** -0.5, 0.3125, ((0, 8), (1, 4)))
    second_gain = jnp.clip(1.0 + 0.1 * jax.random.normal(splits[13], (D,), jnp.float32), 0.5, 1.5)
    mlp_in = centred(splits[14], (2, D, FF), D ** -0.5, 0.125, ((1, 4), (2, 8)))
    mlp_down = centred(splits[15], (FF, D), (FF // 2) ** -0.5, 0.109375, ((0, 8), (1, 4)))
    return {"tokens": tokens, "lengths": lengths, "cotangent": cotangent, "first_gain": first_gain, "proj_in": proj_in, "conv_weight": conv_weight, "conv_bias": conv_bias, "rate_weight": rate_weight, "rate_bias": rate_bias, "input_weight": input_weight, "input_bias": input_bias, "decay_param": decay_param, "proj_out": proj_out, "second_gain": second_gain, "mlp_in": mlp_in, "mlp_down": mlp_down}


decay_scale = 8.0
norm_eps = 1e-06

@jax.custom_vjp
def low(v):
    return lax.optimization_barrier(v.astype(jnp.bfloat16)).astype(jnp.float32)

@jax.custom_vjp
def low_back(v):
    return v

def low_keep(v):
    return (low(v), None)

def low_pass(kept, grad):
    return (grad,)

def back_keep(v):
    return (v, None)

def back_low(kept, grad):
    return (low(grad),)
low.defvjp(low_keep, low_pass)
low_back.defvjp(back_keep, back_low)

def rms_scale(values, norm_gain):
    return values * lax.rsqrt(lax.optimization_barrier(jnp.mean(values * values, axis=-1, keepdims=True)) + norm_eps) * norm_gain

def lagged(values, offset):
    return jnp.pad(values, ((0, 0), (offset, 0), (0, 0)))[:, :values.shape[1]]

def linear_combine(earlier, latter):
    return (earlier[0] * latter[0], latter[0] * earlier[1] + latter[1])

def mixer_core(y_branch, x_branch, conv_weight, conv_bias, rate_weight, rate_bias, input_weight, input_bias, decay_param, mask_f, lengths):
    convolved = conv_bias + conv_weight[0] * x_branch
    for offset in range(1, 4):
        convolved = convolved + conv_weight[offset] * lagged(x_branch, offset)
    seq_count, seq_len, channels = convolved.shape
    block_count = rate_weight.shape[0]
    block_width = rate_weight.shape[1]
    blocked = convolved.reshape(seq_count, seq_len, block_count, block_width)
    rate_pre = jnp.einsum('stnc,ncd->stnd', blocked, rate_weight, precision=lax.Precision.HIGHEST)
    in_pre = jnp.einsum('stnc,ncd->stnd', blocked, input_weight, precision=lax.Precision.HIGHEST)
    rate_gate = jax.nn.sigmoid(rate_pre.reshape(seq_count, seq_len, channels) + rate_bias)
    in_gate = jax.nn.sigmoid(in_pre.reshape(seq_count, seq_len, channels) + input_bias)
    log_decay = -decay_scale * jax.nn.softplus(-decay_param) * rate_gate
    drive_term = jnp.sqrt(-jnp.expm1(2.0 * log_decay)) * in_gate * convolved * mask_f
    decay_rate = jnp.exp(log_decay * mask_f)
    carried, states = lax.associative_scan(linear_combine, (decay_rate, drive_term), axis=1)
    mixer_out = jax.nn.gelu(y_branch) * states
    positions = (lengths[:, None] - 3 + jnp.arange(3, dtype=jnp.int32)[None, :]).astype(jnp.int32)
    conv_state = jnp.take_along_axis(x_branch, positions[:, :, None], axis=1)
    return (mixer_out, states[:, -1], conv_state)

def highest(left, right):
    return jnp.dot(left, right, precision=lax.Precision.HIGHEST)

def residual_block(params, tokens, mask_f, lengths):
    first_gain, proj_in, conv_weight, conv_bias, rate_weight, rate_bias, input_weight, input_bias, decay_param, proj_out, second_gain, mlp_in, mlp_down = params
    norm_in = low(rms_scale(tokens, first_gain))
    branch_y = low_back(highest(norm_in, proj_in[0]))
    branch_x = low_back(highest(norm_in, proj_in[1]))
    mixer_out, final_state, conv_state = mixer_core(branch_y, branch_x, conv_weight, conv_bias, rate_weight, rate_bias, input_weight, input_bias, decay_param, mask_f, lengths)
    mixer_out = low(mixer_out)
    resid = tokens + low_back(highest(mixer_out, proj_out))
    norm_mid = low(rms_scale(resid, second_gain))
    gate_pre = low_back(highest(norm_mid, mlp_in[0]))
    up_pre = low_back(highest(norm_mid, mlp_in[1]))
    hidden = low(jax.nn.gelu(gate_pre) * up_pre)
    return (resid + low_back(highest(hidden, mlp_down)), (final_state, conv_state))

def reference(tokens, lengths, cotangent, first_gain, proj_in, conv_weight, conv_bias, rate_weight, rate_bias, input_weight, input_bias, decay_param, proj_out, second_gain, mlp_in, mlp_down):
    params = tuple((entry.astype(jnp.float32) for entry in (first_gain, proj_in, conv_weight, conv_bias, rate_weight, rate_bias, input_weight, input_bias, decay_param, proj_out, second_gain, mlp_in, mlp_down)))

    def grouped(values):
        return values.reshape((SEQS // SEQ_GRP, SEQ_GRP) + values.shape[1:])

    def group_step(totals, inputs_now):
        group_tokens, group_cot, group_len = inputs_now
        mask_f = (jnp.arange(LEN, dtype=jnp.int32)[None, :] < group_len[:, None]).astype(jnp.float32)[:, :, None]

        def forward(params_in, tokens_in):
            return residual_block(params_in, tokens_in, mask_f, group_len)
        output, backward, states = jax.vjp(forward, params, group_tokens.astype(jnp.float32), has_aux=True)
        grad_params, grad_in = backward(group_cot.astype(jnp.float32) * mask_f)
        totals = jax.tree.map(jnp.add, totals, grad_params)
        return (totals, (output.astype(jnp.bfloat16), grad_in.astype(jnp.bfloat16), states[0], states[1]))
    initial = jax.tree.map(jnp.zeros_like, params)
    totals, (outputs, grad_rows, finals, conv_states) = lax.scan(group_step, initial, (grouped(tokens), grouped(cotangent), grouped(lengths)))
    return (outputs.reshape(SEQS, LEN, D), grad_rows.reshape(SEQS, LEN, D), finals.reshape(SEQS, R), conv_states.reshape(SEQS, 3, R), totals[0], totals[1], totals[2], totals[3], totals[4], totals[5], totals[6], totals[7], totals[8], totals[9], totals[10], totals[11], totals[12])
```

```python
from functools import partial

import jax
import jax.numpy as jnp
from jax import lax
from jax.experimental import pallas as pl
from jax.experimental.pallas import tpu as pltpu
from jax.sharding import PartitionSpec as P

decay_scale = 8.0
norm_eps = 1e-06
gelu_in = 0.7978845608028654
gelu_cube = 0.044715
f32 = jnp.float32
bf16 = jnp.bfloat16


def gelu_tanh(v):
    return jnp.tanh(gelu_in * (v + gelu_cube * v * v * v))


def gelu_pair(v):
    t = gelu_tanh(v)
    half = 0.5 * (1.0 + t)
    slope = half + 0.5 * v * (1.0 - t * t) * (gelu_in + (3.0 * gelu_in * gelu_cube) * v * v)
    return v * half, slope


def one_minus_exp(v, decay):
    series = 1.0 - v * (1.0 / 7.0)
    for order in (6.0, 5.0, 4.0, 3.0, 2.0):
        series = 1.0 - v * (1.0 / order) * series
    return jnp.where(v < 0.3, v * series, 1.0 - decay * decay)


def split_dot(values, weight):
    high = values.astype(bf16)
    low = (values - high.astype(f32)).astype(bf16)
    return jnp.dot(high, weight, preferred_element_type=f32) + jnp.dot(
        low, weight, preferred_element_type=f32
    )


def tile_scan(decay, drive, backward):
    rows, channels = decay.shape
    a = decay.reshape(rows // 8, 8, channels)
    b = drive.reshape(rows // 8, 8, channels)
    row = lax.broadcasted_iota(jnp.int32, (1, 8, channels), 1)
    for step in (1, 2, 4):
        if backward:
            keep, shift = row < 8 - step, 8 - step
        else:
            keep, shift = row >= step, step
        a_moved = jnp.where(keep, pltpu.roll(a, shift, 1), 1.0)
        b_moved = jnp.where(keep, pltpu.roll(b, shift, 1), 0.0)
        b = b + a * b_moved
        a = a * a_moved
    return a, b


def mixer_forward_kernel(
    place, lengths, pre, conv_weight, conv_bias, gate_weight, gate_bias, rate_scale,
    mixed, conv_out, rate_out, in_out, states_out, final_state, conv_state, x_tail, carry,
):
    chunk = pl.program_id(0)
    _, _, _, seq_count, local_len, channels = pre.shape

    @pl.when(chunk == 0)
    def _():
        x_tail[...] = jnp.zeros_like(x_tail)
        carry[...] = jnp.zeros_like(carry)

    convs = []
    for seq in range(seq_count):
        x = pre[0, 1, 0, seq]
        extended = jnp.concatenate((x_tail[seq], x), axis=0)
        conv = conv_bias[...] + conv_weight[0:1] * x
        for lag in range(1, 4):
            conv = conv + conv_weight[lag : lag + 1] * extended[8 - lag : 8 - lag + local_len]
        x_tail[seq] = x[local_len - 8 :]
        convs.append(conv)
        for tap in range(3):
            position = lengths[seq] - 3 + tap

            @pl.when(position // local_len == chunk)
            def _(seq=seq, tap=tap, position=position):
                conv_state[seq, tap : tap + 1] = pre[
                    0, 1, 0, seq, pl.ds(lax.rem(position, local_len), 1)
                ]

    conv_all = jnp.concatenate(convs, axis=0)
    gates = jax.nn.sigmoid(split_dot(conv_all, gate_weight[...]) + gate_bias[...])
    for seq in range(seq_count):
        rows = slice(seq * local_len, (seq + 1) * local_len)
        conv = convs[seq]
        rate_gate = gates[rows, :channels]
        in_gate = gates[rows, channels:]
        step_log = rate_scale[...] * rate_gate
        decay = jnp.exp(-step_log)
        root = jnp.sqrt(one_minus_exp(2.0 * step_log, decay))
        position = chunk * local_len + lax.broadcasted_iota(jnp.int32, (local_len, 1), 0)
        live = position < lengths[seq]
        drive = jnp.where(live, root * in_gate * conv, 0.0)
        a, b = tile_scan(jnp.where(live, decay, 1.0), drive, False)
        last = carry[seq]
        gated, _ = gelu_pair(pre[0, 0, 0, seq])
        tiles = []
        for tile in range(local_len // 8):
            tiles.append(b[tile] + a[tile] * last)
            last = tiles[-1][7:8]
        states = jnp.concatenate(tiles, axis=0)
        states_out[0, 0, seq] = states
        mixed[0, 0, seq] = (gated * states).astype(bf16)
        carry[seq] = last
        final_state[seq : seq + 1] = last
        conv_out[0, 0, seq] = conv
        rate_out[0, 0, seq] = rate_gate
        in_out[0, 0, seq] = in_gate


def mixer_backward_kernel(
    place, lengths, pre, back, conv_in, rate_in, in_in, states_in, conv_weight, gate_back, rate_scale,
    y_grad, x_grad, sums, gate_sums, carry, grad_head,
):
    step = pl.program_id(0)
    chunk = pl.num_programs(0) - 1 - step
    _, _, _, seq_count, local_len, channels = pre.shape

    @pl.when(step == 0)
    def _():
        carry[...] = jnp.zeros_like(carry)
        grad_head[...] = jnp.zeros_like(grad_head)
        sums[...] = jnp.zeros_like(sums)
        gate_sums[...] = jnp.zeros_like(gate_sums)

    rate_pre, in_pre, direct = [], [], []
    decay_sum = jnp.zeros((1, channels), f32)
    for seq in range(seq_count):
        position = chunk * local_len + lax.broadcasted_iota(jnp.int32, (local_len, 1), 0)
        live = position < lengths[seq]
        rate_gate = rate_in[0, 0, seq]
        in_gate = in_in[0, 0, seq]
        conv = conv_in[0, 0, seq]
        states = states_in[0, 0, seq]
        mixer_grad = back[0, 0, seq]
        gated, slope = gelu_pair(pre[0, 0, 0, seq])
        step_log = rate_scale[...] * rate_gate
        decay_raw = jnp.exp(-step_log)
        decay = jnp.where(live, decay_raw, 1.0)
        y_grad[0, 0, seq] = (mixer_grad * states * slope).astype(bf16)
        source = mixer_grad * gated
        a, b = tile_scan(decay, decay * source, True)
        following = carry[seq]
        tiles = []
        for tile in reversed(range(local_len // 8)):
            passed = b[tile] + a[tile] * following
            tiles.append(jnp.concatenate((passed[1:], following), axis=0))
            following = passed[0:1]
        carry[seq] = following
        adjoint = source + jnp.concatenate(tiles[::-1], axis=0)
        adjoint = jnp.where(live, adjoint, 0.0)
        square = one_minus_exp(2.0 * step_log, decay_raw)
        inverse_root = lax.rsqrt(square)
        root = square * inverse_root
        gated_conv = in_gate * conv
        logd_grad = adjoint * (
            states - root * gated_conv - gated_conv * decay_raw * decay_raw * inverse_root
        )
        rate_part = logd_grad * rate_gate
        decay_sum = decay_sum + jnp.sum(rate_part, axis=0, keepdims=True)
        rate_pre.append(-rate_scale[...] * rate_part * (1.0 - rate_gate))
        through = adjoint * root
        in_pre.append(through * gated_conv * (1.0 - in_gate))
        direct.append(through * in_gate)
    rate_all = jnp.concatenate(rate_pre, axis=0)
    in_all = jnp.concatenate(in_pre, axis=0)
    both = jnp.concatenate((rate_all, in_all), axis=1)
    conv_grad = jnp.concatenate(direct, axis=0) + split_dot(both, gate_back[...])
    conv_all = jnp.concatenate([conv_in[0, 0, seq] for seq in range(seq_count)], axis=0)
    gate_sums[...] += lax.dot_general(
        conv_all.astype(bf16), both.astype(bf16), (((0,), (0,)), ((), ())), preferred_element_type=f32
    )
    tap_sums = [jnp.zeros((1, channels), f32) for _ in range(4)]
    for seq in range(seq_count):
        part = conv_grad[seq * local_len : (seq + 1) * local_len]
        extended = jnp.concatenate((part, grad_head[seq]), axis=0)
        x = pre[0, 1, 0, seq]
        total = conv_weight[0:1] * part
        tap_sums[0] = tap_sums[0] + jnp.sum(part * x, axis=0, keepdims=True)
        for lag in range(1, 4):
            moved = extended[lag : lag + local_len]
            total = total + conv_weight[lag : lag + 1] * moved
            tap_sums[lag] = tap_sums[lag] + jnp.sum(moved * x, axis=0, keepdims=True)
        x_grad[0, 0, seq] = total.astype(bf16)
        grad_head[seq] = part[:8]
    sums[0:1] += jnp.sum(rate_all, axis=0, keepdims=True)
    sums[1:2] += jnp.sum(in_all, axis=0, keepdims=True)
    sums[2:3] += decay_sum
    sums[3:4] += jnp.sum(conv_grad, axis=0, keepdims=True)
    for lag in range(4):
        sums[4 + lag : 5 + lag] += tap_sums[lag]


def chunk_place(chunk, place, chips):
    return lax.rem(place[0] - chunk // 2 + chips, chips), lax.rem(chunk + place[1], 2)


def mixer_forward(pre, lengths, place, conv_weight, conv_bias, gate_weight, gate_bias, rate_scale):
    chips, _, _, seq_count, local_len, channels = pre.shape

    def in_map(chunk, place, lengths):
        chip, core = chunk_place(chunk, place, chips)
        return (chip, 0, core, 0, 0, 0)

    def out_map(chunk, place, lengths):
        chip, core = chunk_place(chunk, place, chips)
        return (chip, core, 0, 0, 0)

    def whole(shape):
        return pl.BlockSpec(shape, lambda chunk, place, lengths: (0,) * len(shape))

    block = pl.BlockSpec((1, 1, seq_count, local_len, channels), out_map)
    full = (chips, 2, seq_count, local_len, channels)
    rows = chips * 2 * seq_count * local_len
    return pl.pallas_call(
        mixer_forward_kernel,
        grid_spec=pltpu.PrefetchScalarGridSpec(
            num_scalar_prefetch=2,
            grid=(2 * chips,),
            in_specs=[
                pl.BlockSpec((1, 2, 1, seq_count, local_len, channels), in_map),
                whole(conv_weight.shape),
                whole(conv_bias.shape),
                whole(gate_weight.shape),
                whole(gate_bias.shape),
                whole(rate_scale.shape),
            ],
            out_specs=[block] * 5 + [whole((seq_count, channels)), whole((seq_count, 3, channels))],
            scratch_shapes=[
                pltpu.VMEM((seq_count, 8, channels), f32),
                pltpu.VMEM((seq_count, 1, channels), f32),
            ],
        ),
        out_shape=[jax.ShapeDtypeStruct(full, bf16)]
        + [jax.ShapeDtypeStruct(full, f32)] * 4
        + [
            jax.ShapeDtypeStruct((seq_count, channels), f32),
            jax.ShapeDtypeStruct((seq_count, 3, channels), f32),
        ],
        compiler_params=pltpu.CompilerParams(vmem_limit_bytes=32 << 20),
        cost_estimate=pl.CostEstimate(
            flops=rows * channels * 200, bytes_accessed=rows * channels * 26, transcendentals=0
        ),
        name="mixer_forward",
    )(place, lengths, pre, conv_weight, conv_bias, gate_weight, gate_bias, rate_scale)


def mixer_backward(pre, back, saved, lengths, place, conv_weight, gate_back, rate_scale):
    chips, _, _, seq_count, local_len, channels = pre.shape

    def in_map(step, place, lengths):
        chip, core = chunk_place(2 * chips - 1 - step, place, chips)
        return (chip, 0, core, 0, 0, 0)

    def out_map(step, place, lengths):
        chip, core = chunk_place(2 * chips - 1 - step, place, chips)
        return (chip, core, 0, 0, 0)

    def whole(shape):
        return pl.BlockSpec(shape, lambda step, place, lengths: (0,) * len(shape))

    block = pl.BlockSpec((1, 1, seq_count, local_len, channels), out_map)
    full = (chips, 2, seq_count, local_len, channels)
    rows = chips * 2 * seq_count * local_len
    return pl.pallas_call(
        mixer_backward_kernel,
        grid_spec=pltpu.PrefetchScalarGridSpec(
            num_scalar_prefetch=2,
            grid=(2 * chips,),
            in_specs=[pl.BlockSpec((1, 2, 1, seq_count, local_len, channels), in_map)]
            + [block] * 5
            + [whole(conv_weight.shape), whole(gate_back.shape), whole(rate_scale.shape)],
            out_specs=[block, block, whole((8, channels)), whole((channels, 2 * channels))],
            scratch_shapes=[
                pltpu.VMEM((seq_count, 1, channels), f32),
                pltpu.VMEM((seq_count, 8, channels), f32),
            ],
        ),
        out_shape=[
            jax.ShapeDtypeStruct(full, bf16),
            jax.ShapeDtypeStruct(full, bf16),
            jax.ShapeDtypeStruct((8, channels), f32),
            jax.ShapeDtypeStruct((channels, 2 * channels), f32),
        ],
        compiler_params=pltpu.CompilerParams(vmem_limit_bytes=32 << 20),
        cost_estimate=pl.CostEstimate(
            flops=rows * channels * 300, bytes_accessed=rows * channels * 32, transcendentals=0
        ),
        name="mixer_backward",
    )(place, lengths, pre, back, *saved, conv_weight, gate_back, rate_scale)


def block_diagonal(weight):
    count, width, _ = weight.shape
    rows = [
        jnp.pad(weight[at], ((0, 0), (at * width, (count - 1 - at) * width))) for at in range(count)
    ]
    return jnp.concatenate(rows, axis=0)


def diagonal_blocks(values, count):
    width = values.shape[0] // count
    return jnp.stack(
        [values[at * width : (at + 1) * width, at * width : (at + 1) * width] for at in range(count)]
    )


def narrow_whole(weight):
    return lax.all_gather(weight, "narrow", axis=1, tiled=True)


def narrow_sum(grad):
    return lax.psum_scatter(
        grad.astype(bf16), "narrow", scatter_dimension=1, tiled=True
    ).astype(f32)


def swap_cores(values, wide):
    return lax.ppermute(values, "wide", [(at, at ^ 1) for at in range(wide)])


def next_chip(values, wide):
    return lax.ppermute(values, "wide", [(at, (at + 2) % wide) for at in range(wide)])


def gather_ring(rows, wide):
    held, blocks = rows, []
    for hop in range(wide // 2):
        if hop:
            held = next_chip(held, wide)
        blocks.append(jnp.concatenate((held, swap_cores(held, wide)), axis=0))
    return blocks


def ring_order(chips):
    return list(range(1, chips)) + [0]


class RingSum:
    def __init__(self, wide):
        self.wide = wide
        self.moving = None

    def add(self, block, hop):
        mine, other = jnp.split(block, 2, axis=0)
        total = mine + swap_cores(other.astype(bf16), self.wide).astype(f32)
        if self.moving is not None:
            total = total + self.moving.astype(f32)
        if hop:
            self.moving = next_chip(total.astype(bf16), self.wide)
        return total


def norm_forward(values, gain):
    scale = lax.rsqrt(jnp.mean(values * values, axis=-1, keepdims=True) + norm_eps)
    return scale, (values * scale * gain).astype(bf16)


def norm_backward(values, scale, gain, grad):
    unit = values * scale
    scaled = grad * gain
    back = scale * (scaled - unit * jnp.mean(scaled * unit, axis=-1, keepdims=True))
    return back, jnp.sum(grad * unit, axis=0)


def dot(left, right):
    return jnp.dot(left, right, preferred_element_type=f32)


def dot_nt(left, right):
    return lax.dot_general(left, right, (((1,), (1,)), ((), ())), preferred_element_type=f32)


def dot_tn(left, right):
    return lax.dot_general(left, right, (((0,), (0,)), ((), ())), preferred_element_type=f32)


def body(
    tokens, lengths, cotangent, first_gain, proj_in, conv_weight, conv_bias, rate_weight, rate_bias,
    input_weight, input_bias, decay_param, proj_out, second_gain, mlp_in, mlp_down,
):
    seq_count, local_len, width = tokens.shape
    wide = lax.axis_size("wide")
    chips = wide // 2
    me = lax.axis_index("wide")
    place = jnp.stack((me // 2, me % 2)).astype(jnp.int32)
    channels = proj_in.shape[2]
    gate_count = rate_weight.shape[0]
    block_shape = (2, seq_count, local_len, channels)
    order = ring_order(chips)
    positions = me * local_len + jnp.arange(local_len, dtype=jnp.int32)
    mask = (positions[None, :] < lengths[:, None]).astype(f32).reshape(-1, 1)

    tokens_f = tokens.reshape(-1, width).astype(f32)
    scale_one, norm_in = norm_forward(tokens_f, first_gain)
    out_grad = cotangent.reshape(-1, width).astype(f32) * mask

    whole_in = narrow_whole(proj_in)
    rows_first = gather_ring(norm_in, wide)
    whole_out = narrow_whole(proj_out)
    whole_mlp_in = narrow_whole(mlp_in)
    whole_down = narrow_whole(mlp_down)
    rows_back = gather_ring(out_grad.astype(bf16), wide)

    pre = jnp.stack(
        [
            jnp.stack([dot(rows, whole_in[kind]).reshape(block_shape) for kind in range(2)])
            for rows in rows_first
        ]
    )
    gate_weight = jnp.concatenate((block_diagonal(rate_weight), block_diagonal(input_weight)), axis=1)
    gate_bias = jnp.concatenate((rate_bias, input_bias))[None, :]
    rate_scale = (decay_scale * jax.nn.softplus(-decay_param))[None, :]
    mixed, conv, rate_gate, in_gate, states, final_state, conv_state = mixer_forward(
        pre, lengths, place, conv_weight, conv_bias[None, :], gate_weight, gate_bias, rate_scale
    )
    mixed_rows = mixed.reshape(chips, -1, channels)
    ring = RingSum(wide)
    for hop in order:
        mix_sum = ring.add(dot(mixed_rows[hop], whole_out), hop)
    resid = tokens_f + mix_sum

    scale_two, norm_mid = norm_forward(resid, second_gain)
    rows_second = gather_ring(norm_mid, wide)
    hidden, gate_grads, up_grads = {}, {}, {}
    ring_mid, ring_out = RingSum(wide), RingSum(wide)
    for hop in order:
        gate_pre = dot(rows_second[hop], whole_mlp_in[0])
        up_pre = dot(rows_second[hop], whole_mlp_in[1])
        hidden_grad = dot_nt(rows_back[hop], whole_down)
        gated, slope = gelu_pair(gate_pre)
        hidden[hop] = (gated * up_pre).astype(bf16)
        gate_grads[hop] = (hidden_grad * up_pre * slope).astype(bf16)
        up_grads[hop] = (hidden_grad * gated).astype(bf16)
        mid_sum = ring_mid.add(
            dot_nt(gate_grads[hop], whole_mlp_in[0]) + dot_nt(up_grads[hop], whole_mlp_in[1]), hop
        )
    for hop in order:
        mlp_sum = ring_out.add(dot(hidden[hop], whole_down), hop)
    output = (resid + mlp_sum).astype(bf16)

    from_norm, gain_two = norm_backward(resid, scale_two, second_gain, mid_sum)
    resid_grad = out_grad + from_norm
    rows_resid = gather_ring(resid_grad.astype(bf16), wide)
    all_second = jnp.concatenate(rows_second, axis=0)
    all_back = jnp.concatenate(rows_back, axis=0)
    all_resid = jnp.concatenate(rows_resid, axis=0)

    def joined(parts):
        return jnp.concatenate([parts[hop] for hop in range(chips)], axis=0)

    grad_mlp_in = narrow_sum(
        jnp.stack((dot_tn(all_second, joined(gate_grads)), dot_tn(all_second, joined(up_grads))))
    )
    grad_mlp_down = narrow_sum(dot_tn(joined(hidden), all_back))
    grad_proj_out = narrow_sum(dot_tn(mixed.reshape(-1, channels), all_resid))

    back = jnp.stack([dot_nt(rows, whole_out).reshape(block_shape) for rows in rows_resid])
    y_grad, x_grad, sums, gate_sums = mixer_backward(
        pre, back, (conv, rate_gate, in_gate, states), lengths, place, conv_weight,
        gate_weight.T, rate_scale,
    )
    y_rows = y_grad.reshape(chips, -1, channels)
    x_rows = x_grad.reshape(chips, -1, channels)
    ring_in = RingSum(wide)
    for hop in order:
        in_sum = ring_in.add(dot_nt(y_rows[hop], whole_in[0]) + dot_nt(x_rows[hop], whole_in[1]), hop)
    all_first = jnp.concatenate(rows_first, axis=0)
    grad_proj_in = narrow_sum(
        jnp.stack(
            (
                dot_tn(all_first, y_grad.reshape(-1, channels)),
                dot_tn(all_first, x_grad.reshape(-1, channels)),
            )
        )
    )
    sums = lax.psum(
        (
            sums,
            diagonal_blocks(gate_sums[:, :channels], gate_count),
            diagonal_blocks(gate_sums[:, channels:], gate_count),
        ),
        "narrow",
    )
    sums, grad_rate_weight, grad_input_weight = sums
    from_norm, gain_one = norm_backward(tokens_f, scale_one, first_gain, in_sum)
    grad_tokens = (resid_grad + from_norm).astype(bf16)
    gains = lax.psum((gain_one, gain_two), ("wide", "narrow"))
    return (
        output.reshape(tokens.shape),
        grad_tokens.reshape(tokens.shape),
        final_state,
        conv_state,
        gains[0],
        grad_proj_in,
        sums[4:8],
        sums[3],
        grad_rate_weight,
        sums[0],
        grad_input_weight,
        sums[1],
        sums[2] * decay_scale * jax.nn.sigmoid(-decay_param),
        grad_proj_out,
        gains[1],
        grad_mlp_in,
        grad_mlp_down,
    )


def solution(mesh):
    return jax.shard_map(
        body,
        mesh=mesh,
        in_specs=(
            P("narrow", "wide", None),
            P("narrow"),
            P("narrow", "wide", None),
            P(),
            P(None, "narrow", "wide"),
            P(None, "wide"),
            P("wide"),
            P("wide", None, None),
            P("wide"),
            P("wide", None, None),
            P("wide"),
            P("wide"),
            P("wide", "narrow"),
            P(),
            P(None, "narrow", "wide"),
            P("wide", "narrow"),
        ),
        out_specs=(
            P("narrow", "wide", None),
            P("narrow", "wide", None),
            P("narrow", "wide"),
            P("narrow", None, "wide"),
            P(),
            P(None, "narrow", "wide"),
            P(None, "wide"),
            P("wide"),
            P("wide", None, None),
            P("wide"),
            P("wide", None, None),
            P("wide"),
            P("wide"),
            P("wide", "narrow"),
            P(),
            P(None, "narrow", "wide"),
            P("wide", "narrow"),
        ),
        check_vma=False,
    )
```

```python
from functools import partial

import jax
import jax.numpy as jnp
from jax import lax
from jax.experimental import pallas as pl
from jax.experimental.pallas import tpu as pltpu
from jax.sharding import PartitionSpec as P

decay_scale = 8.0
norm_eps = 1e-06
gelu_in = 0.7978845608028654
gelu_cube = 0.044715
f32 = jnp.float32
bf16 = jnp.bfloat16
kernel_cost = pl.CostEstimate(flops=1, bytes_accessed=1, transcendentals=0)


def gelu_tanh(v):
    return jnp.tanh(gelu_in * (v + gelu_cube * v * v * v))


def gelu_pair(v):
    t = gelu_tanh(v)
    half = 0.5 * (1.0 + t)
    slope = half + 0.5 * v * (1.0 - t * t) * (gelu_in + (3.0 * gelu_in * gelu_cube) * v * v)
    return v * half, slope


def one_minus_exp(v, decay):
    series = 1.0 - v * (1.0 / 7.0)
    for order in (6.0, 5.0, 4.0, 3.0, 2.0):
        series = 1.0 - v * (1.0 / order) * series
    return jnp.where(v < 0.3, v * series, 1.0 - decay * decay)


def gate_tiles(channels, block_width, tile):
    tiles, offset = [], 0
    for start in range(0, channels, tile):
        stop = min(start + tile, channels)
        low = start // block_width * block_width // 128 * 128
        high = min(-(-((stop - 1) // block_width + 1) * block_width // 128) * 128, channels)
        tiles.append((start, stop, low, high, offset))
        offset += high - low
    return tiles


def split_rows(values):
    high = values.astype(bf16)
    return jnp.concatenate((high, (values - high.astype(f32)).astype(bf16)), axis=0)


def joined_dot(halves, weight):
    both = jnp.dot(halves, weight, preferred_element_type=f32)
    rows = both.shape[0] // 2
    return both[:rows] + both[rows:]


def tile_scan(decay, drive, backward):
    rows, channels = decay.shape
    a = decay.reshape(rows // 8, 8, channels)
    b = drive.reshape(rows // 8, 8, channels)
    row = lax.broadcasted_iota(jnp.int32, (1, 8, channels), 1)
    for step in (1, 2, 4):
        if backward:
            keep, shift = row < 8 - step, 8 - step
        else:
            keep, shift = row >= step, step
        a_moved = jnp.where(keep, pltpu.roll(a, shift, 1), 1.0)
        b_moved = jnp.where(keep, pltpu.roll(b, shift, 1), 0.0)
        b = b + a * b_moved
        a = a * a_moved
    return a, b


def mixer_forward_kernel(
    chips, block_width, place, lengths, *refs
):
    pre_refs, refs = refs[:chips], refs[chips:]
    conv_weight, conv_bias, gate_weight, gate_bias, rate_scale = refs[:5]
    mixed, conv_out, rate_out, in_out, states_out, final_state, conv_state = refs[5:12]
    pre_now, x_tail, carry = refs[12:]
    chunk = pl.program_id(0)
    seq_count, local_len, channels = pre_now.shape
    channels //= 2
    pick_block(chunk, place, chips, (pre_refs, pre_now))

    @pl.when(chunk == 0)
    def _():
        x_tail[...] = jnp.zeros_like(x_tail)
        carry[...] = jnp.zeros_like(carry)

    convs = []
    for seq in range(seq_count):
        x = pre_now[seq, :, channels:]
        extended = jnp.concatenate((x_tail[seq], x), axis=0)
        conv = conv_bias[...] + conv_weight[0:1] * x
        for lag in range(1, 4):
            conv = conv + conv_weight[lag : lag + 1] * extended[8 - lag : 8 - lag + local_len]
        x_tail[seq] = x[local_len - 8 :]
        convs.append(conv)
        for tap in range(3):
            position = lengths[seq] - 3 + tap

            @pl.when(position // local_len == chunk)
            def _(seq=seq, tap=tap, position=position):
                conv_state[seq, tap : tap + 1] = pre_now[
                    seq, pl.ds(lax.rem(position, local_len), 1), channels:
                ]

    conv_all = jnp.concatenate(convs, axis=0)
    parted = split_rows(conv_all)
    rate_parts, in_parts = [], []
    for start, stop, low, high, at in gate_tiles(channels, block_width, 128):
        both = joined_dot(parted[:, low:high], gate_weight[at : at + high - low])
        rate_parts.append(both[:, : stop - start])
        in_parts.append(both[:, 128 : 128 + stop - start])
    rate_all = jax.nn.sigmoid(jnp.concatenate(rate_parts, axis=1) + gate_bias[0:1])
    in_all = jax.nn.sigmoid(jnp.concatenate(in_parts, axis=1) + gate_bias[1:2])
    for seq in range(seq_count):
        rows = slice(seq * local_len, (seq + 1) * local_len)
        conv = convs[seq]
        rate_gate = rate_all[rows]
        in_gate = in_all[rows]
        step_log = rate_scale[...] * rate_gate
        decay = jnp.exp(-step_log)
        root = jnp.sqrt(one_minus_exp(2.0 * step_log, decay))
        position = chunk * local_len + lax.broadcasted_iota(jnp.int32, (local_len, 1), 0)
        live = position < lengths[seq]
        drive = jnp.where(live, root * in_gate * conv, 0.0)
        a, b = tile_scan(jnp.where(live, decay, 1.0), drive, False)
        last = carry[seq]
        gated, _ = gelu_pair(pre_now[seq, :, :channels])
        tiles = []
        for tile in range(local_len // 8):
            tiles.append(b[tile] + a[tile] * last)
            last = tiles[-1][7:8]
        states = jnp.concatenate(tiles, axis=0)
        states_out[0, 0, seq] = states
        mixed[0, 0, seq] = (gated * states).astype(bf16)
        carry[seq] = last
        final_state[seq : seq + 1] = last
        conv_out[0, 0, seq] = conv
        rate_out[0, 0, seq] = rate_gate
        in_out[0, 0, seq] = in_gate


def mixer_backward_kernel(
    chips, block_width, place, lengths, *refs
):
    pre_refs, back_refs, refs = refs[:chips], refs[chips : 2 * chips], refs[2 * chips :]
    conv_in, rate_in, in_in, states_in, conv_weight, gate_back, rate_scale = refs[:7]
    grads, sums, gate_sums = refs[7:10]
    pre_now, back_now, carry, grad_head = refs[10:]
    step = pl.program_id(0)
    chunk = pl.num_programs(0) - 1 - step
    seq_count, local_len, channels = back_now.shape
    pick_block(chunk, place, chips, (pre_refs, pre_now), (back_refs, back_now))

    @pl.when(step == 0)
    def _():
        carry[...] = jnp.zeros_like(carry)
        grad_head[...] = jnp.zeros_like(grad_head)
        sums[...] = jnp.zeros_like(sums)
        gate_sums[...] = jnp.zeros_like(gate_sums)

    rate_pre, in_pre, direct = [], [], []
    decay_sum = jnp.zeros((1, channels), f32)
    for seq in range(seq_count):
        position = chunk * local_len + lax.broadcasted_iota(jnp.int32, (local_len, 1), 0)
        live = position < lengths[seq]
        rate_gate = rate_in[0, 0, seq]
        in_gate = in_in[0, 0, seq]
        conv = conv_in[0, 0, seq]
        states = states_in[0, 0, seq]
        mixer_grad = back_now[seq]
        gated, slope = gelu_pair(pre_now[seq, :, :channels])
        step_log = rate_scale[...] * rate_gate
        decay_raw = jnp.exp(-step_log)
        decay = jnp.where(live, decay_raw, 1.0)
        grads[0, 0, seq, :, :channels] = (mixer_grad * states * slope).astype(bf16)
        source = mixer_grad * gated
        a, b = tile_scan(decay, decay * source, True)
        following = carry[seq]
        tiles = []
        for tile in reversed(range(local_len // 8)):
            passed = b[tile] + a[tile] * following
            tiles.append(jnp.concatenate((passed[1:], following), axis=0))
            following = passed[0:1]
        carry[seq] = following
        adjoint = source + jnp.concatenate(tiles[::-1], axis=0)
        adjoint = jnp.where(live, adjoint, 0.0)
        square = one_minus_exp(2.0 * step_log, decay_raw)
        inverse_root = lax.rsqrt(square)
        root = square * inverse_root
        gated_conv = in_gate * conv
        logd_grad = adjoint * (
            states - root * gated_conv - gated_conv * decay_raw * decay_raw * inverse_root
        )
        rate_part = logd_grad * rate_gate
        decay_sum = decay_sum + jnp.sum(rate_part, axis=0, keepdims=True)
        rate_pre.append(-rate_scale[...] * rate_part * (1.0 - rate_gate))
        through = adjoint * root
        in_pre.append(through * gated_conv * (1.0 - in_gate))
        direct.append(through * in_gate)
    rate_all = jnp.concatenate(rate_pre, axis=0)
    in_all = jnp.concatenate(in_pre, axis=0)
    conv_all = jnp.concatenate([conv_in[0, 0, seq] for seq in range(seq_count)], axis=0).astype(bf16)
    rate_b, in_b = rate_all.astype(bf16), in_all.astype(bf16)
    for start, stop, low, high, at in gate_tiles(channels, block_width, 128):
        both = jnp.concatenate((rate_b[:, start:stop], in_b[:, start:stop]), axis=1)
        part = lax.dot_general(
            conv_all[:, low:high], both, (((0,), (0,)), ((), ())), preferred_element_type=f32
        )
        if stop - start == 128:
            gate_sums[at : at + high - low] += part
        else:
            gate_sums[at : at + high - low, : stop - start] += part[:, : stop - start]
            gate_sums[at : at + high - low, 128 : 128 + stop - start] += part[:, stop - start :]
    rate_parted, in_parted = split_rows(rate_all), split_rows(in_all)
    parts = []
    for start, stop, low, high, at in gate_tiles(channels, block_width, 256):
        both = jnp.concatenate((rate_parted[:, low:high], in_parted[:, low:high]), axis=1)
        part = joined_dot(both, gate_back[2 * at : 2 * (at + high - low)])
        parts.append(part[:, : stop - start])
    conv_grad = jnp.concatenate(direct, axis=0) + jnp.concatenate(parts, axis=1)
    tap_sums = [jnp.zeros((1, channels), f32) for _ in range(4)]
    for seq in range(seq_count):
        part = conv_grad[seq * local_len : (seq + 1) * local_len]
        extended = jnp.concatenate((part, grad_head[seq]), axis=0)
        x = pre_now[seq, :, channels:]
        total = conv_weight[0:1] * part
        tap_sums[0] = tap_sums[0] + jnp.sum(part * x, axis=0, keepdims=True)
        for lag in range(1, 4):
            moved = extended[lag : lag + local_len]
            total = total + conv_weight[lag : lag + 1] * moved
            tap_sums[lag] = tap_sums[lag] + jnp.sum(moved * x, axis=0, keepdims=True)
        grads[0, 0, seq, :, channels:] = total.astype(bf16)
        grad_head[seq] = part[:8]
    sums[0:1] += jnp.sum(rate_all, axis=0, keepdims=True)
    sums[1:2] += jnp.sum(in_all, axis=0, keepdims=True)
    sums[2:3] += decay_sum
    sums[3:4] += jnp.sum(conv_grad, axis=0, keepdims=True)
    for lag in range(4):
        sums[4 + lag : 5 + lag] += tap_sums[lag]


def chunk_place(chunk, place, chips):
    return lax.rem(place[0] - chunk // 2 + chips, chips), lax.rem(chunk + place[1], 2)


def pick_block(chunk, place, chips, *pairs):
    chip, _ = chunk_place(chunk, place, chips)
    for hop in range(chips):

        @pl.when(chip == hop)
        def _(hop=hop):
            for refs, now in pairs:
                now[...] = refs[hop][0]


def mixer_specs(shape, chips, chunk_of):
    def hop_map(hop, step, place, lengths):
        first = 2 * lax.rem(place[0] - hop + chips, chips)
        return (jnp.where(chunk_of(step) <= first, place[1], 1 - place[1]), 0, 0, 0)

    def block_map(step, place, lengths):
        chip, core = chunk_place(chunk_of(step), place, chips)
        return (chip, core, 0, 0, 0)

    def hops(lanes):
        return [pl.BlockSpec((1, *shape[1:3], lanes), partial(hop_map, hop)) for hop in range(chips)]

    def block(lanes):
        return pl.BlockSpec((1, 1, *shape[1:3], lanes), block_map)

    return hops, block


def whole_spec(shape):
    return pl.BlockSpec(shape, lambda step, place, lengths: (0,) * len(shape))


def mixer_forward(
    pre_blocks, lengths, place, conv_weight, conv_bias, gate_weight, gate_bias, rate_scale, block_width
):
    chips = len(pre_blocks)
    _, seq_count, local_len, channels = pre_blocks[0].shape
    channels //= 2
    hops, block = mixer_specs(pre_blocks[0].shape, chips, lambda step: step)
    full = (chips, 2, seq_count, local_len, channels)
    params = (conv_weight, conv_bias, gate_weight, gate_bias, rate_scale)
    return pl.pallas_call(
        partial(mixer_forward_kernel, chips, block_width),
        grid_spec=pltpu.PrefetchScalarGridSpec(
            num_scalar_prefetch=2,
            grid=(2 * chips,),
            in_specs=hops(2 * channels) + [whole_spec(param.shape) for param in params],
            out_specs=[block(channels)] * 5
            + [whole_spec((seq_count, channels)), whole_spec((seq_count, 3, channels))],
            scratch_shapes=[
                pltpu.VMEM((seq_count, local_len, 2 * channels), f32),
                pltpu.VMEM((seq_count, 8, channels), f32),
                pltpu.VMEM((seq_count, 1, channels), f32),
            ],
        ),
        out_shape=[pltpu.HBM(full, bf16)]
        + [pltpu.HBM(full, f32)] * 4
        + [
            jax.ShapeDtypeStruct((seq_count, channels), f32),
            jax.ShapeDtypeStruct((seq_count, 3, channels), f32),
        ],
        compiler_params=pltpu.CompilerParams(vmem_limit_bytes=32 << 20),
        cost_estimate=kernel_cost,
        name="mixer_forward",
    )(place, lengths, *pre_blocks, *params)


def mixer_backward(
    pre_blocks, back_blocks, saved, lengths, place, conv_weight, gate_back, rate_scale, block_width
):
    chips = len(pre_blocks)
    _, seq_count, local_len, channels = pre_blocks[0].shape
    channels //= 2
    hops, block = mixer_specs(pre_blocks[0].shape, chips, lambda step: 2 * chips - 1 - step)
    full = (chips, 2, seq_count, local_len, channels)
    params = (conv_weight, gate_back, rate_scale)
    packed = gate_tiles(channels, block_width, 128)[-1]
    packed = packed[4] + packed[3] - packed[2]
    return pl.pallas_call(
        partial(mixer_backward_kernel, chips, block_width),
        grid_spec=pltpu.PrefetchScalarGridSpec(
            num_scalar_prefetch=2,
            grid=(2 * chips,),
            in_specs=hops(2 * channels)
            + hops(channels)
            + [block(channels)] * 4
            + [whole_spec(param.shape) for param in params],
            out_specs=[block(2 * channels), whole_spec((8, channels)), whole_spec((packed, 256))],
            scratch_shapes=[
                pltpu.VMEM((seq_count, local_len, 2 * channels), f32),
                pltpu.VMEM((seq_count, local_len, channels), f32),
                pltpu.VMEM((seq_count, 1, channels), f32),
                pltpu.VMEM((seq_count, 8, channels), f32),
            ],
        ),
        out_shape=[
            pltpu.HBM((*full[:-1], 2 * channels), bf16),
            jax.ShapeDtypeStruct((8, channels), f32),
            jax.ShapeDtypeStruct((packed, 256), f32),
        ],
        compiler_params=pltpu.CompilerParams(vmem_limit_bytes=32 << 20),
        cost_estimate=kernel_cost,
        name="mixer_backward",
    )(place, lengths, *pre_blocks, *back_blocks, *saved, *params)


def mlp_kernel(tiles, rows, back, own_in, other_in, own_down, other_down, *refs):
    hidden, gate_grads, up_grads, middle, out, middle_sum, out_sum = refs
    step = pl.program_id(0)

    @pl.when(step == 0)
    def _():
        middle_sum[...] = jnp.zeros_like(middle_sum)
        out_sum[...] = jnp.zeros_like(out_sum)

    def units(weight_in, weight_down):
        gated, slope = gelu_pair(dot(rows[...], weight_in[0]))
        up_pre = dot(rows[...], weight_in[1])
        hidden_grad = dot_nt(back[...], weight_down[...])
        hidden_b = (gated * up_pre).astype(bf16)
        gate_b = (hidden_grad * up_pre * slope).astype(bf16)
        up_b = (hidden_grad * gated).astype(bf16)
        hidden[...] = hidden_b
        gate_grads[...] = gate_b
        up_grads[...] = up_b
        out_sum[...] += dot(hidden_b, weight_down[...])
        middle_sum[...] += dot_nt(gate_b, weight_in[0]) + dot_nt(up_b, weight_in[1])

    @pl.when(step < tiles)
    def _():
        units(own_in, own_down)

    @pl.when(step >= tiles)
    def _():
        units(other_in, other_down)

    @pl.when(step == 2 * tiles - 1)
    def _():
        middle[...] = middle_sum[...]
        out[...] = out_sum[...]


def mlp_block(rows, back, own_in, other_in, own_down, other_down):
    count, width = rows.shape
    units = own_down.shape[0]
    tile = 256 if units % 256 == 0 else 128
    tiles = units // tile

    def own_tile(step):
        return jnp.minimum(step, tiles - 1)

    def other_tile(step):
        return jnp.maximum(step - tiles, 0)

    whole = pl.BlockSpec((count, width), lambda step: (0, 0))
    tiled = pl.BlockSpec((count, tile), lambda step: (0, step))
    return pl.pallas_call(
        partial(mlp_kernel, tiles),
        grid=(2 * tiles,),
        in_specs=[
            whole,
            whole,
            pl.BlockSpec((2, width, tile), lambda step: (0, 0, own_tile(step))),
            pl.BlockSpec((2, width, tile), lambda step: (0, 0, other_tile(step))),
            pl.BlockSpec((tile, width), lambda step: (own_tile(step), 0)),
            pl.BlockSpec((tile, width), lambda step: (other_tile(step), 0)),
        ],
        out_specs=[tiled] * 3 + [whole] * 2,
        out_shape=[pltpu.HBM((count, 2 * units), bf16)] * 3 + [pltpu.HBM((count, width), f32)] * 2,
        scratch_shapes=[pltpu.VMEM((count, width), f32)] * 2,
        compiler_params=pltpu.CompilerParams(vmem_limit_bytes=40 << 20),
        cost_estimate=kernel_cost,
        name="mlp_block",
    )(rows, back, own_in, other_in, own_down, other_down)


def weight_grad_kernel(count, filled, *refs):
    lefts, rights = refs[:count], refs[count : 2 * count]
    own, other = refs[2 * count + 2 * filled :]
    total = dot_tn(lefts[0][...], rights[0][...])
    for left, right in zip(lefts[1:], rights[1:]):
        total = total + dot_tn(left[...], right[...])
    kinds, half, _ = own.shape
    for kind in range(kinds):
        start = 2 * kind * half
        own[kind] = total[start : start + half]
        other[kind] = total[start + half : start + 2 * half].astype(bf16)


def weight_grad(lefts, rights, kinds, slots=1, slot=0, filled=()):
    count = len(rights)
    rows, width = rights[0].shape
    columns = lefts[0].shape[1]
    half, tile = columns // kinds // 2, min(512, width)

    joined = len(lefts) == 1

    def left_spec(at):
        block = at if joined else 0
        return pl.BlockSpec((rows, columns), lambda step: (block, 0))

    lefts = list(lefts) * (count if joined else 1)
    out_spec = pl.BlockSpec((kinds, half, tile), lambda step: (slot, 0, step))
    return pl.pallas_call(
        partial(weight_grad_kernel, count, len(filled) // 2),
        grid=(width // tile,),
        in_specs=[left_spec(at) for at in range(count)]
        + [pl.BlockSpec((rows, tile), lambda step: (0, step))] * count
        + [pl.BlockSpec(memory_space=pl.ANY)] * len(filled),
        out_specs=[out_spec] * 2,
        out_shape=[
            pltpu.HBM((slots * kinds, half, width), f32),
            pltpu.HBM((slots * kinds, half, width), bf16),
        ],
        input_output_aliases={2 * count + at: at for at in range(len(filled))},
        compiler_params=pltpu.CompilerParams(vmem_limit_bytes=40 << 20),
        cost_estimate=kernel_cost,
        name="weight_grad",
    )(*lefts, *rights, *filled)


def block_diagonal(weight):
    count, width, _ = weight.shape
    rows = [
        jnp.pad(weight[at], ((0, 0), (at * width, (count - 1 - at) * width))) for at in range(count)
    ]
    return jnp.concatenate(rows, axis=0)


def pack_gates(rate, into, block_width):
    def padded(values, width):
        return jnp.pad(values, ((0, 0), (0, width - values.shape[1])))

    channels = rate.shape[0]
    forward, back = [], []
    for start, stop, low, high, _ in gate_tiles(channels, block_width, 128):
        forward.append(
            jnp.concatenate(
                (padded(rate[low:high, start:stop], 128), padded(into[low:high, start:stop], 128)), axis=1
            )
        )
    for start, stop, low, high, _ in gate_tiles(channels, block_width, 256):
        back.append(padded(rate.T[low:high, start:stop], 256))
        back.append(padded(into.T[low:high, start:stop], 256))
    return jnp.concatenate(forward, axis=0), jnp.concatenate(back, axis=0)


def unpack_gates(packed, channels, block_width):
    tiles = gate_tiles(channels, block_width, 128)
    kinds = []
    for column in (0, 128):
        blocks = []
        for base in range(0, channels, block_width):
            pieces = []
            for start, stop, low, _, at in tiles:
                left, right = max(start, base), min(stop, base + block_width)
                if left < right:
                    row = at + base - low
                    pieces.append(
                        packed[row : row + block_width, column + left - start : column + right - start]
                    )
            blocks.append(jnp.concatenate(pieces, axis=1))
        kinds.append(jnp.stack(blocks))
    return jnp.stack(kinds)


def narrow_whole(weight, dim):
    return lax.all_gather(weight, "narrow", axis=dim, tiled=True)


def narrow_sum(grad, dim):
    return lax.psum_scatter(grad, "narrow", scatter_dimension=dim, tiled=True)


class DirectSum:
    def __init__(self, grad):
        self.size = lax.axis_size("narrow")
        self.grad, self.got = grad, {}

    def piece(self, flip):
        span = self.grad.shape[1] // self.size
        start = (lax.axis_index("narrow") ^ flip) * span
        return lax.dynamic_slice_in_dim(self.grad, start, span, axis=1)

    def send(self, flips):
        for flip in flips:
            pairs = [(at, at ^ flip) for at in range(self.size)]
            self.got[flip] = lax.ppermute(self.piece(flip), "narrow", pairs)

    def total(self):
        return plus(self.piece(0).astype(f32), *self.got.values())


def swap_cores(values, wide):
    return lax.ppermute(values, "wide", [(at, at ^ 1) for at in range(wide)])


def fence(*values):
    return lax.optimization_barrier(values)


class Chips:
    def __init__(self, wide, chip):
        self.chip, self.count = chip, wide // 2
        self.wide = wide

    def move(self, values, pairs):
        devices = [(2 * a + core, 2 * b + core) for a, b in pairs for core in range(2)]
        return lax.ppermute(values, "wide", devices)

    def ring(self, values):
        return self.move(values, [(at, (at + 1) % self.count) for at in range(self.count)])

    def gather_step(self, step, right, left):
        count = self.count
        to_right = [(at, at + 1) for at in range(step - 1, count - 1)]
        to_left = [(at, at - 1) for at in range(1, count - step + 1)]
        if 2 * step > count + 1:
            both = self.move(jnp.where(self.chip >= step - 1, right, left), to_right + to_left)
            return both, both
        return self.move(right, to_right), self.move(left, to_left)

    def gathered(self, hop, rights, lefts):
        return jnp.where(self.chip >= hop, rights[hop], lefts[self.count - hop])

    def sum_step(self, step, right, left):
        count = self.count
        to_right = [(at, at + 1) for at in range(step)]
        to_left = [(at, at - 1) for at in range(count - step, count)]
        if 2 * step < count - 1:
            both = self.move(jnp.where(self.chip < step, right, left), to_right + to_left)
            return both, both
        return self.move(right, to_right), self.move(left, to_left)


class Exchange:
    def __init__(self, line, rows):
        self.line, self.own = line, rows
        self.packed = line.count == 4
        if self.packed:
            self.odd = line.chip % 2 == 1
            self.edge = (line.chip == 0) | (line.chip == 3)
        self.ends, self.mids = [], []
        self.backs, self.moved = {0: (rows, rows)}, (0.0, 0.0)

    def pair(self, end, mid):
        self.ends.append(self.line.move(end, [(0, 1), (1, 0), (2, 3), (3, 2)]))
        self.mids.append(self.line.move(mid, [(1, 2), (2, 1)]))

    def step(self, number, parts):
        line, count = self.line, self.line.count
        if not self.packed:
            if number < count:
                self.backs[number] = line.gather_step(number, *self.backs[number - 1])
            if number > 1:
                sent = [
                    plus(parts[hop], self.moved[way]).astype(bf16)
                    for way, hop in enumerate((number - 1, count - number + 1))
                ]
                self.moved = line.sum_step(number - 1, *sent)
        elif number == 1:
            self.pair(self.own, self.own)
        elif number == 2:
            part = jnp.where(line.chip == 0, parts[1], parts[3]).astype(bf16)
            self.pair(jnp.where(self.edge, part, self.mids[0]), self.ends[0])
        elif number == 3:
            mid = plus(parts[2], self.ends[1]).astype(bf16)
            self.pair(jnp.where(self.edge, parts[2].astype(bf16), self.mids[1]), mid)
        else:
            end = plus(jnp.where(self.odd, parts[1], parts[3]), self.mids[2])
            mid = plus(jnp.where(line.chip == 1, parts[3], parts[1]), self.ends[2])
            self.pair(end.astype(bf16), mid.astype(bf16))

    def fence(self, *values):
        state = (self.ends, self.mids, self.backs, self.moved)
        state, values = fence(state, values)
        self.ends, self.mids, self.backs, self.moved = state
        return values

    def rows(self):
        if self.packed:
            far = jnp.where(self.edge, self.ends[2], self.mids[0])
            two = jnp.where(self.edge, self.ends[1], self.mids[1])
            near = self.ends[0]
            return [self.own, jnp.where(self.odd, near, far), two, jnp.where(self.odd, far, near)]
        rights, lefts = ({at: pair[way] for at, pair in self.backs.items()} for way in range(2))
        hops = range(1, self.line.count)
        return [self.own] + [self.line.gathered(hop, rights, lefts) for hop in hops]

    def total(self, part):
        if self.packed:
            return plus(part, self.ends[3], self.mids[3])
        return plus(part, *self.moved)


def plus(total, *moved):
    for values in moved:
        total = total + values.astype(f32)
    return total


def paired_sum(values, axis):
    size = lax.axis_size(axis)
    if size & (size - 1):
        return lax.psum(values, axis)
    bit = 1
    while bit < size:
        values = values + lax.ppermute(values, axis, [(at, at ^ bit) for at in range(size)])
        bit *= 2
    return values


def direct_sum(values, axis):
    size = lax.axis_size(axis)
    if size & (size - 1):
        return lax.psum(values, axis)
    terms = [values] + [
        lax.ppermute(values, axis, [(at, at ^ flip) for at in range(size)]) for flip in range(1, size)
    ]
    while len(terms) > 1:
        terms = [left + right for left, right in zip(terms[::2], terms[1::2])]
    return terms[0]


def norm_forward(values, gain):
    scale = lax.rsqrt(jnp.mean(values * values, axis=-1, keepdims=True) + norm_eps)
    return scale, (values * scale * gain).astype(bf16)


def norm_backward(values, scale, gain, grad):
    unit = values * scale
    scaled = grad * gain
    back = scale * (scaled - unit * jnp.mean(scaled * unit, axis=-1, keepdims=True))
    return back, jnp.sum(grad * unit, axis=0)


def dot(left, right):
    return jnp.dot(left, right, preferred_element_type=f32)


def dot_nt(left, right):
    return lax.dot_general(left, right, (((1,), (1,)), ((), ())), preferred_element_type=f32)


def dot_tn(left, right):
    return lax.dot_general(left, right, (((0,), (0,)), ((), ())), preferred_element_type=f32)


def body(
    tokens, lengths, cotangent, first_gain, proj_in, conv_weight, conv_bias, rate_weight, rate_bias,
    input_weight, input_bias, decay_param, proj_out, second_gain, mlp_in, mlp_down,
):
    seq_count, local_len, width = tokens.shape
    wide = lax.axis_size("wide")
    chips = wide // 2
    me = lax.axis_index("wide")
    chip, core = me // 2, me % 2
    place = jnp.stack((chip, core)).astype(jnp.int32)
    channels = proj_in.shape[2]
    block_width = rate_weight.shape[1]
    seq_half = seq_count // 2
    block_shape = (2, seq_half, local_len, 2 * channels)
    line = Chips(wide, chip)
    last = chips - 1

    def swap(values):
        return swap_cores(values, wide)

    def by_sequence(values):
        parts = values.reshape(2, seq_half * local_len, width)
        mine = jnp.where(core == 0, parts[0], parts[1])
        return jnp.concatenate((mine, swap(jnp.where(core == 0, parts[1], parts[0]))), axis=0)

    def both_orders(mine, other):
        return jnp.where(core == 0, jnp.stack((mine, other)), jnp.stack((other, mine)))

    def by_position(rows):
        own, other = jnp.split(rows, 2, axis=0)
        return both_orders(own, swap(other)).reshape(tokens.shape)

    def by_channel(values):
        mine, other = values[..., :channels], values[..., channels:]
        both = both_orders(mine, swap(other))
        return both.reshape(seq_count, *both.shape[2:])

    lengths = lax.dynamic_slice_in_dim(lengths, core * seq_half, seq_half)
    chunk = 2 * chip + (jnp.arange(2, dtype=jnp.int32) ^ core)
    positions = chunk[:, None] * local_len + jnp.arange(local_len, dtype=jnp.int32)
    mask = (positions[:, None, :] < lengths[None, :, None]).astype(f32).reshape(-1, 1)

    def both_cores(own, dim):
        return jnp.concatenate((own, swap(own)), axis=dim)

    own_in = narrow_whole(jnp.swapaxes(proj_in, 1, 2), 2)
    own_out = narrow_whole(proj_out, 1)
    own_mlp_in = narrow_whole(mlp_in, 1)
    own_down = narrow_whole(mlp_down, 1)
    tokens_f = by_sequence(tokens).astype(f32)
    scale_one, norm_in = norm_forward(tokens_f, first_gain)

    params = jnp.concatenate(
        (conv_weight, conv_bias[None], rate_bias[None], input_bias[None], decay_param[None]), axis=0
    )
    norm_in, params, cotangent = fence(norm_in, params, cotangent)
    rows_first = [norm_in]
    pre_blocks = []

    def project(rows):
        return dot_nt(rows, whole_in).reshape(2, seq_half, local_len, 4 * channels)

    for hop in range(1, chips):
        moved = line.ring(rows_first[-1])
        if hop == 1:
            out_grad = by_sequence(cotangent).astype(f32) * mask
            out_grad_b = out_grad.astype(bf16)
            params = both_cores(params, 1)
            gates = both_cores(jnp.stack((rate_weight, input_weight)), 1)
            gate_weight, gate_back = pack_gates(
                block_diagonal(gates[0]), block_diagonal(gates[1]), block_width
            )
            rate_scale = decay_scale * jax.nn.softplus(-params[7:8])
            moved, out_grad_b, gate_weight = fence(moved, out_grad_b, gate_weight)
        if hop == last - 1:
            moved, own_in = fence(moved, own_in)
        if hop == last:
            whole_in = both_cores(own_in, 1).reshape(-1, width)
            pre_blocks = [project(rows) for rows in rows_first]
            moved, out_grad_b, own_out, pre_blocks = fence(moved, out_grad_b, own_out, pre_blocks)
        rows_first.append(moved)

    lanes = Exchange(line, out_grad_b)
    lanes.step(1, None)
    whole_out = both_cores(own_out, 0)
    pre_blocks.append(project(rows_first[last]))
    mixed, conv, rate_gate, in_gate, states, final_state, conv_state = mixer_forward(
        pre_blocks, lengths, place, params[:4], params[4:5], gate_weight, params[5:7],
        rate_scale, block_width,
    )
    mixed_rows = mixed.reshape(chips, -1, 2 * channels)
    parts = {hop: dot(mixed_rows[hop], whole_out) for hop in (1, last)}
    parts, mixed_rows = lanes.fence(parts, mixed_rows)
    for step in range(2, chips + 1):
        lanes.step(step, parts)
        for hop in (step, chips - step):
            if hop < chips and hop not in parts:
                parts[hop] = dot(mixed_rows[hop], whole_out)
        if step == chips - 1:
            if 0 not in parts:
                parts[0] = dot(mixed_rows[0], whole_out)
            parts, own_mlp_in = lanes.fence(parts, own_mlp_in)
            other_mlp_in = swap(own_mlp_in)
        elif step < chips:
            (parts,) = lanes.fence(parts)
    rows_back = lanes.rows()
    parts, rows_back, own_down = lanes.fence(parts, rows_back, own_down)
    resid = tokens_f + lanes.total(parts[0])

    scale_two, norm_mid = norm_forward(resid, second_gain)
    norm_mid, own_down = fence(norm_mid, own_down)
    other_down = swap(own_down)
    rows_second = [norm_mid]
    hidden, gate_grads, up_grads, parts, outs = [], [], [], [], []
    sums = None
    for hop in range(chips):
        if hop < last:
            rows_second.append(line.ring(rows_second[hop]))
        if hop > 1:
            sums = line.ring(total_b)
        made = mlp_block(
            rows_second[hop], rows_back[hop], own_mlp_in, other_mlp_in, own_down, other_down
        )
        rows_second, made, sums = fence(rows_second, made, sums)
        for kept, value in zip((hidden, gate_grads, up_grads, parts, outs), made):
            kept.append(value)
        if hop:
            total = parts[hop] if sums is None else plus(parts[hop], sums)
            total_b = total.astype(bf16)
    sums = line.ring(total_b)
    grads_mlp = weight_grad(gate_grads, rows_second, 1, slots=2)
    grads_down = weight_grad(hidden, rows_back, 1)
    sums, grads_mlp, grads_down, up_grads = fence(sums, grads_mlp, grads_down, up_grads)
    mid_sum = plus(parts[0], sums)

    from_norm, gain_two = norm_backward(resid, scale_two, second_gain, mid_sum)
    resid_grad = out_grad + from_norm
    resid_grad_b = resid_grad.astype(bf16)
    resid_grad_b, up_grads, outs = fence(resid_grad_b, up_grads, outs)

    def shared(grads):
        own, other = grads
        return (own + swap(other).astype(f32)).astype(bf16).reshape(-1, width)

    def back_block(rows):
        return dot_nt(rows, whole_out).reshape(2, seq_half, local_len, 2 * channels)

    lanes = Exchange(line, resid_grad_b)
    lanes.step(1, None)
    grads_mlp = weight_grad(up_grads, rows_second, 1, slots=2, slot=1, filled=grads_mlp)
    grads_mlp, outs = lanes.fence(grads_mlp, outs)
    for step in range(2, chips + 1):
        lanes.step(step, outs)
        if step == 2:
            part_mlp_in = shared(grads_mlp)
            part_mlp_in, grads_down = lanes.fence(part_mlp_in, grads_down)
            grad_mlp_in = narrow_sum(part_mlp_in, 1)
        elif step == 3:
            part_down = shared(grads_down)
            back_blocks = [back_block(resid_grad_b)]
            part_down, back_blocks = lanes.fence(part_down, back_blocks)
            grad_mlp_down = narrow_sum(part_down, 1)
        elif step < chips:
            lanes.fence()
    rows_resid = lanes.rows()
    back_blocks += [back_block(rows) for rows in rows_resid[1:]]
    grads, small, gate_sums = mixer_backward(
        pre_blocks, back_blocks, (conv, rate_gate, in_gate, states),
        lengths, place, params[:4], gate_back, rate_scale, block_width,
    )
    grad_rows = grads.reshape(chips, -1, 4 * channels)
    sent = dot(grad_rows[1], whole_in).astype(bf16)
    sent, grads, small, gate_sums, mixed, grad_mlp_in = lanes.fence(
        sent, grads, small, gate_sums, mixed, grad_mlp_in
    )
    output = (resid + lanes.total(outs[0])).astype(bf16)

    grad_rows = grads.reshape(chips, -1, 4 * channels)
    count = rate_weight.shape[0]
    size = lax.axis_size("narrow")
    for hop in range(1, chips):
        moving = line.ring(sent)
        part = dot(grad_rows[(hop + 1) % chips], whole_in)
        if hop == 1:
            grads_in = weight_grad([grads.reshape(-1, 4 * channels)], rows_first, 2)
            part_in = shared(grads_in)
            gate_grads = unpack_gates(gate_sums, 2 * channels, block_width)
            mine = jnp.concatenate((small[:, :channels].reshape(-1), gate_grads[:, :count].reshape(-1)))
            other = jnp.concatenate((small[:, channels:].reshape(-1), gate_grads[:, count:].reshape(-1)))
            part_in, moving, part, mixed, mine, other, output = fence(
                part_in, moving, part, mixed, mine, other, output
            )
        elif hop == 2:
            sum_in = DirectSum(part_in)
            sum_in.send(range(1, size))
            grads_out = weight_grad([mixed.reshape(-1, 2 * channels)], rows_resid, 1)
            part_out = shared(grads_out)
            own_rows = own_in.reshape(-1, width).astype(f32)
            gain_one = jnp.sum(own_rows * part_in.astype(f32), axis=0) / first_gain
            flat = mine + swap(other)
            part_out, moving, part, flat, gain_one, sum_in.got, grad_mlp_down = fence(
                part_out, moving, part, flat, gain_one, sum_in.got, grad_mlp_down
            )
        elif hop == last:
            sum_out = DirectSum(part_out)
            sum_out.send(range(1, size))
            flat = paired_sum(flat, "narrow")
            gains = direct_sum(jnp.stack((gain_one, gain_two)), "wide")
            moving, gains, flat, sum_out.got = fence(moving, gains, flat, sum_out.got)
        sent = plus(part, moving).astype(bf16)
    in_sum = plus(part, moving)
    gains = direct_sum(gains, "narrow")
    grad_mlp_in, grad_mlp_down = grad_mlp_in.astype(f32), grad_mlp_down.astype(f32)
    grad_proj_in = sum_in.total().reshape(2, channels, -1)
    grad_proj_out = sum_out.total()
    from_norm, _ = norm_backward(tokens_f, scale_one, first_gain, in_sum)
    grad_tokens = (resid_grad + from_norm).astype(bf16)
    sums = flat[: 8 * channels].reshape(8, channels)
    grad_rate_weight, grad_input_weight = flat[8 * channels :].reshape(2, *rate_weight.shape)
    grad_mlp_in = grad_mlp_in.reshape(2, mlp_in.shape[2], -1)
    return (
        by_position(output),
        by_position(grad_tokens),
        by_channel(final_state),
        by_channel(conv_state),
        gains[0],
        jnp.swapaxes(grad_proj_in, 1, 2),
        sums[4:8],
        sums[3],
        grad_rate_weight,
        sums[0],
        grad_input_weight,
        sums[1],
        sums[2] * decay_scale * jax.nn.sigmoid(-decay_param),
        grad_proj_out,
        gains[1],
        jnp.swapaxes(grad_mlp_in, 1, 2),
        grad_mlp_down,
    )


def solution(mesh):
    return jax.shard_map(
        body,
        mesh=mesh,
        in_specs=(
            P("narrow", "wide", None),
            P("narrow"),
            P("narrow", "wide", None),
            P(),
            P(None, "narrow", "wide"),
            P(None, "wide"),
            P("wide"),
            P("wide", None, None),
            P("wide"),
            P("wide", None, None),
            P("wide"),
            P("wide"),
            P("wide", "narrow"),
            P(),
            P(None, "narrow", "wide"),
            P("wide", "narrow"),
        ),
        out_specs=(
            P("narrow", "wide", None),
            P("narrow", "wide", None),
            P("narrow", "wide"),
            P("narrow", None, "wide"),
            P(),
            P(None, "narrow", "wide"),
            P(None, "wide"),
            P("wide"),
            P("wide", None, None),
            P("wide"),
            P("wide", None, None),
            P("wide"),
            P("wide"),
            P("wide", "narrow"),
            P(),
            P(None, "narrow", "wide"),
            P("wide", "narrow"),
        ),
        check_vma=False,
    )
```

```python
from functools import partial

import jax
import jax.numpy as jnp
from jax import lax
from jax.experimental import pallas as pl
from jax.experimental.pallas import tpu as pltpu
from jax.sharding import PartitionSpec as P

decay_scale = 8.0
norm_eps = 1e-06
gelu_in = 0.7978845608028654
gelu_cube = 0.044715
f32 = jnp.float32
bf16 = jnp.bfloat16
kernel_cost = pl.CostEstimate(flops=1, bytes_accessed=1, transcendentals=0)


def gelu_tanh(v):
    return jnp.tanh(gelu_in * (v + gelu_cube * v * v * v))


def gelu_pair(v):
    t = gelu_tanh(v)
    half = 0.5 * (1.0 + t)
    slope = half + 0.5 * v * (1.0 - t * t) * (gelu_in + (3.0 * gelu_in * gelu_cube) * v * v)
    return v * half, slope


def one_minus_exp(v, decay):
    series = 1.0 - v * (1.0 / 7.0)
    for order in (6.0, 5.0, 4.0, 3.0, 2.0):
        series = 1.0 - v * (1.0 / order) * series
    return jnp.where(v < 0.3, v * series, 1.0 - decay * decay)


def gate_tiles(channels, block_width, tile):
    tiles, offset = [], 0
    for start in range(0, channels, tile):
        stop = min(start + tile, channels)
        low = start // block_width * block_width // 128 * 128
        high = min(-(-((stop - 1) // block_width + 1) * block_width // 128) * 128, channels)
        tiles.append((start, stop, low, high, offset))
        offset += high - low
    return tiles


def split_rows(values):
    high = values.astype(bf16)
    return jnp.concatenate((high, (values - high.astype(f32)).astype(bf16)), axis=0)


def joined_dot(halves, weight):
    both = jnp.dot(halves, weight, preferred_element_type=f32)
    rows = both.shape[0] // 2
    return both[:rows] + both[rows:]


def tile_scan(decay, drive, backward):
    rows, channels = decay.shape
    a = decay.reshape(rows // 8, 8, channels)
    b = drive.reshape(rows // 8, 8, channels)
    row = lax.broadcasted_iota(jnp.int32, (1, 8, channels), 1)
    for step in (1, 2, 4):
        if backward:
            keep, shift = row < 8 - step, 8 - step
        else:
            keep, shift = row >= step, step
        a_moved = jnp.where(keep, pltpu.roll(a, shift, 1), 1.0)
        b_moved = jnp.where(keep, pltpu.roll(b, shift, 1), 0.0)
        b = b + a * b_moved
        a = a * a_moved
    return a, b


def mixer_forward_kernel(
    chips, block_width, place, lengths, *refs
):
    pre_refs, refs = refs[:chips], refs[chips:]
    conv_weight, conv_bias, gate_weight, gate_bias, rate_scale = refs[:5]
    mixed, conv_out, rate_out, in_out, states_out, final_state, conv_state = refs[5:12]
    pre_now, x_tail, carry = refs[12:]
    chunk = pl.program_id(0)
    seq_count, local_len, channels = pre_now.shape
    channels //= 2
    pick_block(chunk, place, chips, pre_refs, pre_now)

    @pl.when(chunk == 0)
    def _():
        x_tail[...] = jnp.zeros_like(x_tail)
        carry[...] = jnp.zeros_like(carry)

    convs = []
    for seq in range(seq_count):
        x = pre_now[seq, :, channels:]
        extended = jnp.concatenate((x_tail[seq], x), axis=0)
        conv = conv_bias[...] + conv_weight[0:1] * x
        for lag in range(1, 4):
            conv = conv + conv_weight[lag : lag + 1] * extended[8 - lag : 8 - lag + local_len]
        x_tail[seq] = x[local_len - 8 :]
        convs.append(conv)
        for tap in range(3):
            position = lengths[seq] - 3 + tap

            @pl.when(position // local_len == chunk)
            def _(seq=seq, tap=tap, position=position):
                conv_state[seq, tap : tap + 1] = pre_now[
                    seq, pl.ds(lax.rem(position, local_len), 1), channels:
                ]

    conv_all = jnp.concatenate(convs, axis=0)
    parted = split_rows(conv_all)
    rate_parts, in_parts = [], []
    for start, stop, low, high, at in gate_tiles(channels, block_width, 128):
        both = joined_dot(parted[:, low:high], gate_weight[at : at + high - low])
        rate_parts.append(both[:, : stop - start])
        in_parts.append(both[:, 128 : 128 + stop - start])
    rate_all = jax.nn.sigmoid(jnp.concatenate(rate_parts, axis=1) + gate_bias[0:1])
    in_all = jax.nn.sigmoid(jnp.concatenate(in_parts, axis=1) + gate_bias[1:2])
    for seq in range(seq_count):
        rows = slice(seq * local_len, (seq + 1) * local_len)
        conv = convs[seq]
        rate_gate = rate_all[rows]
        in_gate = in_all[rows]
        step_log = rate_scale[...] * rate_gate
        decay = jnp.exp(-step_log)
        root = jnp.sqrt(one_minus_exp(2.0 * step_log, decay))
        position = chunk * local_len + lax.broadcasted_iota(jnp.int32, (local_len, 1), 0)
        live = position < lengths[seq]
        drive = jnp.where(live, root * in_gate * conv, 0.0)
        a, b = tile_scan(jnp.where(live, decay, 1.0), drive, False)
        last = carry[seq]
        gated, _ = gelu_pair(pre_now[seq, :, :channels])
        tiles = []
        for tile in range(local_len // 8):
            tiles.append(b[tile] + a[tile] * last)
            last = tiles[-1][7:8]
        states = jnp.concatenate(tiles, axis=0)
        states_out[0, 0, seq] = states
        mixed[0, 0, seq] = (gated * states).astype(bf16)
        carry[seq] = last
        final_state[seq : seq + 1] = last
        conv_out[0, 0, seq] = conv
        rate_out[0, 0, seq] = rate_gate
        in_out[0, 0, seq] = in_gate


def mixer_backward_kernel(
    chips, block_width, crossed, place, lengths, *refs
):
    pre_refs, back_refs, refs = refs[:chips], refs[chips : 2 * chips], refs[2 * chips :]
    conv_in, rate_in, in_in, states_in, conv_weight, gate_back, rate_scale = refs[:7]
    grads, sums, gate_grads = refs[7:10]
    pre_now, back_now, carry, grad_head, gate_sums = refs[10:]
    step = pl.program_id(0)
    chunk = pl.num_programs(0) - 1 - step
    seq_count, local_len, channels = back_now.shape
    pick_block(chunk, place, chips, pre_refs, pre_now)
    pick_block(chunk, place, chips, back_refs, back_now, crossed)

    @pl.when(step == 0)
    def _():
        carry[...] = jnp.zeros_like(carry)
        grad_head[...] = jnp.zeros_like(grad_head)
        sums[...] = jnp.zeros_like(sums)
        gate_sums[...] = jnp.zeros_like(gate_sums)

    rate_pre, in_pre, direct = [], [], []
    decay_sum = jnp.zeros((1, channels), f32)
    for seq in range(seq_count):
        position = chunk * local_len + lax.broadcasted_iota(jnp.int32, (local_len, 1), 0)
        live = position < lengths[seq]
        rate_gate = rate_in[0, 0, seq]
        in_gate = in_in[0, 0, seq]
        conv = conv_in[0, 0, seq]
        states = states_in[0, 0, seq]
        mixer_grad = back_now[seq]
        gated, slope = gelu_pair(pre_now[seq, :, :channels])
        step_log = rate_scale[...] * rate_gate
        decay_raw = jnp.exp(-step_log)
        decay = jnp.where(live, decay_raw, 1.0)
        grads[0, 0, seq, :, :channels] = (mixer_grad * states * slope).astype(bf16)
        source = mixer_grad * gated
        a, b = tile_scan(decay, decay * source, True)
        following = carry[seq]
        tiles = []
        for tile in reversed(range(local_len // 8)):
            passed = b[tile] + a[tile] * following
            tiles.append(jnp.concatenate((passed[1:], following), axis=0))
            following = passed[0:1]
        carry[seq] = following
        adjoint = source + jnp.concatenate(tiles[::-1], axis=0)
        adjoint = jnp.where(live, adjoint, 0.0)
        square = one_minus_exp(2.0 * step_log, decay_raw)
        inverse_root = lax.rsqrt(square)
        root = square * inverse_root
        gated_conv = in_gate * conv
        logd_grad = adjoint * (
            states - root * gated_conv - gated_conv * decay_raw * decay_raw * inverse_root
        )
        rate_part = logd_grad * rate_gate
        decay_sum = decay_sum + jnp.sum(rate_part, axis=0, keepdims=True)
        rate_pre.append(-rate_scale[...] * rate_part * (1.0 - rate_gate))
        through = adjoint * root
        in_pre.append(through * gated_conv * (1.0 - in_gate))
        direct.append(through * in_gate)
    rate_all = jnp.concatenate(rate_pre, axis=0)
    in_all = jnp.concatenate(in_pre, axis=0)
    conv_all = jnp.concatenate([conv_in[0, 0, seq] for seq in range(seq_count)], axis=0).astype(bf16)
    rate_b, in_b = rate_all.astype(bf16), in_all.astype(bf16)
    for start, stop, low, high, at in gate_tiles(channels, block_width, 128):
        both = jnp.concatenate((rate_b[:, start:stop], in_b[:, start:stop]), axis=1)
        part = lax.dot_general(
            conv_all[:, low:high], both, (((0,), (0,)), ((), ())), preferred_element_type=f32
        )
        if stop - start == 128:
            gate_sums[at : at + high - low] += part
        else:
            gate_sums[at : at + high - low, : stop - start] += part[:, : stop - start]
            gate_sums[at : at + high - low, 128 : 128 + stop - start] += part[:, stop - start :]
    rate_parted, in_parted = split_rows(rate_all), split_rows(in_all)
    parts = []
    for start, stop, low, high, at in gate_tiles(channels, block_width, 256):
        both = jnp.concatenate((rate_parted[:, low:high], in_parted[:, low:high]), axis=1)
        part = joined_dot(both, gate_back[2 * at : 2 * (at + high - low)])
        parts.append(part[:, : stop - start])
    conv_grad = jnp.concatenate(direct, axis=0) + jnp.concatenate(parts, axis=1)
    tap_sums = [jnp.zeros((1, channels), f32) for _ in range(4)]
    for seq in range(seq_count):
        part = conv_grad[seq * local_len : (seq + 1) * local_len]
        extended = jnp.concatenate((part, grad_head[seq]), axis=0)
        x = pre_now[seq, :, channels:]
        total = conv_weight[0:1] * part
        tap_sums[0] = tap_sums[0] + jnp.sum(part * x, axis=0, keepdims=True)
        for lag in range(1, 4):
            moved = extended[lag : lag + local_len]
            total = total + conv_weight[lag : lag + 1] * moved
            tap_sums[lag] = tap_sums[lag] + jnp.sum(moved * x, axis=0, keepdims=True)
        grads[0, 0, seq, :, channels:] = total.astype(bf16)
        grad_head[seq] = part[:8]
    sums[0:1] += jnp.sum(rate_all, axis=0, keepdims=True)
    sums[1:2] += jnp.sum(in_all, axis=0, keepdims=True)
    sums[2:3] += decay_sum
    sums[3:4] += jnp.sum(conv_grad, axis=0, keepdims=True)
    for lag in range(4):
        sums[4 + lag : 5 + lag] += tap_sums[lag]

    @pl.when(chunk == 0)
    def _():
        tiles = gate_tiles(channels, block_width, 128)
        for kind, column in enumerate((0, 128)):
            for base in range(0, channels, block_width):
                pieces = []
                for start, stop, low, _, at in tiles:
                    left, right = max(start, base), min(stop, base + block_width)
                    if left < right:
                        row = at + base - low
                        span = gate_sums[row : row + block_width, column : column + 128]
                        pieces.append(span[:, left - start : right - start])
                gate_grads[base // block_width, kind] = jnp.concatenate(pieces, axis=1)


def chunk_place(chunk, place, chips):
    return lax.rem(place[0] - chunk // 2 + chips, chips), lax.rem(chunk + place[1], 2)


def pick_block(chunk, place, chips, refs, now, crossed=False):
    slot = (chunk // 2) ^ place[0] if crossed else chunk_place(chunk, place, chips)[0]
    for hop in range(chips):

        @pl.when(slot == hop)
        def _(hop=hop):
            now[...] = refs[hop][0]


def mixer_specs(shape, chips, chunk_of):
    def hop_map(hop, crossed, step, place, lengths):
        first = 2 * (place[0] ^ hop if crossed else lax.rem(place[0] - hop + chips, chips))
        return (jnp.where(chunk_of(step) <= first, place[1], 1 - place[1]), 0, 0, 0)

    def block_map(step, place, lengths):
        chip, core = chunk_place(chunk_of(step), place, chips)
        return (chip, core, 0, 0, 0)

    def hops(lanes, crossed=False):
        block = (1, *shape[1:3], lanes)
        return [pl.BlockSpec(block, partial(hop_map, hop, crossed)) for hop in range(chips)]

    def block(lanes):
        return pl.BlockSpec((1, 1, *shape[1:3], lanes), block_map)

    return hops, block


def whole_spec(shape):
    return pl.BlockSpec(shape, lambda step, place, lengths: (0,) * len(shape))


def mixer_forward(
    pre_blocks, lengths, place, conv_weight, conv_bias, gate_weight, gate_bias, rate_scale, block_width
):
    chips = len(pre_blocks)
    _, seq_count, local_len, channels = pre_blocks[0].shape
    channels //= 2
    hops, block = mixer_specs(pre_blocks[0].shape, chips, lambda step: step)
    full = (chips, 2, seq_count, local_len, channels)
    params = (conv_weight, conv_bias, gate_weight, gate_bias, rate_scale)
    return pl.pallas_call(
        partial(mixer_forward_kernel, chips, block_width),
        grid_spec=pltpu.PrefetchScalarGridSpec(
            num_scalar_prefetch=2,
            grid=(2 * chips,),
            in_specs=hops(2 * channels) + [whole_spec(param.shape) for param in params],
            out_specs=[block(channels)] * 5
            + [whole_spec((seq_count, channels)), whole_spec((seq_count, 3, channels))],
            scratch_shapes=[
                pltpu.VMEM((seq_count, local_len, 2 * channels), f32),
                pltpu.VMEM((seq_count, 8, channels), f32),
                pltpu.VMEM((seq_count, 1, channels), f32),
            ],
        ),
        out_shape=[pltpu.HBM(full, bf16)]
        + [pltpu.HBM(full, f32)] * 4
        + [
            jax.ShapeDtypeStruct((seq_count, channels), f32),
            jax.ShapeDtypeStruct((seq_count, 3, channels), f32),
        ],
        compiler_params=pltpu.CompilerParams(vmem_limit_bytes=32 << 20),
        cost_estimate=kernel_cost,
        name="mixer_forward",
    )(place, lengths, *pre_blocks, *params)


def mixer_backward(
    pre_blocks, back_blocks, crossed, saved, lengths, place, conv_weight, gate_back, rate_scale, block_width
):
    chips = len(pre_blocks)
    _, seq_count, local_len, channels = pre_blocks[0].shape
    channels //= 2
    hops, block = mixer_specs(pre_blocks[0].shape, chips, lambda step: 2 * chips - 1 - step)
    full = (chips, 2, seq_count, local_len, channels)
    params = (conv_weight, gate_back, rate_scale)
    packed = gate_tiles(channels, block_width, 128)[-1]
    packed = packed[4] + packed[3] - packed[2]
    gate_shape = (channels // block_width, 2, block_width, block_width)
    return pl.pallas_call(
        partial(mixer_backward_kernel, chips, block_width, crossed),
        grid_spec=pltpu.PrefetchScalarGridSpec(
            num_scalar_prefetch=2,
            grid=(2 * chips,),
            in_specs=hops(2 * channels)
            + hops(channels, crossed)
            + [block(channels)] * 4
            + [whole_spec(param.shape) for param in params],
            out_specs=[block(2 * channels), whole_spec((8, channels)), whole_spec(gate_shape)],
            scratch_shapes=[
                pltpu.VMEM((seq_count, local_len, 2 * channels), f32),
                pltpu.VMEM((seq_count, local_len, channels), f32),
                pltpu.VMEM((seq_count, 1, channels), f32),
                pltpu.VMEM((seq_count, 8, channels), f32),
                pltpu.VMEM((packed, 256), f32),
            ],
        ),
        out_shape=[
            pltpu.HBM((*full[:-1], 2 * channels), bf16),
            jax.ShapeDtypeStruct((8, channels), f32),
            jax.ShapeDtypeStruct(gate_shape, f32),
        ],
        compiler_params=pltpu.CompilerParams(vmem_limit_bytes=32 << 20),
        cost_estimate=kernel_cost,
        name="mixer_backward",
    )(place, lengths, *pre_blocks, *back_blocks, *saved, *params)


def mlp_kernel(tiles, rows, back, own_in, other_in, own_down, other_down, *refs):
    hidden, gate_grads, up_grads, middle, out, middle_sum, out_sum = refs
    step = pl.program_id(0)

    @pl.when(step == 0)
    def _():
        middle_sum[...] = jnp.zeros_like(middle_sum)
        out_sum[...] = jnp.zeros_like(out_sum)

    def units(weight_in, weight_down):
        gated, slope = gelu_pair(dot(rows[...], weight_in[0]))
        up_pre = dot(rows[...], weight_in[1])
        hidden_grad = dot_nt(back[...], weight_down[...])
        hidden_b = (gated * up_pre).astype(bf16)
        gate_b = (hidden_grad * up_pre * slope).astype(bf16)
        up_b = (hidden_grad * gated).astype(bf16)
        hidden[...] = hidden_b
        gate_grads[...] = gate_b
        up_grads[...] = up_b
        out_sum[...] += dot(hidden_b, weight_down[...])
        middle_sum[...] += dot_nt(gate_b, weight_in[0]) + dot_nt(up_b, weight_in[1])

    @pl.when(step < tiles)
    def _():
        units(own_in, own_down)

    @pl.when(step >= tiles)
    def _():
        units(other_in, other_down)

    @pl.when(step == 2 * tiles - 1)
    def _():
        middle[...] = middle_sum[...]
        out[...] = out_sum[...].astype(bf16)


def mlp_block(rows, back, own_in, other_in, own_down, other_down):
    count, width = rows.shape
    units = own_down.shape[0]
    tile = 256 if units % 256 == 0 else 128
    tiles = units // tile

    def own_tile(step):
        return jnp.minimum(step, tiles - 1)

    def other_tile(step):
        return jnp.maximum(step - tiles, 0)

    whole = pl.BlockSpec((count, width), lambda step: (0, 0))
    tiled = pl.BlockSpec((count, tile), lambda step: (0, step))
    return pl.pallas_call(
        partial(mlp_kernel, tiles),
        grid=(2 * tiles,),
        in_specs=[
            whole,
            whole,
            pl.BlockSpec((2, width, tile), lambda step: (0, 0, own_tile(step))),
            pl.BlockSpec((2, width, tile), lambda step: (0, 0, other_tile(step))),
            pl.BlockSpec((tile, width), lambda step: (own_tile(step), 0)),
            pl.BlockSpec((tile, width), lambda step: (other_tile(step), 0)),
        ],
        out_specs=[tiled] * 3 + [whole] * 2,
        out_shape=[pltpu.HBM((count, 2 * units), bf16)] * 3
        + [pltpu.HBM((count, width), f32), pltpu.HBM((count, width), bf16)],
        scratch_shapes=[pltpu.VMEM((count, width), f32)] * 2,
        compiler_params=pltpu.CompilerParams(vmem_limit_bytes=40 << 20),
        cost_estimate=kernel_cost,
        name="mlp_block",
    )(rows, back, own_in, other_in, own_down, other_down)


def weight_grad_kernel(count, kinds, weighted, *refs):
    lefts, rights = refs[:count], refs[count : 2 * count]
    outs = refs[2 * count + weighted :]
    total = dot_tn(lefts[0][...], rights[0][...])
    for left, right in zip(lefts[1:], rights[1:]):
        total = total + dot_tn(left[...], right[...])
    half = outs[0].shape[0]
    for kind in range(kinds):
        start = 2 * kind * half
        outs[kind][...] = total[start : start + half]
        outs[kinds + kind][...] = total[start + half : start + 2 * half].astype(bf16)
    if weighted:
        weight = refs[2 * count][...]
        outs[2 * kinds][...] = jnp.sum(total * weight.astype(f32), axis=0, keepdims=True)


def weight_grad(lefts, rights, kinds, weight=None):
    count = len(rights)
    rows, width = rights[0].shape
    columns = lefts[0].shape[1]
    half, tile = columns // kinds // 2, min(512, width)
    joined = len(lefts) == 1

    def left_spec(at):
        block = at if joined else 0
        return pl.BlockSpec((rows, columns), lambda step: (block, 0))

    lefts = list(lefts) * (count if joined else 1)
    weights = [] if weight is None else [weight]
    made = pl.pallas_call(
        partial(weight_grad_kernel, count, kinds, len(weights)),
        grid=(width // tile,),
        in_specs=[left_spec(at) for at in range(count)]
        + [pl.BlockSpec((rows, tile), lambda step: (0, step))] * count
        + [pl.BlockSpec((columns, tile), lambda step: (0, step))] * len(weights),
        out_specs=[pl.BlockSpec((half, tile), lambda step: (0, step))] * (2 * kinds)
        + [pl.BlockSpec((1, tile), lambda step: (0, step))] * len(weights),
        out_shape=[pltpu.HBM((half, width), f32)] * kinds
        + [pltpu.HBM((half, width), bf16)] * kinds
        + [jax.ShapeDtypeStruct((1, width), f32)] * len(weights),
        compiler_params=pltpu.CompilerParams(vmem_limit_bytes=40 << 20),
        cost_estimate=kernel_cost,
        name="weight_grad",
    )(*lefts, *rights, *weights)
    return list(zip(made[:kinds], made[kinds : 2 * kinds])), made[2 * kinds :]


def row_dot_kernel(rows, weight, out):
    out[...] = dot(rows[...], weight[...]).astype(out.dtype)


def row_dot(rows, weight, block, count, kind=f32):
    depth, width = weight.shape
    size, tile = rows.shape[0] // count, min(512, width)
    return pl.pallas_call(
        row_dot_kernel,
        grid=(width // tile,),
        in_specs=[
            pl.BlockSpec((size, depth), lambda step: (block, 0)),
            pl.BlockSpec((depth, tile), lambda step: (0, step)),
        ],
        out_specs=pl.BlockSpec((size, tile), lambda step: (0, step)),
        out_shape=pltpu.HBM((size, width), kind),
        compiler_params=pltpu.CompilerParams(vmem_limit_bytes=32 << 20),
        cost_estimate=kernel_cost,
        name="row_dot",
    )(rows, weight)


def join_kernel(count, tiles, *refs):
    out = refs[2 * count]
    for at in range(count):

        @pl.when(pl.program_id(0) // tiles == at)
        def _(at=at):
            out[...] = (refs[2 * at][...] + refs[2 * at + 1][...].astype(f32)).astype(bf16)


def join(*pairs):
    count = len(pairs)
    rows, width = pairs[0][0].shape
    tile = 128 if rows % 128 == 0 else rows // 2
    tiles = rows // tile

    def spec(at):
        return pl.BlockSpec((tile, width), lambda step: (jnp.clip(step - at * tiles, 0, tiles - 1), 0))

    return pl.pallas_call(
        partial(join_kernel, count, tiles),
        grid=(count * tiles,),
        in_specs=[spec(at) for at in range(count) for _ in range(2)],
        out_specs=pl.BlockSpec((tile, width), lambda step: (step, 0)),
        out_shape=pltpu.HBM((count * rows, width), bf16),
        compiler_params=pltpu.CompilerParams(vmem_limit_bytes=40 << 20),
        cost_estimate=kernel_cost,
        name="join",
    )(*[value for pair in pairs for value in pair])


def block_diagonal(weight):
    count, width, _ = weight.shape
    rows = [
        jnp.pad(weight[at], ((0, 0), (at * width, (count - 1 - at) * width))) for at in range(count)
    ]
    return jnp.concatenate(rows, axis=0)


def pack_gates(rate, into, block_width):
    def padded(values, width):
        return jnp.pad(values, ((0, 0), (0, width - values.shape[1])))

    channels = rate.shape[0]
    forward, back = [], []
    for start, stop, low, high, _ in gate_tiles(channels, block_width, 128):
        forward.append(
            jnp.concatenate(
                (padded(rate[low:high, start:stop], 128), padded(into[low:high, start:stop], 128)), axis=1
            )
        )
    for start, stop, low, high, _ in gate_tiles(channels, block_width, 256):
        back.append(padded(rate.T[low:high, start:stop], 256))
        back.append(padded(into.T[low:high, start:stop], 256))
    return jnp.concatenate(forward, axis=0), jnp.concatenate(back, axis=0)


def narrow_whole(weight, dim):
    return lax.all_gather(weight, "narrow", axis=dim, tiled=True)


def narrow_sum(grad, dim):
    return lax.psum_scatter(grad, "narrow", scatter_dimension=dim, tiled=True)


class DirectSum:
    def __init__(self, grad, got=()):
        self.size = lax.axis_size("narrow")
        self.grad, self.got = grad, list(got)

    def state(self):
        return self.grad, self.got

    def piece(self, flip):
        span = self.grad.shape[1] // self.size
        start = (lax.axis_index("narrow") ^ flip) * span
        return lax.dynamic_slice_in_dim(self.grad, start, span, axis=1)

    def send(self, flips):
        for flip in flips:
            pairs = [(at, at ^ flip) for at in range(self.size)]
            self.got.append(lax.ppermute(self.piece(flip), "narrow", pairs))

    def total(self):
        return plus(self.piece(0), *self.got)


def swap_cores(values, wide):
    return lax.ppermute(values, "wide", [(at, at ^ 1) for at in range(wide)])


def fence(*values):
    return lax.optimization_barrier(values)


class Chips:
    def __init__(self, wide, place):
        self.place, self.chip, self.count = place, place[0], wide // 2
        self.wide = wide

    def move(self, values, pairs):
        devices = [(2 * a + core, 2 * b + core) for a, b in pairs for core in range(2)]
        return lax.ppermute(values, "wide", devices)

    def ring(self, values):
        return self.move(values, [(at, (at + 1) % self.count) for at in range(self.count)])

    def gather_step(self, step, right, left):
        count = self.count
        to_right = [(at, at + 1) for at in range(step - 1, count - 1)]
        to_left = [(at, at - 1) for at in range(1, count - step + 1)]
        if 2 * step > count + 1:
            both = self.move(jnp.where(self.chip >= step - 1, right, left), to_right + to_left)
            return both, both
        return self.move(right, to_right), self.move(left, to_left)

    def gathered(self, hop, rights, lefts):
        return jnp.where(self.chip >= hop, rights[hop], lefts[self.count - hop])

    def sum_step(self, step, right, left):
        count = self.count
        to_right = [(at, at + 1) for at in range(step)]
        to_left = [(at, at - 1) for at in range(count - step, count)]
        if 2 * step < count - 1:
            both = self.move(jnp.where(self.chip < step, right, left), to_right + to_left)
            return both, both
        return self.move(right, to_right), self.move(left, to_left)


def advance_kernel(place, end_part, end_moved, mid_part, mid_moved, end, mid, *, inner):
    added = end_part[...].astype(f32) + end_moved[...].astype(f32)
    mid[...] = (mid_part[...].astype(f32) + mid_moved[...].astype(f32)).astype(bf16)
    if inner:
        edge = (place[0] == 0) | (place[0] == 3)

        @pl.when(edge)
        def _():
            end[...] = end_part[...].astype(bf16)

        @pl.when(jnp.logical_not(edge))
        def _():
            end[...] = end_moved[...]
    else:
        end[...] = added.astype(bf16)


def advance(place, end_part, end_moved, mid_part, mid_moved, inner):
    rows, width = end_moved.shape
    tile = min(64, rows)
    spec = pl.BlockSpec((tile, width), lambda step, place: (step, 0))
    return pl.pallas_call(
        partial(advance_kernel, inner=inner),
        grid_spec=pltpu.PrefetchScalarGridSpec(
            num_scalar_prefetch=1, grid=(rows // tile,), in_specs=[spec] * 4, out_specs=[spec] * 2
        ),
        out_shape=[pltpu.HBM((rows, width), bf16)] * 2,
        compiler_params=pltpu.CompilerParams(vmem_limit_bytes=32 << 20),
        cost_estimate=kernel_cost,
        name="advance",
    )(place, end_part, end_moved, mid_part, mid_moved)


class Exchange:
    def __init__(self, line, rows):
        self.line, self.own = line, rows
        self.packed = line.count == 4
        if self.packed:
            self.odd = line.chip % 2 == 1
            self.edge = (line.chip == 0) | (line.chip == 3)
        self.ends, self.mids, self.chosen = [], [], ()
        self.backs, self.moved = {0: (rows, rows)}, (0.0, 0.0)

    def pair(self, end, mid):
        self.ends.append(self.line.move(end, [(0, 1), (1, 0), (2, 3), (3, 2)]))
        self.mids.append(self.line.move(mid, [(1, 2), (2, 1)]))

    def step(self, number, parts):
        line, count = self.line, self.line.count
        if not self.packed:
            if number < count:
                self.backs[number] = line.gather_step(number, *self.backs[number - 1])
            if number > 1:
                sent = [
                    plus(parts[hop], self.moved[way]).astype(bf16)
                    for way, hop in enumerate((number - 1, count - number + 1))
                ]
                self.moved = line.sum_step(number - 1, *sent)
        elif number == 1:
            self.pair(self.own, self.own)
        elif number == 2:
            part = jnp.where(line.chip == 0, parts[1], parts[3]).astype(bf16)
            self.pair(jnp.where(self.edge, part, self.mids[0]), self.ends[0])
        elif number == 3:
            self.pair(*advance(line.place, parts[2], self.mids[1], parts[2], self.ends[1], True))
            self.chosen = (
                jnp.where(self.odd, parts[1], parts[3]),
                jnp.where(line.chip == 1, parts[3], parts[1]),
            )
        else:
            self.pair(
                *advance(line.place, self.chosen[0], self.mids[2], self.chosen[1], self.ends[2], False)
            )

    def fence(self, *values):
        state = (self.ends, self.mids, self.chosen, self.backs, self.moved)
        state, values = fence(state, values)
        self.ends, self.mids, self.chosen, self.backs, self.moved = state
        return values

    def arrived(self, number):
        if self.packed:
            if number == 1:
                return self.ends[0]
            if number == 2:
                return jnp.where(self.edge, self.ends[1], self.mids[1])
            return jnp.where(self.edge, self.ends[2], self.mids[0])
        return self.rows()[number] if number < self.line.count else None

    def rows(self):
        if self.packed:
            near, two, far = (self.arrived(number) for number in (1, 2, 3))
            return [self.own, jnp.where(self.odd, near, far), two, jnp.where(self.odd, far, near)]
        rights, lefts = ({at: pair[way] for at, pair in self.backs.items()} for way in range(2))
        hops = range(1, self.line.count)
        return [self.own] + [self.line.gathered(hop, rights, lefts) for hop in hops]

    def total(self, part):
        if self.packed:
            return plus(part, self.ends[3], self.mids[3])
        return plus(part, *self.moved)


def plus(total, *moved):
    total = total.astype(f32)
    for values in moved:
        total = total + (values.astype(f32) if isinstance(values, jax.Array) else values)
    return total


def paired_step(values, axis, bit):
    size = lax.axis_size(axis)
    return values + lax.ppermute(values, axis, [(at, at ^ bit) for at in range(size)])


def direct_sum(values, axis, stride=1):
    size = lax.axis_size(axis)
    terms = [values] + [
        lax.ppermute(values, axis, [(at, at ^ flip) for at in range(size)])
        for flip in range(stride, size, stride)
    ]
    while len(terms) > 1:
        terms = [left + right for left, right in zip(terms[::2], terms[1::2])]
    return terms[0]


def norm_forward(values, gain):
    scale = lax.rsqrt(jnp.mean(values * values, axis=-1, keepdims=True) + norm_eps)
    return scale, (values * scale * gain).astype(bf16)


def norm_backward(values, scale, gain, grad):
    unit = values * scale
    scaled = grad * gain
    back = scale * (scaled - unit * jnp.mean(scaled * unit, axis=-1, keepdims=True))
    return back, jnp.sum(grad * unit, axis=0)


def dot(left, right):
    return jnp.dot(left, right, preferred_element_type=f32)


def dot_nt(left, right):
    return lax.dot_general(left, right, (((1,), (1,)), ((), ())), preferred_element_type=f32)


def dot_tn(left, right):
    return lax.dot_general(left, right, (((0,), (0,)), ((), ())), preferred_element_type=f32)


def body(
    tokens, lengths, cotangent, first_gain, proj_in, conv_weight, conv_bias, rate_weight, rate_bias,
    input_weight, input_bias, decay_param, proj_out, second_gain, mlp_in, mlp_down,
):
    seq_count, local_len, width = tokens.shape
    wide = lax.axis_size("wide")
    chips = wide // 2
    me = lax.axis_index("wide")
    chip, core = me // 2, me % 2
    place = jnp.stack((chip, core)).astype(jnp.int32)
    channels = proj_in.shape[2]
    block_width = rate_weight.shape[1]
    seq_half = seq_count // 2
    block_shape = (2, seq_half, local_len, 2 * channels)
    line = Chips(wide, place)
    last = chips - 1

    def swap(values):
        return swap_cores(values, wide)

    def by_sequence(values):
        parts = values.reshape(2, seq_half * local_len, width)
        mine = jnp.where(core == 0, parts[0], parts[1])
        return jnp.concatenate((mine, swap(jnp.where(core == 0, parts[1], parts[0]))), axis=0)

    def both_orders(mine, other):
        return jnp.where(core == 0, jnp.stack((mine, other)), jnp.stack((other, mine)))

    def by_position(rows):
        own, other = jnp.split(rows, 2, axis=0)
        return both_orders(own, swap(other)).reshape(tokens.shape)

    def by_channel(values):
        mine, other = values[..., :channels], values[..., channels:]
        both = both_orders(mine, swap(other))
        return both.reshape(seq_count, *both.shape[2:])

    lengths = lax.dynamic_slice_in_dim(lengths, core * seq_half, seq_half)
    chunk = 2 * chip + (jnp.arange(2, dtype=jnp.int32) ^ core)
    positions = chunk[:, None] * local_len + jnp.arange(local_len, dtype=jnp.int32)
    mask = (positions[:, None, :] < lengths[None, :, None]).astype(f32).reshape(-1, 1)

    def both_cores(own, dim):
        return jnp.concatenate((own, swap(own)), axis=dim)

    own_in = narrow_whole(jnp.swapaxes(proj_in, 1, 2), 2)
    own_out = narrow_whole(proj_out, 1)
    own_mlp_in = narrow_whole(mlp_in, 1)
    own_down = narrow_whole(mlp_down, 1)
    tokens_f = by_sequence(tokens).astype(f32)
    scale_one, norm_in = norm_forward(tokens_f, first_gain)

    params = jnp.concatenate(
        (conv_weight, conv_bias[None], rate_bias[None], input_bias[None], decay_param[None]), axis=0
    )
    norm_in, params, cotangent = fence(norm_in, params, cotangent)

    def project(rows):
        return dot_nt(rows, whole_in).reshape(2, seq_half, local_len, 4 * channels)

    rows_first = [norm_in]
    for hop in range(1, chips):
        moved = line.ring(rows_first[-1])
        if hop == 1:
            out_grad = by_sequence(cotangent).astype(f32) * mask
            out_grad_b = out_grad.astype(bf16)
            params = both_cores(params, 1)
            gates = both_cores(jnp.stack((rate_weight, input_weight)), 1)
            gate_weight, gate_back = pack_gates(
                block_diagonal(gates[0]), block_diagonal(gates[1]), block_width
            )
            rate_scale = decay_scale * jax.nn.softplus(-params[7:8])
            moved, out_grad_b, gate_weight = fence(moved, out_grad_b, gate_weight)
        if hop == last - 1:
            moved, own_in = fence(moved, own_in)
        if hop == last:
            whole_in = both_cores(own_in, 1).reshape(-1, width)
            pre_blocks = [project(rows) for rows in rows_first]
            moved, out_grad_b, own_out, pre_blocks = fence(moved, out_grad_b, own_out, pre_blocks)
        rows_first.append(moved)

    lanes = Exchange(line, out_grad_b)
    lanes.step(1, None)
    whole_out = both_cores(own_out, 0)
    pre_blocks.append(project(rows_first[last]))
    mixed, conv, rate_gate, in_gate, states, final_state, conv_state = mixer_forward(
        pre_blocks, lengths, place, params[:4], params[4:5], gate_weight, params[5:7],
        rate_scale, block_width,
    )
    mixed_rows = mixed.reshape(chips, -1, 2 * channels)
    parts = {hop: dot(mixed_rows[hop], whole_out) for hop in (1, last)}
    parts, mixed_rows, final_state, conv_state = lanes.fence(
        parts, mixed_rows, final_state, conv_state
    )
    for step in range(2, chips + 1):
        lanes.step(step, parts)
        for hop in (step, chips - step):
            if hop < chips and hop not in parts:
                parts[hop] = dot(mixed_rows[hop], whole_out)
        if step == 2:
            final_state, conv_state = by_channel(final_state), by_channel(conv_state)
            parts, final_state, conv_state = lanes.fence(parts, final_state, conv_state)
        elif step == chips - 1:
            if 0 not in parts:
                parts[0] = dot(mixed_rows[0], whole_out)
            parts, own_mlp_in = lanes.fence(parts, own_mlp_in)
            other_mlp_in = swap(own_mlp_in)
        elif step < chips:
            (parts,) = lanes.fence(parts)
    rows_back = lanes.rows()
    parts, rows_back, own_down = lanes.fence(parts, rows_back, own_down)
    resid = tokens_f + lanes.total(parts[0])

    scale_two, norm_mid = norm_forward(resid, second_gain)
    norm_mid, own_down = fence(norm_mid, own_down)
    other_down = swap(own_down)
    rows_second = [norm_mid]
    hidden, gate_grads, up_grads, parts, outs = [], [], [], [], []
    sums = None
    for hop in range(chips):
        if hop < last:
            rows_second.append(line.ring(rows_second[hop]))
        if hop > 1:
            sums = line.ring(total_b)
        made = mlp_block(
            rows_second[hop], rows_back[hop], own_mlp_in, other_mlp_in, own_down, other_down
        )
        rows_second, made, sums = fence(rows_second, made, sums)
        for kept, value in zip((hidden, gate_grads, up_grads, parts, outs), made):
            kept.append(value)
        if hop:
            total = parts[hop] if sums is None else plus(parts[hop], sums)
            total_b = total.astype(bf16)
    sums = line.ring(total_b)
    [grads_gate], _ = weight_grad(gate_grads, rows_second, 1)
    [grads_down], _ = weight_grad(hidden, rows_back, 1)
    sums, grads_gate, grads_down, up_grads = fence(sums, grads_gate, grads_down, up_grads)
    mid_sum = plus(parts[0], sums)

    from_norm, gain_two = norm_backward(resid, scale_two, second_gain, mid_sum)
    resid_grad = out_grad + from_norm
    resid_grad_b = resid_grad.astype(bf16)
    resid_grad_b, up_grads, outs = fence(resid_grad_b, up_grads, outs)

    def back_block(rows):
        return dot_nt(rows, whole_out).reshape(2, seq_half, local_len, 2 * channels)

    lanes = Exchange(line, resid_grad_b)
    lanes.step(1, None)
    [grads_up], _ = weight_grad(up_grads, rows_second, 1)
    from_down = swap(grads_down[1])
    grads_up, from_down, outs = lanes.fence(grads_up, from_down, outs)
    back_blocks = [back_block(resid_grad_b)]
    for step in range(2, chips + 1):
        lanes.step(step, outs)
        if step == 2:
            part_down = join((grads_down[0], from_down))
            from_gate, from_up = swap(grads_gate[1]), swap(grads_up[1])
            part_down, from_gate, from_up = lanes.fence(part_down, from_gate, from_up)
            grad_mlp_down = narrow_sum(part_down, 1)
        elif step == 3:
            part_mlp_in = join((grads_gate[0], from_gate), (grads_up[0], from_up))
            if lanes.packed:
                back_blocks += [back_block(lanes.arrived(at)) for at in (1, 2)]
            part_mlp_in, back_blocks = lanes.fence(part_mlp_in, back_blocks)
            grad_mlp_in = narrow_sum(part_mlp_in, 1)
        elif step < chips:
            lanes.fence()
    if lanes.packed:
        back_blocks.append(back_block(lanes.arrived(3)))
    else:
        back_blocks += [back_block(rows) for rows in lanes.rows()[1:]]
    grads, small, gate_grads = mixer_backward(
        pre_blocks, back_blocks, lanes.packed, (conv, rate_gate, in_gate, states),
        lengths, place, params[:4], gate_back, rate_scale, block_width,
    )
    grad_rows = grads.reshape(-1, 4 * channels)
    part = row_dot(grad_rows, whole_in, 1, chips, bf16)
    part, grad_rows, small, gate_grads, mixed, grad_mlp_down = lanes.fence(
        part, grad_rows, small, gate_grads, mixed, grad_mlp_down
    )

    size = lax.axis_size("narrow")
    split = size // 2 + 1
    count = rate_weight.shape[0]

    def gate_rows(gates, sums):
        return jnp.concatenate((gates.reshape(-1, block_width), sums.reshape(-1, block_width)), axis=0)

    gate_mine = gate_rows(gate_grads[:count], small[:, :channels])
    gate_other = gate_rows(gate_grads[count:], small[:, channels:])
    sent = part
    for hop in range(1, chips):
        moving = line.ring(sent)
        part = row_dot(grad_rows, whole_in, (hop + 1) % chips, chips)
        if hop == 1:
            grads_in, [gain_one] = weight_grad([grad_rows], rows_first, 2, weight=whole_in)
            [grads_out], _ = weight_grad([mixed.reshape(-1, 2 * channels)], lanes.rows(), 1)
            gate_sum = (gate_mine + swap(gate_other.astype(bf16)).astype(f32)).astype(bf16)
            grads_in, grads_out, gain_one, moving, part, gate_sum, resid = fence(
                grads_in, grads_out, gain_one, moving, part, gate_sum, resid
            )
        elif hop == 2:
            parts = join(*[(own, swap(other)) for own, other in (*grads_in, grads_out)])
            gains = jnp.concatenate((gain_one / first_gain, gain_two[None]), axis=0)
            gains = direct_sum(gains, "narrow")
            gate_sum = paired_step(gate_sum, "narrow", 1)
            parts, moving, part, grad_mlp_in, gains, gate_sum, resid = fence(
                parts, moving, part, grad_mlp_in, gains, gate_sum, resid
            )
        elif hop == last:
            sum_proj = DirectSum(parts)
            sum_proj.send(range(1, split))
            output = by_position((resid + lanes.total(outs[0])).astype(bf16))
            bit = 2
            while bit < size:
                gate_sum = paired_step(gate_sum, "narrow", bit)
                bit *= 2
            moving, sum_proj.got, parts, gains, gate_sum, output = fence(
                moving, sum_proj.got, parts, gains, gate_sum, output
            )
        sent = plus(part, moving).astype(bf16)
    in_sum = plus(part, moving)
    sum_proj.grad = parts
    sum_proj.send(range(split, size))
    gains = gains + swap(gains)
    gains = direct_sum(gains, "wide", 2)
    from_norm, _ = norm_backward(tokens_f, scale_one, first_gain, in_sum)
    grad_tokens = (resid_grad + from_norm).astype(bf16)
    grad_tokens, gains = fence(grad_tokens, gains)
    grad_proj = sum_proj.total()
    gate_sum = gate_sum.astype(f32)
    gate_grads = gate_sum[: count * 2 * block_width].reshape(count, 2, block_width, block_width)
    small = gate_sum[count * 2 * block_width :].reshape(8, channels)
    grad_mlp_in, grad_mlp_down = grad_mlp_in.astype(f32), grad_mlp_down.astype(f32)
    grad_proj_in = grad_proj[: 2 * channels].reshape(2, channels, -1)
    grad_proj_out = grad_proj[2 * channels :]
    grad_mlp_in = grad_mlp_in.reshape(2, mlp_in.shape[2], -1)
    return (
        output,
        by_position(grad_tokens),
        final_state,
        conv_state,
        gains[0],
        jnp.swapaxes(grad_proj_in, 1, 2),
        small[4:8],
        small[3],
        gate_grads[:, 0],
        small[0],
        gate_grads[:, 1],
        small[1],
        small[2] * decay_scale * jax.nn.sigmoid(-decay_param),
        grad_proj_out,
        gains[1],
        jnp.swapaxes(grad_mlp_in, 1, 2),
        grad_mlp_down,
    )


def solution(mesh):
    return jax.shard_map(
        body,
        mesh=mesh,
        in_specs=(
            P("narrow", "wide", None),
            P("narrow"),
            P("narrow", "wide", None),
            P(),
            P(None, "narrow", "wide"),
            P(None, "wide"),
            P("wide"),
            P("wide", None, None),
            P("wide"),
            P("wide", None, None),
            P("wide"),
            P("wide"),
            P("wide", "narrow"),
            P(),
            P(None, "narrow", "wide"),
            P("wide", "narrow"),
        ),
        out_specs=(
            P("narrow", "wide", None),
            P("narrow", "wide", None),
            P("narrow", "wide"),
            P("narrow", None, "wide"),
            P(),
            P(None, "narrow", "wide"),
            P(None, "wide"),
            P("wide"),
            P("wide", None, None),
            P("wide"),
            P("wide", None, None),
            P("wide"),
            P("wide"),
            P("wide", "narrow"),
            P(),
            P(None, "narrow", "wide"),
            P("wide", "narrow"),
        ),
        check_vma=False,
    )
```

```python
from functools import partial

import jax
import jax.numpy as jnp
from jax import lax
from jax.experimental import pallas as pl
from jax.experimental.pallas import tpu as pltpu
from jax.sharding import PartitionSpec as P

decay_scale = 8.0
norm_eps = 1e-06
gelu_in = 0.7978845608028654
gelu_cube = 0.044715
f32 = jnp.float32
bf16 = jnp.bfloat16
kernel_cost = pl.CostEstimate(flops=1, bytes_accessed=1, transcendentals=0)
chain_cost = pl.CostEstimate(flops=1, bytes_accessed=1 << 26, transcendentals=0)


def gelu_tanh(v):
    return jnp.tanh(gelu_in * (v + gelu_cube * v * v * v))


def gelu_pair(v):
    t = gelu_tanh(v)
    half = 0.5 * (1.0 + t)
    slope = half + 0.5 * v * (1.0 - t * t) * (gelu_in + (3.0 * gelu_in * gelu_cube) * v * v)
    return v * half, slope


def one_minus_exp(v, decay):
    series = 1.0 - v * (1.0 / 7.0)
    for order in (6.0, 5.0, 4.0, 3.0, 2.0):
        series = 1.0 - v * (1.0 / order) * series
    return jnp.where(v < 0.3, v * series, 1.0 - decay * decay)


def gate_tiles(channels, block_width, tile):
    tiles, offset = [], 0
    for start in range(0, channels, tile):
        stop = min(start + tile, channels)
        low = start // block_width * block_width // 128 * 128
        high = min(-(-((stop - 1) // block_width + 1) * block_width // 128) * 128, channels)
        tiles.append((start, stop, low, high, offset))
        offset += high - low
    return tiles


def split_rows(values):
    high = values.astype(bf16)
    return jnp.concatenate((high, (values - high.astype(f32)).astype(bf16)), axis=0)


def joined_dot(halves, weight):
    both = jnp.dot(halves, weight, preferred_element_type=f32)
    rows = both.shape[0] // 2
    return both[:rows] + both[rows:]


def tile_scan(decay, drive, backward):
    rows, channels = decay.shape
    a = decay.reshape(rows // 8, 8, channels)
    b = drive.reshape(rows // 8, 8, channels)
    row = lax.broadcasted_iota(jnp.int32, (1, 8, channels), 1)
    for step in (1, 2, 4):
        if backward:
            keep, shift = row < 8 - step, 8 - step
        else:
            keep, shift = row >= step, step
        a_moved = jnp.where(keep, pltpu.roll(a, shift, 1), 1.0)
        b_moved = jnp.where(keep, pltpu.roll(b, shift, 1), 0.0)
        b = b + a * b_moved
        a = a * a_moved
    return a, b


def mixer_forward_kernel(
    chips, block_width, place, lengths, *refs
):
    pre_refs, refs = refs[:chips], refs[chips:]
    conv_weight, conv_bias, gate_weight, gate_bias, rate_scale = refs[:5]
    mixed, *saved = refs[5:15]
    final_state, conv_state, pre_now, x_tail, carry = refs[15:]
    chunk = pl.program_id(0)
    seq_count, local_len, channels = pre_now.shape
    channels //= 2
    pick_block(chunk, place, chips, pre_refs, pre_now)

    @pl.when(chunk == 0)
    def _():
        x_tail[...] = jnp.zeros_like(x_tail)
        carry[...] = jnp.zeros_like(carry)

    convs = []
    for seq in range(seq_count):
        x = pre_now[seq, :, channels:]
        extended = jnp.concatenate((x_tail[seq], x), axis=0)
        conv = conv_bias[...] + conv_weight[0:1] * x
        for lag in range(1, 4):
            conv = conv + conv_weight[lag : lag + 1] * extended[8 - lag : 8 - lag + local_len]
        x_tail[seq] = x[local_len - 8 :]
        convs.append(conv)
        for tap in range(3):
            position = lengths[seq] - 3 + tap

            @pl.when(position // local_len == chunk)
            def _(seq=seq, tap=tap, position=position):
                conv_state[seq, tap : tap + 1] = pre_now[
                    seq, pl.ds(lax.rem(position, local_len), 1), channels:
                ]

    conv_all = jnp.concatenate(convs, axis=0)
    parted = split_rows(conv_all)
    rate_parts, in_parts = [], []
    for start, stop, low, high, at in gate_tiles(channels, block_width, 128):
        both = joined_dot(parted[:, low:high], gate_weight[at : at + high - low])
        rate_parts.append(both[:, : stop - start])
        in_parts.append(both[:, 128 : 128 + stop - start])
    rate_all = jax.nn.sigmoid(jnp.concatenate(rate_parts, axis=1) + gate_bias[0:1])
    in_all = jax.nn.sigmoid(jnp.concatenate(in_parts, axis=1) + gate_bias[1:2])
    for seq in range(seq_count):
        rows = slice(seq * local_len, (seq + 1) * local_len)
        conv = convs[seq]
        rate_gate = rate_all[rows]
        in_gate = in_all[rows]
        step_log = rate_scale[...] * rate_gate
        decay = jnp.exp(-step_log)
        square = jnp.maximum(one_minus_exp(2.0 * step_log, decay), 1e-36)
        inverse_root = lax.rsqrt(square)
        root = square * inverse_root
        position = chunk * local_len + lax.broadcasted_iota(jnp.int32, (local_len, 1), 0)
        live = position < lengths[seq]
        gated_conv = in_gate * conv
        driven = root * gated_conv
        kept_decay = jnp.where(live, decay, 1.0)
        a, b = tile_scan(kept_decay, jnp.where(live, driven, 0.0), False)
        last = carry[seq]
        tiles = []
        for tile in range(local_len // 8):
            tiles.append(b[tile] + a[tile] * last)
            last = tiles[-1][7:8]
        states = jnp.concatenate(tiles, axis=0)
        carry[seq] = last
        final_state[seq : seq + 1] = last
        gated, slope = gelu_pair(pre_now[seq, :, :channels])
        mixed[0, 0, seq] = (gated * states).astype(bf16)
        rate_factor = (states - driven - gated_conv * decay * decay * inverse_root) * rate_gate
        for out, value in zip(
            saved,
            (
                gated,
                slope * states,
                kept_decay,
                rate_factor,
                -rate_scale[...] * rate_factor * (1.0 - rate_gate),
                driven * (1.0 - in_gate),
                root * in_gate,
                pre_now[seq, :, channels:],
                conv.astype(bf16),
            ),
        ):
            out[0, 0, seq] = value


def mixer_backward_kernel(
    chips, block_width, crossed, place, lengths, *refs
):
    back_refs, refs = refs[:chips], refs[chips:]
    gated_in, y_in, decay_in, rate_in, rate_pre_in, in_pre_in, direct_in, x_in, conv_in = refs[:9]
    conv_weight, gate_back, grads, sums, gate_grads = refs[9:14]
    back_now, carry, grad_head, gate_sums = refs[14:]
    step = pl.program_id(0)
    chunk = pl.num_programs(0) - 1 - step
    seq_count, local_len, channels = back_now.shape
    pick_block(chunk, place, chips, back_refs, back_now, crossed)

    @pl.when(step == 0)
    def _():
        carry[...] = jnp.zeros_like(carry)
        grad_head[...] = jnp.zeros_like(grad_head)
        sums[...] = jnp.zeros_like(sums)
        gate_sums[...] = jnp.zeros_like(gate_sums)

    rate_pre, in_pre, direct = [], [], []
    decay_sum = jnp.zeros((1, channels), f32)
    for seq in range(seq_count):
        position = chunk * local_len + lax.broadcasted_iota(jnp.int32, (local_len, 1), 0)
        live = position < lengths[seq]
        mixer_grad = back_now[seq]
        grads[0, 0, seq, :, :channels] = (mixer_grad * y_in[0, 0, seq]).astype(bf16)
        source = mixer_grad * gated_in[0, 0, seq]
        decay = decay_in[0, 0, seq]
        a, b = tile_scan(decay, decay * source, True)
        following = carry[seq]
        tiles = []
        for tile in reversed(range(local_len // 8)):
            passed = b[tile] + a[tile] * following
            tiles.append(jnp.concatenate((passed[1:], following), axis=0))
            following = passed[0:1]
        carry[seq] = following
        adjoint = source + jnp.concatenate(tiles[::-1], axis=0)
        adjoint = jnp.where(live, adjoint, 0.0)
        decay_sum = decay_sum + jnp.sum(adjoint * rate_in[0, 0, seq], axis=0, keepdims=True)
        rate_pre.append(adjoint * rate_pre_in[0, 0, seq])
        in_pre.append(adjoint * in_pre_in[0, 0, seq])
        direct.append(adjoint * direct_in[0, 0, seq])
    rate_all = jnp.concatenate(rate_pre, axis=0)
    in_all = jnp.concatenate(in_pre, axis=0)
    conv_all = jnp.concatenate([conv_in[0, 0, seq] for seq in range(seq_count)], axis=0)
    rate_b, in_b = rate_all.astype(bf16), in_all.astype(bf16)
    for start, stop, low, high, at in gate_tiles(channels, block_width, 128):
        both = jnp.concatenate((rate_b[:, start:stop], in_b[:, start:stop]), axis=1)
        part = lax.dot_general(
            conv_all[:, low:high], both, (((0,), (0,)), ((), ())), preferred_element_type=f32
        )
        if stop - start == 128:
            gate_sums[at : at + high - low] += part
        else:
            gate_sums[at : at + high - low, : stop - start] += part[:, : stop - start]
            gate_sums[at : at + high - low, 128 : 128 + stop - start] += part[:, stop - start :]
    parts = []
    for start, stop, low, high, at in gate_tiles(channels, block_width, 256):
        both = jnp.concatenate((rate_b[:, low:high], in_b[:, low:high]), axis=1)
        parts.append(dot(both, gate_back[2 * at : 2 * (at + high - low)])[:, : stop - start])
    conv_grad = jnp.concatenate(direct, axis=0) + jnp.concatenate(parts, axis=1)
    tap_sums = [jnp.zeros((1, channels), f32) for _ in range(4)]
    for seq in range(seq_count):
        part = conv_grad[seq * local_len : (seq + 1) * local_len]
        extended = jnp.concatenate((part, grad_head[seq]), axis=0)
        x = x_in[0, 0, seq]
        total = conv_weight[0:1] * part
        tap_sums[0] = tap_sums[0] + jnp.sum(part * x, axis=0, keepdims=True)
        for lag in range(1, 4):
            moved = extended[lag : lag + local_len]
            total = total + conv_weight[lag : lag + 1] * moved
            tap_sums[lag] = tap_sums[lag] + jnp.sum(moved * x, axis=0, keepdims=True)
        grads[0, 0, seq, :, channels:] = total.astype(bf16)
        grad_head[seq] = part[:8]
    sums[0:1] += jnp.sum(rate_all, axis=0, keepdims=True)
    sums[1:2] += jnp.sum(in_all, axis=0, keepdims=True)
    sums[2:3] += decay_sum
    sums[3:4] += jnp.sum(conv_grad, axis=0, keepdims=True)
    for lag in range(4):
        sums[4 + lag : 5 + lag] += tap_sums[lag]

    @pl.when(chunk == 0)
    def _():
        tiles = gate_tiles(channels, block_width, 128)
        for kind, column in enumerate((0, 128)):
            for base in range(0, channels, block_width):
                pieces = []
                for start, stop, low, _, at in tiles:
                    left, right = max(start, base), min(stop, base + block_width)
                    if left < right:
                        row = at + base - low
                        span = gate_sums[row : row + block_width, column : column + 128]
                        pieces.append(span[:, left - start : right - start])
                gate_grads[base // block_width, kind] = jnp.concatenate(pieces, axis=1)


def chunk_place(chunk, place, chips):
    return lax.rem(place[0] - chunk // 2 + chips, chips), lax.rem(chunk + place[1], 2)


def pick_block(chunk, place, chips, refs, now, crossed=False):
    slot = (chunk // 2) ^ place[0] if crossed else chunk_place(chunk, place, chips)[0]
    for hop in range(chips):

        @pl.when(slot == hop)
        def _(hop=hop):
            now[...] = refs[hop][0]


def mixer_specs(shape, chips, chunk_of):
    def hop_map(hop, crossed, step, place, lengths):
        first = 2 * (place[0] ^ hop if crossed else lax.rem(place[0] - hop + chips, chips))
        return (jnp.where(chunk_of(step) <= first, place[1], 1 - place[1]), 0, 0, 0)

    def block_map(step, place, lengths):
        chip, core = chunk_place(chunk_of(step), place, chips)
        return (chip, core, 0, 0, 0)

    def hops(lanes, crossed=False):
        block = (1, *shape[1:3], lanes)
        return [pl.BlockSpec(block, partial(hop_map, hop, crossed)) for hop in range(chips)]

    def block(lanes):
        return pl.BlockSpec((1, 1, *shape[1:3], lanes), block_map)

    return hops, block


def whole_spec(shape):
    return pl.BlockSpec(shape, lambda step, place, lengths: (0,) * len(shape))


def mixer_forward(
    pre_blocks, lengths, place, conv_weight, conv_bias, gate_weight, gate_bias, rate_scale, block_width
):
    chips = len(pre_blocks)
    _, seq_count, local_len, channels = pre_blocks[0].shape
    channels //= 2
    hops, block = mixer_specs(pre_blocks[0].shape, chips, lambda step: step)
    full = (chips, 2, seq_count, local_len, channels)
    params = (conv_weight, conv_bias, gate_weight, gate_bias, rate_scale)
    return pl.pallas_call(
        partial(mixer_forward_kernel, chips, block_width),
        grid_spec=pltpu.PrefetchScalarGridSpec(
            num_scalar_prefetch=2,
            grid=(2 * chips,),
            in_specs=hops(2 * channels) + [whole_spec(param.shape) for param in params],
            out_specs=[block(channels)] * 10
            + [whole_spec((seq_count, channels)), whole_spec((seq_count, 3, channels))],
            scratch_shapes=[
                pltpu.VMEM((seq_count, local_len, 2 * channels), f32),
                pltpu.VMEM((seq_count, 8, channels), f32),
                pltpu.VMEM((seq_count, 1, channels), f32),
            ],
        ),
        out_shape=[pltpu.HBM(full, bf16)]
        + [pltpu.HBM(full, f32)] * 8
        + [pltpu.HBM(full, bf16)]
        + [
            jax.ShapeDtypeStruct((seq_count, channels), f32),
            jax.ShapeDtypeStruct((seq_count, 3, channels), f32),
        ],
        compiler_params=pltpu.CompilerParams(vmem_limit_bytes=32 << 20),
        cost_estimate=kernel_cost,
        name="mixer_forward",
    )(place, lengths, *pre_blocks, *params)


def mixer_backward(
    back_blocks, crossed, saved, lengths, place, conv_weight, gate_back, block_width
):
    chips = len(back_blocks)
    _, seq_count, local_len, channels = back_blocks[0].shape
    hops, block = mixer_specs(back_blocks[0].shape, chips, lambda step: 2 * chips - 1 - step)
    full = (chips, 2, seq_count, local_len, channels)
    params = (conv_weight, gate_back)
    packed = gate_tiles(channels, block_width, 128)[-1]
    packed = packed[4] + packed[3] - packed[2]
    gate_shape = (channels // block_width, 2, block_width, block_width)
    return pl.pallas_call(
        partial(mixer_backward_kernel, chips, block_width, crossed),
        grid_spec=pltpu.PrefetchScalarGridSpec(
            num_scalar_prefetch=2,
            grid=(2 * chips,),
            in_specs=hops(channels, crossed)
            + [block(channels)] * 9
            + [whole_spec(param.shape) for param in params],
            out_specs=[block(2 * channels), whole_spec((8, channels)), whole_spec(gate_shape)],
            scratch_shapes=[
                pltpu.VMEM((seq_count, local_len, channels), f32),
                pltpu.VMEM((seq_count, 1, channels), f32),
                pltpu.VMEM((seq_count, 8, channels), f32),
                pltpu.VMEM((packed, 256), f32),
            ],
        ),
        out_shape=[
            pltpu.HBM((*full[:-1], 2 * channels), bf16),
            jax.ShapeDtypeStruct((8, channels), f32),
            jax.ShapeDtypeStruct(gate_shape, f32),
        ],
        compiler_params=pltpu.CompilerParams(vmem_limit_bytes=32 << 20),
        cost_estimate=kernel_cost,
        name="mixer_backward",
    )(place, lengths, *back_blocks, *saved, *params)


def mlp_kernel(tiles, rows, back, own_in, other_in, own_down, other_down, *refs):
    hidden, gate_grads, up_grads, middle, out, middle_sum, out_sum = refs
    step = pl.program_id(0)

    @pl.when(step == 0)
    def _():
        middle_sum[...] = jnp.zeros_like(middle_sum)
        out_sum[...] = jnp.zeros_like(out_sum)

    def units(weight_in, weight_down):
        gated, slope = gelu_pair(dot(rows[...], weight_in[0]))
        up_pre = dot(rows[...], weight_in[1])
        hidden_grad = dot_nt(back[...], weight_down[...])
        hidden_b = (gated * up_pre).astype(bf16)
        gate_b = (hidden_grad * up_pre * slope).astype(bf16)
        up_b = (hidden_grad * gated).astype(bf16)
        hidden[...] = hidden_b
        gate_grads[...] = gate_b
        up_grads[...] = up_b
        out_sum[...] += dot(hidden_b, weight_down[...])
        middle_sum[...] += dot_nt(gate_b, weight_in[0]) + dot_nt(up_b, weight_in[1])

    @pl.when(step < tiles)
    def _():
        units(own_in, own_down)

    @pl.when(step >= tiles)
    def _():
        units(other_in, other_down)

    @pl.when(step == 2 * tiles - 1)
    def _():
        middle[...] = middle_sum[...]
        out[...] = out_sum[...].astype(bf16)


def mlp_block(rows, back, own_in, other_in, own_down, other_down):
    count, width = rows.shape
    units = own_down.shape[0]
    tile = 256 if units % 256 == 0 else 128
    tiles = units // tile

    def own_tile(step):
        return jnp.minimum(step, tiles - 1)

    def other_tile(step):
        return jnp.maximum(step - tiles, 0)

    whole = pl.BlockSpec((count, width), lambda step: (0, 0))
    tiled = pl.BlockSpec((count, tile), lambda step: (0, step))
    return pl.pallas_call(
        partial(mlp_kernel, tiles),
        grid=(2 * tiles,),
        in_specs=[
            whole,
            whole,
            pl.BlockSpec((2, width, tile), lambda step: (0, 0, own_tile(step))),
            pl.BlockSpec((2, width, tile), lambda step: (0, 0, other_tile(step))),
            pl.BlockSpec((tile, width), lambda step: (own_tile(step), 0)),
            pl.BlockSpec((tile, width), lambda step: (other_tile(step), 0)),
        ],
        out_specs=[tiled] * 3 + [whole] * 2,
        out_shape=[pltpu.HBM((count, 2 * units), bf16)] * 3
        + [pltpu.HBM((count, width), f32), pltpu.HBM((count, width), bf16)],
        scratch_shapes=[pltpu.VMEM((count, width), f32)] * 2,
        compiler_params=pltpu.CompilerParams(vmem_limit_bytes=36 << 20),
        cost_estimate=kernel_cost,
        name="mlp_block",
    )(rows, back, own_in, other_in, own_down, other_down)


def weight_grad_kernel(count, kinds, weighted, *refs):
    lefts, rights = refs[:count], refs[count : 2 * count]
    outs = refs[2 * count + weighted :]
    total = dot_tn(lefts[0][...], rights[0][...])
    for left, right in zip(lefts[1:], rights[1:]):
        total = total + dot_tn(left[...], right[...])
    half = outs[0].shape[0]
    for kind in range(kinds):
        start = 2 * kind * half
        outs[kind][...] = total[start : start + half]
        outs[kinds + kind][...] = total[start + half : start + 2 * half].astype(bf16)
    if weighted:
        weight = refs[2 * count][...]
        outs[2 * kinds][...] = jnp.sum(total * weight.astype(f32), axis=0, keepdims=True)


def weight_grad(lefts, rights, kinds, weight=None):
    count = len(rights)
    rows, width = rights[0].shape
    columns = lefts[0].shape[1]
    half, tile = columns // kinds // 2, min(512, width)
    joined = len(lefts) == 1

    def left_spec(at):
        block = at if joined else 0
        return pl.BlockSpec((rows, columns), lambda step: (block, 0))

    lefts = list(lefts) * (count if joined else 1)
    weights = [] if weight is None else [weight]
    made = pl.pallas_call(
        partial(weight_grad_kernel, count, kinds, len(weights)),
        grid=(width // tile,),
        in_specs=[left_spec(at) for at in range(count)]
        + [pl.BlockSpec((rows, tile), lambda step: (0, step))] * count
        + [pl.BlockSpec((columns, tile), lambda step: (0, step))] * len(weights),
        out_specs=[pl.BlockSpec((half, tile), lambda step: (0, step))] * (2 * kinds)
        + [pl.BlockSpec((1, tile), lambda step: (0, step))] * len(weights),
        out_shape=[pltpu.HBM((half, width), f32)] * kinds
        + [pltpu.HBM((half, width), bf16)] * kinds
        + [jax.ShapeDtypeStruct((1, width), f32)] * len(weights),
        compiler_params=pltpu.CompilerParams(vmem_limit_bytes=28 << 20),
        cost_estimate=kernel_cost,
        name="weight_grad",
    )(*lefts, *rights, *weights)
    return list(zip(made[:kinds], made[kinds : 2 * kinds])), made[2 * kinds :]


def row_dot_kernel(rows, weight, *refs):
    total = dot(rows[...], weight[...])
    if len(refs) > 1:
        total = total + refs[0][...].astype(f32)
    refs[-1][...] = total.astype(refs[-1].dtype)


def row_dot(rows, weight, block, count, kind=f32, moving=()):
    depth, width = weight.shape
    size, tile = rows.shape[0] // count, min(512, width)
    return pl.pallas_call(
        row_dot_kernel,
        grid=(width // tile,),
        in_specs=[
            pl.BlockSpec((size, depth), lambda step: (block, 0)),
            pl.BlockSpec((depth, tile), lambda step: (0, step)),
        ]
        + [pl.BlockSpec((size, tile), lambda step: (0, step))] * len(moving),
        out_specs=pl.BlockSpec((size, tile), lambda step: (0, step)),
        out_shape=pltpu.HBM((size, width), kind),
        compiler_params=pltpu.CompilerParams(vmem_limit_bytes=10 << 20),
        cost_estimate=chain_cost if moving else kernel_cost,
        name="row_dot",
    )(rows, weight, *moving)


def join_kernel(count, tiles, *refs):
    out = refs[-1]
    for at in range(count):

        @pl.when(pl.program_id(0) // tiles == at)
        def _(at=at):
            out[...] = (refs[2 * at][...] + refs[2 * at + 1][...].astype(f32)).astype(bf16)


def join(*pairs, slots=1, slot=0, filled=(), tile=128):
    count = len(pairs)
    rows, width = pairs[0][0].shape
    tile = tile if rows % tile == 0 else rows // 2
    tiles = rows // tile

    def spec(at):
        return pl.BlockSpec((tile, width), lambda step: (jnp.clip(step - at * tiles, 0, tiles - 1), 0))

    return pl.pallas_call(
        partial(join_kernel, count, tiles),
        grid=(count * tiles,),
        in_specs=[spec(at) for at in range(count) for _ in range(2)]
        + [pl.BlockSpec(memory_space=pl.ANY)] * len(filled),
        out_specs=pl.BlockSpec((tile, width), lambda step: (slot * count * tiles + step, 0)),
        out_shape=pltpu.HBM((slots * count * rows, width), bf16),
        input_output_aliases={2 * count: 0} if filled else {},
        compiler_params=pltpu.CompilerParams(vmem_limit_bytes=16 << 20),
        cost_estimate=kernel_cost,
        name="join",
    )(*[value for pair in pairs for value in pair], *filled)


def block_diagonal(weight):
    count, width, _ = weight.shape
    rows = [
        jnp.pad(weight[at], ((0, 0), (at * width, (count - 1 - at) * width))) for at in range(count)
    ]
    return jnp.concatenate(rows, axis=0)


def pack_gates(rate, into, block_width):
    def padded(values, width):
        return jnp.pad(values, ((0, 0), (0, width - values.shape[1])))

    channels = rate.shape[0]
    forward, back = [], []
    for start, stop, low, high, _ in gate_tiles(channels, block_width, 128):
        forward.append(
            jnp.concatenate(
                (padded(rate[low:high, start:stop], 128), padded(into[low:high, start:stop], 128)), axis=1
            )
        )
    for start, stop, low, high, _ in gate_tiles(channels, block_width, 256):
        back.append(padded(rate.T[low:high, start:stop], 256))
        back.append(padded(into.T[low:high, start:stop], 256))
    return jnp.concatenate(forward, axis=0), jnp.concatenate(back, axis=0)


def narrow_whole(weight, dim):
    return lax.all_gather(weight, "narrow", axis=dim, tiled=True)


def narrow_sum(grad, dim):
    return lax.psum_scatter(grad, "narrow", scatter_dimension=dim, tiled=True)


class DirectSum:
    def __init__(self, grad):
        self.size = lax.axis_size("narrow")
        self.grad, self.got = grad, []

    def piece(self, flip):
        span = self.grad.shape[1] // self.size
        start = (lax.axis_index("narrow") ^ flip) * span
        return lax.dynamic_slice_in_dim(self.grad, start, span, axis=1)

    def send(self, flips):
        for flip in flips:
            pairs = [(at, at ^ flip) for at in range(self.size)]
            self.got.append(lax.ppermute(self.piece(flip), "narrow", pairs))

    def total(self):
        return plus(self.piece(0), *self.got)


def swap_cores(values, wide):
    return lax.ppermute(values, "wide", [(at, at ^ 1) for at in range(wide)])


def fence(*values):
    return lax.optimization_barrier(values)


class Chips:
    def __init__(self, wide, place):
        self.place, self.chip, self.count = place, place[0], wide // 2
        self.wide = wide

    def move(self, values, pairs):
        devices = [(2 * a + core, 2 * b + core) for a, b in pairs for core in range(2)]
        return lax.ppermute(values, "wide", devices)

    def ring(self, values):
        return self.move(values, [(at, (at + 1) % self.count) for at in range(self.count)])

    def gather_step(self, step, right, left):
        count = self.count
        to_right = [(at, at + 1) for at in range(step - 1, count - 1)]
        to_left = [(at, at - 1) for at in range(1, count - step + 1)]
        if 2 * step > count + 1:
            both = self.move(jnp.where(self.chip >= step - 1, right, left), to_right + to_left)
            return both, both
        return self.move(right, to_right), self.move(left, to_left)

    def gathered(self, hop, rights, lefts):
        return jnp.where(self.chip >= hop, rights[hop], lefts[self.count - hop])

    def sum_step(self, step, right, left):
        count = self.count
        to_right = [(at, at + 1) for at in range(step)]
        to_left = [(at, at - 1) for at in range(count - step, count)]
        if 2 * step < count - 1:
            both = self.move(jnp.where(self.chip < step, right, left), to_right + to_left)
            return both, both
        return self.move(right, to_right), self.move(left, to_left)


def advance_kernel(place, end_part, end_moved, mid_part, mid_moved, end, mid, *, inner):
    added = end_part[...].astype(f32) + end_moved[...].astype(f32)
    mid[...] = (mid_part[...].astype(f32) + mid_moved[...].astype(f32)).astype(bf16)
    if inner:
        edge = (place[0] == 0) | (place[0] == 3)

        @pl.when(edge)
        def _():
            end[...] = end_part[...].astype(bf16)

        @pl.when(jnp.logical_not(edge))
        def _():
            end[...] = end_moved[...]
    else:
        end[...] = added.astype(bf16)


def advance(place, end_part, end_moved, mid_part, mid_moved, inner):
    rows, width = end_moved.shape
    tile = min(64, rows)
    spec = pl.BlockSpec((tile, width), lambda step, place: (step, 0))
    return pl.pallas_call(
        partial(advance_kernel, inner=inner),
        grid_spec=pltpu.PrefetchScalarGridSpec(
            num_scalar_prefetch=1, grid=(rows // tile,), in_specs=[spec] * 4, out_specs=[spec] * 2
        ),
        out_shape=[pltpu.HBM((rows, width), bf16)] * 2,
        compiler_params=pltpu.CompilerParams(vmem_limit_bytes=8 << 20),
        cost_estimate=kernel_cost,
        name="advance",
    )(place, end_part, end_moved, mid_part, mid_moved)


class Exchange:
    def __init__(self, line, rows):
        self.line, self.own = line, rows
        self.packed = line.count == 4
        if self.packed:
            self.odd = line.chip % 2 == 1
            self.edge = (line.chip == 0) | (line.chip == 3)
        self.ends, self.mids, self.chosen = [], [], ()
        self.backs, self.moved = {0: (rows, rows)}, (0.0, 0.0)

    def pair(self, end, mid):
        self.ends.append(self.line.move(end, [(0, 1), (1, 0), (2, 3), (3, 2)]))
        self.mids.append(self.line.move(mid, [(1, 2), (2, 1)]))

    def first(self, choose):
        if self.packed:
            self.chosen = (choose(self.line.chip == 0, 1, 3),)

    def step(self, number, choose):
        line, count = self.line, self.line.count
        if not self.packed:
            if number < count:
                self.backs[number] = line.gather_step(number, *self.backs[number - 1])
            if number > 1:
                sent = [
                    plus(choose(True, hop, hop), self.moved[way]).astype(bf16)
                    for way, hop in enumerate((number - 1, count - number + 1))
                ]
                self.moved = line.sum_step(number - 1, *sent)
        elif number == 1:
            self.pair(self.own, self.own)
        elif number == 2:
            self.pair(jnp.where(self.edge, self.chosen[0], self.mids[0]), self.ends[0])
            self.chosen = (choose(self.odd, 1, 3), choose(line.chip == 1, 3, 1), choose(True, 2, 2))
        elif number == 3:
            end, mid, two = self.chosen
            self.pair(*advance(line.place, two, self.mids[1], two, self.ends[1], True))
        else:
            end, mid, _ = self.chosen
            self.pair(*advance(line.place, end, self.mids[2], mid, self.ends[2], False))

    def fence(self, *values):
        state = (self.ends, self.mids, self.chosen, self.backs, self.moved)
        state, values = fence(state, values)
        self.ends, self.mids, self.chosen, self.backs, self.moved = state
        return values

    def arrived(self, number):
        if self.packed:
            if number == 1:
                return self.ends[0]
            if number == 2:
                return jnp.where(self.edge, self.ends[1], self.mids[1])
            return jnp.where(self.edge, self.ends[2], self.mids[0])
        return self.rows()[number] if number < self.line.count else None

    def rows(self):
        if self.packed:
            near, two, far = (self.arrived(number) for number in (1, 2, 3))
            return [self.own, jnp.where(self.odd, near, far), two, jnp.where(self.odd, far, near)]
        rights, lefts = ({at: pair[way] for at, pair in self.backs.items()} for way in range(2))
        hops = range(1, self.line.count)
        return [self.own] + [self.line.gathered(hop, rights, lefts) for hop in hops]

    def total(self, part):
        if self.packed:
            return plus(part, self.ends[3], self.mids[3])
        return plus(part, *self.moved)


def plus(total, *moved):
    total = total.astype(f32)
    for values in moved:
        total = total + (values.astype(f32) if isinstance(values, jax.Array) else values)
    return total


def paired_step(values, axis, bit):
    size = lax.axis_size(axis)
    return values + lax.ppermute(values, axis, [(at, at ^ bit) for at in range(size)])


def direct_sum(values, axis, stride=1):
    size = lax.axis_size(axis)
    terms = [values] + [
        lax.ppermute(values, axis, [(at, at ^ flip) for at in range(size)])
        for flip in range(stride, size, stride)
    ]
    while len(terms) > 1:
        terms = [left + right for left, right in zip(terms[::2], terms[1::2])]
    return terms[0]


def norm_forward(values, gain):
    scale = lax.rsqrt(jnp.mean(values * values, axis=-1, keepdims=True) + norm_eps)
    return scale, (values * scale * gain).astype(bf16)


def norm_backward(values, scale, gain, grad):
    unit = values * scale
    scaled = grad * gain
    back = scale * (scaled - unit * jnp.mean(scaled * unit, axis=-1, keepdims=True))
    return back, jnp.sum(grad * unit, axis=0)


def dot(left, right):
    return jnp.dot(left, right, preferred_element_type=f32)


def dot_nt(left, right):
    return lax.dot_general(left, right, (((1,), (1,)), ((), ())), preferred_element_type=f32)


def dot_tn(left, right):
    return lax.dot_general(left, right, (((0,), (0,)), ((), ())), preferred_element_type=f32)


def body(
    tokens, lengths, cotangent, first_gain, proj_in, conv_weight, conv_bias, rate_weight, rate_bias,
    input_weight, input_bias, decay_param, proj_out, second_gain, mlp_in, mlp_down,
):
    seq_count, local_len, width = tokens.shape
    wide = lax.axis_size("wide")
    chips = wide // 2
    me = lax.axis_index("wide")
    chip, core = me // 2, me % 2
    place = jnp.stack((chip, core)).astype(jnp.int32)
    channels = proj_in.shape[2]
    block_width = rate_weight.shape[1]
    seq_half = seq_count // 2
    block_shape = (2, seq_half, local_len, 2 * channels)
    line = Chips(wide, place)
    last = chips - 1

    def swap(values):
        return swap_cores(values, wide)

    def by_sequence(values):
        parts = values.reshape(2, seq_half * local_len, width)
        mine = jnp.where(core == 0, parts[0], parts[1])
        return jnp.concatenate((mine, swap(jnp.where(core == 0, parts[1], parts[0]))), axis=0)

    def both_orders(mine, other):
        return jnp.where(core == 0, jnp.stack((mine, other)), jnp.stack((other, mine)))

    def by_position(rows):
        own, other = jnp.split(rows, 2, axis=0)
        return both_orders(own, swap(other)).reshape(tokens.shape)

    def by_channel(values):
        mine, other = values[..., :channels], values[..., channels:]
        both = both_orders(mine, swap(other))
        return both.reshape(seq_count, *both.shape[2:])

    lengths = lax.dynamic_slice_in_dim(lengths, core * seq_half, seq_half)
    chunk = 2 * chip + (jnp.arange(2, dtype=jnp.int32) ^ core)
    positions = chunk[:, None] * local_len + jnp.arange(local_len, dtype=jnp.int32)
    mask = (positions[:, None, :] < lengths[None, :, None]).astype(f32).reshape(-1, 1)

    def both_cores(own, dim):
        return jnp.concatenate((own, swap(own)), axis=dim)

    own_in = narrow_whole(jnp.swapaxes(proj_in, 1, 2), 2)
    own_out = narrow_whole(proj_out, 1)
    own_mlp_in = narrow_whole(mlp_in, 1)
    own_down = narrow_whole(mlp_down, 1)
    tokens_f = by_sequence(tokens).astype(f32)
    scale_one, norm_in = norm_forward(tokens_f, first_gain)

    params = jnp.concatenate(
        (conv_weight, conv_bias[None], rate_bias[None], input_bias[None], decay_param[None]), axis=0
    )
    norm_in, params, cotangent = fence(norm_in, params, cotangent)

    def project(rows):
        return dot_nt(rows, whole_in).reshape(2, seq_half, local_len, 4 * channels)

    rows_first = [norm_in]
    for hop in range(1, chips):
        moved = line.ring(rows_first[-1])
        if hop == 1:
            out_grad = by_sequence(cotangent).astype(f32) * mask
            out_grad_b = out_grad.astype(bf16)
            params = both_cores(params, 1)
            gates = both_cores(jnp.stack((rate_weight, input_weight)), 1)
            gate_weight, gate_back = pack_gates(
                block_diagonal(gates[0]), block_diagonal(gates[1]), block_width
            )
            rate_scale = decay_scale * jax.nn.softplus(-params[7:8])
            moved, out_grad_b, gate_weight = fence(moved, out_grad_b, gate_weight)
        if hop == last - 1:
            moved, own_in = fence(moved, own_in)
        if hop == last:
            whole_in = both_cores(own_in, 1).reshape(-1, width)
            pre_blocks = [project(rows) for rows in rows_first]
            moved, out_grad_b, own_out, pre_blocks = fence(moved, out_grad_b, own_out, pre_blocks)
        rows_first.append(moved)

    lanes = Exchange(line, out_grad_b)
    lanes.step(1, None)
    whole_out = both_cores(own_out, 0)
    pre_blocks.append(project(rows_first[last]))
    mixed, *saved, final_state, conv_state = mixer_forward(
        pre_blocks, lengths, place, params[:4], params[4:5], gate_weight, params[5:7],
        rate_scale, block_width,
    )

    def mixed_part(flag, left, right):
        rows = mixed_rows[left]
        if left != right:
            rows = jnp.where(flag, rows, mixed_rows[right])
        return dot(rows, whole_out).astype(bf16)

    mixed_rows = mixed.reshape(chips, -1, 2 * channels)
    lanes.first(mixed_part)
    mixed_rows, final_state, conv_state = lanes.fence(mixed_rows, final_state, conv_state)
    for step in range(2, chips + 1):
        lanes.step(step, mixed_part)
        if step == 2:
            own_part = dot(mixed_rows[0], whole_out)
            final_state, conv_state = by_channel(final_state), by_channel(conv_state)
            own_part, mixed_rows, final_state, conv_state = lanes.fence(
                own_part, mixed_rows, final_state, conv_state
            )
        elif step == chips - 1:
            own_part, own_mlp_in = lanes.fence(own_part, own_mlp_in)
            other_mlp_in = swap(own_mlp_in)
        elif step < chips:
            (own_part,) = lanes.fence(own_part)
    rows_back = lanes.rows()
    own_part, rows_back, own_down = lanes.fence(own_part, rows_back, own_down)
    resid = tokens_f + lanes.total(own_part)

    scale_two, norm_mid = norm_forward(resid, second_gain)
    norm_mid, own_down = fence(norm_mid, own_down)
    other_down = swap(own_down)
    rows_second = [norm_mid]
    hidden, gate_grads, up_grads, parts, outs = [], [], [], [], []
    sums = None
    for hop in range(chips):
        if hop < last:
            rows_second.append(line.ring(rows_second[hop]))
        if hop > 1:
            sums = line.ring(total_b)
        made = mlp_block(
            rows_second[hop], rows_back[hop], own_mlp_in, other_mlp_in, own_down, other_down
        )
        rows_second, made, sums = fence(rows_second, made, sums)
        for kept, value in zip((hidden, gate_grads, up_grads, parts, outs), made):
            kept.append(value)
        if hop:
            total = parts[hop] if sums is None else plus(parts[hop], sums)
            total_b = total.astype(bf16)
    sums = line.ring(total_b)
    [grads_gate], _ = weight_grad(gate_grads, rows_second, 1)
    [grads_down], _ = weight_grad(hidden, rows_back, 1)
    sums, grads_gate, grads_down, up_grads = fence(sums, grads_gate, grads_down, up_grads)
    mid_sum = plus(parts[0], sums)

    from_norm, gain_two = norm_backward(resid, scale_two, second_gain, mid_sum)
    resid_grad = out_grad + from_norm
    resid_grad_b = resid_grad.astype(bf16)
    resid_grad_b, up_grads, outs = fence(resid_grad_b, up_grads, outs)

    def back_block(rows):
        return dot_nt(rows, whole_out).reshape(2, seq_half, local_len, 2 * channels)

    def out_part(flag, left, right):
        return outs[left] if left == right else jnp.where(flag, outs[left], outs[right])

    lanes = Exchange(line, resid_grad_b)
    lanes.step(1, None)
    lanes.first(out_part)
    [grads_up], _ = weight_grad(up_grads, rows_second, 1)
    from_down, from_gate = swap(grads_down[1]), swap(grads_gate[1])
    grads_up, from_down, from_gate, outs = lanes.fence(grads_up, from_down, from_gate, outs)
    back_blocks = [back_block(resid_grad_b)]
    for step in range(2, chips + 1):
        lanes.step(step, out_part)
        if step == 2:
            part_down = join((grads_down[0], from_down))
            part_mlp_in = join((grads_gate[0], from_gate), slots=2)
            from_up = swap(grads_up[1])
            part_down, part_mlp_in, from_up, outs = lanes.fence(part_down, part_mlp_in, from_up, outs)
            grad_mlp_down = narrow_sum(part_down, 1)
        elif step == 3:
            part_mlp_in = join((grads_up[0], from_up), slots=2, slot=1, filled=(part_mlp_in,))
            if lanes.packed:
                back_blocks += [back_block(lanes.arrived(at)) for at in (1, 2)]
            part_mlp_in, back_blocks = lanes.fence(part_mlp_in, back_blocks)
            grad_mlp_in = narrow_sum(part_mlp_in, 1)
        elif step < chips:
            lanes.fence()
    if lanes.packed:
        back_blocks.append(back_block(lanes.arrived(3)))
    else:
        back_blocks += [back_block(rows) for rows in lanes.rows()[1:]]
    grads, small, gate_grads = mixer_backward(
        back_blocks, lanes.packed, saved, lengths, place, params[:4], gate_back, block_width
    )
    grad_rows = grads.reshape(-1, 4 * channels)
    part = row_dot(grad_rows, whole_in, 1, chips, bf16)
    part, grad_rows, small, gate_grads, mixed, grad_mlp_down = lanes.fence(
        part, grad_rows, small, gate_grads, mixed, grad_mlp_down
    )

    size = lax.axis_size("narrow")
    split = size // 2 + 1
    count = rate_weight.shape[0]

    def gate_rows(gates, sums):
        return jnp.concatenate((gates.reshape(-1, block_width), sums.reshape(-1, block_width)), axis=0)

    gate_mine = gate_rows(gate_grads[:count], small[:, :channels])
    gate_other = gate_rows(gate_grads[count:], small[:, channels:])
    moving = line.ring(part)
    grads_in, [gain_one] = weight_grad([grad_rows], rows_first, 2, weight=whole_in)
    [grads_out], _ = weight_grad([mixed.reshape(-1, 2 * channels)], lanes.rows(), 1)
    gate_sum = (gate_mine + swap(gate_other.astype(bf16)).astype(f32)).astype(bf16)
    gate_sum = paired_step(gate_sum, "narrow", 1)
    grads_in, grads_out, gain_one, moving, gate_sum, resid, grad_rows = fence(
        grads_in, grads_out, gain_one, moving, gate_sum, resid, grad_rows
    )
    for hop in range(2, chips):
        sent = row_dot(grad_rows, whole_in, hop, chips, bf16, (moving,))
        if hop == 2:
            sent, grads_in, grads_out, gain_one = fence(sent, grads_in, grads_out, gain_one)
        moving = line.ring(sent)
    part = row_dot(grad_rows, whole_in, 0, chips)
    parts = join(*[(own, swap(other)) for own, other in (*grads_in, grads_out)])
    gains = jnp.concatenate((gain_one / first_gain, gain_two[None]), axis=0)
    parts, gate_sum, gains = fence(parts, gate_sum, gains)
    gains, parts = fence(direct_sum(gains, "narrow"), parts)
    sum_proj = DirectSum(parts)
    sum_proj.send(range(1, split))
    part, parts, grad_mlp_in, gate_sum, resid, gains, sum_proj.got = fence(
        part, parts, grad_mlp_in, gate_sum, resid, gains, sum_proj.got
    )
    sum_proj.grad = parts
    sum_proj.send(range(split, size))
    output = by_position((resid + lanes.total(outs[0])).astype(bf16))
    gains = gains + swap(gains)
    moving, output, gains, sum_proj.got, gate_sum = fence(
        moving, output, gains, sum_proj.got, gate_sum
    )
    bit = 2
    while bit < size:
        gate_sum = paired_step(gate_sum, "narrow", bit)
        bit *= 2
    in_sum = plus(part, moving)
    from_norm, _ = norm_backward(tokens_f, scale_one, first_gain, in_sum)
    grad_tokens = (resid_grad + from_norm).astype(bf16)
    grad_tokens, gains, sum_proj.got = fence(grad_tokens, gains, sum_proj.got)
    gains = direct_sum(gains, "wide", 2)
    grad_proj = sum_proj.total()
    gate_sum = gate_sum.astype(f32)
    gate_grads = gate_sum[: count * 2 * block_width].reshape(count, 2, block_width, block_width)
    small = gate_sum[count * 2 * block_width :].reshape(8, channels)
    grad_mlp_in, grad_mlp_down = grad_mlp_in.astype(f32), grad_mlp_down.astype(f32)
    grad_proj_in = grad_proj[: 2 * channels].reshape(2, channels, -1)
    grad_proj_out = grad_proj[2 * channels :]
    grad_mlp_in = grad_mlp_in.reshape(2, mlp_in.shape[2], -1)
    return (
        output,
        by_position(grad_tokens),
        final_state,
        conv_state,
        gains[0],
        jnp.swapaxes(grad_proj_in, 1, 2),
        small[4:8],
        small[3],
        gate_grads[:, 0],
        small[0],
        gate_grads[:, 1],
        small[1],
        small[2] * decay_scale * jax.nn.sigmoid(-decay_param),
        grad_proj_out,
        gains[1],
        jnp.swapaxes(grad_mlp_in, 1, 2),
        grad_mlp_down,
    )


def solution(mesh):
    return jax.shard_map(
        body,
        mesh=mesh,
        in_specs=(
            P("narrow", "wide", None),
            P("narrow"),
            P("narrow", "wide", None),
            P(),
            P(None, "narrow", "wide"),
            P(None, "wide"),
            P("wide"),
            P("wide", None, None),
            P("wide"),
            P("wide", None, None),
            P("wide"),
            P("wide"),
            P("wide", "narrow"),
            P(),
            P(None, "narrow", "wide"),
            P("wide", "narrow"),
        ),
        out_specs=(
            P("narrow", "wide", None),
            P("narrow", "wide", None),
            P("narrow", "wide"),
            P("narrow", None, "wide"),
            P(),
            P(None, "narrow", "wide"),
            P(None, "wide"),
            P("wide"),
            P("wide", None, None),
            P("wide"),
            P("wide", None, None),
            P("wide"),
            P("wide"),
            P("wide", "narrow"),
            P(),
            P(None, "narrow", "wide"),
            P("wide", "narrow"),
        ),
        check_vma=False,
    )
```

```python
from functools import partial

import jax
import jax.numpy as jnp
from jax import lax
from jax.experimental import pallas as pl
from jax.experimental.pallas import tpu as pltpu
from jax.sharding import PartitionSpec as P

decay_scale = 8.0
norm_eps = 1e-06
gelu_in = 0.7978845608028654
gelu_cube = 0.044715
f32 = jnp.float32
bf16 = jnp.bfloat16
kernel_cost = pl.CostEstimate(flops=1, bytes_accessed=1, transcendentals=0)
chain_cost = pl.CostEstimate(flops=1 << 35, bytes_accessed=1 << 27, transcendentals=0)


def gelu_tanh(v):
    return jnp.tanh(gelu_in * (v + gelu_cube * v * v * v))


def gelu_pair(v):
    t = gelu_tanh(v)
    half = 0.5 * (1.0 + t)
    slope = half + 0.5 * v * (1.0 - t * t) * (gelu_in + (3.0 * gelu_in * gelu_cube) * v * v)
    return v * half, slope


def one_minus_exp(v, decay):
    series = 1.0 - v * (1.0 / 7.0)
    for order in (6.0, 5.0, 4.0, 3.0, 2.0):
        series = 1.0 - v * (1.0 / order) * series
    return jnp.where(v < 0.3, v * series, 1.0 - decay * decay)


def gate_tiles(channels, block_width, tile):
    tiles, offset = [], 0
    for start in range(0, channels, tile):
        stop = min(start + tile, channels)
        low = start // block_width * block_width // 128 * 128
        high = min(-(-((stop - 1) // block_width + 1) * block_width // 128) * 128, channels)
        tiles.append((start, stop, low, high, offset))
        offset += high - low
    return tiles


def split_rows(values):
    high = values.astype(bf16)
    return jnp.concatenate((high, (values - high.astype(f32)).astype(bf16)), axis=0)


def joined_dot(halves, weight):
    both = jnp.dot(halves, weight, preferred_element_type=f32)
    rows = both.shape[0] // 2
    return both[:rows] + both[rows:]


def tile_scan(decay, drive, backward):
    rows, channels = decay.shape
    a = decay.reshape(rows // 8, 8, channels)
    b = drive.reshape(rows // 8, 8, channels)
    row = lax.broadcasted_iota(jnp.int32, (1, 8, channels), 1)
    for step in (1, 2, 4):
        if backward:
            keep, shift = row < 8 - step, 8 - step
        else:
            keep, shift = row >= step, step
        a_moved = jnp.where(keep, pltpu.roll(a, shift, 1), 1.0)
        b_moved = jnp.where(keep, pltpu.roll(b, shift, 1), 0.0)
        b = b + a * b_moved
        a = a * a_moved
    return a, b


def mixer_forward_kernel(
    chips, block_width, place, lengths, *refs
):
    pre_refs, refs = refs[:chips], refs[chips:]
    conv_weight, conv_bias, gate_weight, gate_bias, rate_scale = refs[:5]
    mixed, *saved = refs[5:15]
    final_state, conv_state, pre_now, x_tail, carry = refs[15:]
    chunk = pl.program_id(0)
    seq_count, local_len, channels = pre_now.shape
    channels //= 2
    pick_block(chunk, place, chips, pre_refs, pre_now)

    @pl.when(chunk == 0)
    def _():
        x_tail[...] = jnp.zeros_like(x_tail)
        carry[...] = jnp.zeros_like(carry)

    convs = []
    for seq in range(seq_count):
        x = pre_now[seq, :, channels:]
        extended = jnp.concatenate((x_tail[seq], x), axis=0)
        conv = conv_bias[...] + conv_weight[0:1] * x
        for lag in range(1, 4):
            conv = conv + conv_weight[lag : lag + 1] * extended[8 - lag : 8 - lag + local_len]
        x_tail[seq] = x[local_len - 8 :]
        convs.append(conv)
        for tap in range(3):
            position = lengths[seq] - 3 + tap

            @pl.when(position // local_len == chunk)
            def _(seq=seq, tap=tap, position=position):
                conv_state[seq, tap : tap + 1] = pre_now[
                    seq, pl.ds(lax.rem(position, local_len), 1), channels:
                ]

    conv_all = jnp.concatenate(convs, axis=0)
    parted = split_rows(conv_all)
    rate_parts, in_parts = [], []
    for start, stop, low, high, at in gate_tiles(channels, block_width, 128):
        both = joined_dot(parted[:, low:high], gate_weight[at : at + high - low])
        rate_parts.append(both[:, : stop - start])
        in_parts.append(both[:, 128 : 128 + stop - start])
    rate_all = jax.nn.sigmoid(jnp.concatenate(rate_parts, axis=1) + gate_bias[0:1])
    in_all = jax.nn.sigmoid(jnp.concatenate(in_parts, axis=1) + gate_bias[1:2])
    for seq in range(seq_count):
        rows = slice(seq * local_len, (seq + 1) * local_len)
        conv = convs[seq]
        rate_gate = rate_all[rows]
        in_gate = in_all[rows]
        step_log = rate_scale[...] * rate_gate
        decay = jnp.exp(-step_log)
        square = jnp.maximum(one_minus_exp(2.0 * step_log, decay), 1e-36)
        inverse_root = lax.rsqrt(square)
        root = square * inverse_root
        position = chunk * local_len + lax.broadcasted_iota(jnp.int32, (local_len, 1), 0)
        live = position < lengths[seq]
        gated_conv = in_gate * conv
        driven = root * gated_conv
        kept_decay = jnp.where(live, decay, 1.0)
        a, b = tile_scan(kept_decay, jnp.where(live, driven, 0.0), False)
        last = carry[seq]
        tiles = []
        for tile in range(local_len // 8):
            tiles.append(b[tile] + a[tile] * last)
            last = tiles[-1][7:8]
        states = jnp.concatenate(tiles, axis=0)
        carry[seq] = last
        final_state[seq : seq + 1] = last
        gated, slope = gelu_pair(pre_now[seq, :, :channels])
        mixed[0, 0, seq] = (gated * states).astype(bf16)
        rate_factor = (states - driven - gated_conv * decay * decay * inverse_root) * rate_gate
        for out, value in zip(
            saved,
            (
                gated,
                slope * states,
                kept_decay,
                rate_factor,
                -rate_scale[...] * rate_factor * (1.0 - rate_gate),
                driven * (1.0 - in_gate),
                root * in_gate,
                pre_now[seq, :, channels:],
                conv.astype(bf16),
            ),
        ):
            out[0, 0, seq] = value


def mixer_backward_kernel(
    chips, block_width, crossed, place, lengths, *refs
):
    back_refs, refs = refs[:chips], refs[chips:]
    gated_in, y_in, decay_in, rate_in, rate_pre_in, in_pre_in, direct_in, x_in, conv_in = refs[:9]
    conv_weight, gate_back, grads, sums, gate_grads = refs[9:14]
    back_now, carry, grad_head, gate_sums = refs[14:]
    step = pl.program_id(0)
    chunk = pl.num_programs(0) - 1 - step
    seq_count, local_len, channels = back_now.shape
    pick_block(chunk, place, chips, back_refs, back_now, crossed)

    @pl.when(step == 0)
    def _():
        carry[...] = jnp.zeros_like(carry)
        grad_head[...] = jnp.zeros_like(grad_head)
        sums[...] = jnp.zeros_like(sums)
        gate_sums[...] = jnp.zeros_like(gate_sums)

    rate_pre, in_pre, direct = [], [], []
    decay_sum = jnp.zeros((1, channels), f32)
    for seq in range(seq_count):
        position = chunk * local_len + lax.broadcasted_iota(jnp.int32, (local_len, 1), 0)
        live = position < lengths[seq]
        mixer_grad = back_now[seq]
        grads[0, 0, seq, :, :channels] = (mixer_grad * y_in[0, 0, seq]).astype(bf16)
        source = mixer_grad * gated_in[0, 0, seq]
        decay = decay_in[0, 0, seq]
        a, b = tile_scan(decay, decay * source, True)
        following = carry[seq]
        tiles = []
        for tile in reversed(range(local_len // 8)):
            passed = b[tile] + a[tile] * following
            tiles.append(jnp.concatenate((passed[1:], following), axis=0))
            following = passed[0:1]
        carry[seq] = following
        adjoint = source + jnp.concatenate(tiles[::-1], axis=0)
        adjoint = jnp.where(live, adjoint, 0.0)
        decay_sum = decay_sum + jnp.sum(adjoint * rate_in[0, 0, seq], axis=0, keepdims=True)
        rate_pre.append(adjoint * rate_pre_in[0, 0, seq])
        in_pre.append(adjoint * in_pre_in[0, 0, seq])
        direct.append(adjoint * direct_in[0, 0, seq])
    rate_all = jnp.concatenate(rate_pre, axis=0)
    in_all = jnp.concatenate(in_pre, axis=0)
    conv_all = jnp.concatenate([conv_in[0, 0, seq] for seq in range(seq_count)], axis=0)
    rate_b, in_b = rate_all.astype(bf16), in_all.astype(bf16)
    for start, stop, low, high, at in gate_tiles(channels, block_width, 128):
        both = jnp.concatenate((rate_b[:, start:stop], in_b[:, start:stop]), axis=1)
        part = lax.dot_general(
            conv_all[:, low:high], both, (((0,), (0,)), ((), ())), preferred_element_type=f32
        )
        if stop - start == 128:
            gate_sums[at : at + high - low] += part
        else:
            gate_sums[at : at + high - low, : stop - start] += part[:, : stop - start]
            gate_sums[at : at + high - low, 128 : 128 + stop - start] += part[:, stop - start :]
    parts = []
    for start, stop, low, high, at in gate_tiles(channels, block_width, 256):
        both = jnp.concatenate((rate_b[:, low:high], in_b[:, low:high]), axis=1)
        parts.append(dot(both, gate_back[2 * at : 2 * (at + high - low)])[:, : stop - start])
    conv_grad = jnp.concatenate(direct, axis=0) + jnp.concatenate(parts, axis=1)
    tap_sums = [jnp.zeros((1, channels), f32) for _ in range(4)]
    for seq in range(seq_count):
        part = conv_grad[seq * local_len : (seq + 1) * local_len]
        extended = jnp.concatenate((part, grad_head[seq]), axis=0)
        x = x_in[0, 0, seq]
        total = conv_weight[0:1] * part
        tap_sums[0] = tap_sums[0] + jnp.sum(part * x, axis=0, keepdims=True)
        for lag in range(1, 4):
            moved = extended[lag : lag + local_len]
            total = total + conv_weight[lag : lag + 1] * moved
            tap_sums[lag] = tap_sums[lag] + jnp.sum(moved * x, axis=0, keepdims=True)
        grads[0, 0, seq, :, channels:] = total.astype(bf16)
        grad_head[seq] = part[:8]
    sums[0:1] += jnp.sum(rate_all, axis=0, keepdims=True)
    sums[1:2] += jnp.sum(in_all, axis=0, keepdims=True)
    sums[2:3] += decay_sum
    sums[3:4] += jnp.sum(conv_grad, axis=0, keepdims=True)
    for lag in range(4):
        sums[4 + lag : 5 + lag] += tap_sums[lag]

    @pl.when(chunk == 0)
    def _():
        tiles = gate_tiles(channels, block_width, 128)
        for kind, column in enumerate((0, 128)):
            for base in range(0, channels, block_width):
                pieces = []
                for start, stop, low, _, at in tiles:
                    left, right = max(start, base), min(stop, base + block_width)
                    if left < right:
                        row = at + base - low
                        span = gate_sums[row : row + block_width, column : column + 128]
                        pieces.append(span[:, left - start : right - start])
                gate_grads[base // block_width, kind] = jnp.concatenate(pieces, axis=1)


def chunk_place(chunk, place, chips):
    return lax.rem(place[0] - chunk // 2 + chips, chips), lax.rem(chunk + place[1], 2)


def pick_block(chunk, place, chips, refs, now, crossed=False):
    slot = (chunk // 2) ^ place[0] if crossed else chunk_place(chunk, place, chips)[0]
    for hop in range(chips):

        @pl.when(slot == hop)
        def _(hop=hop):
            now[...] = refs[hop][0]


def mixer_specs(shape, chips, chunk_of):
    def hop_map(hop, crossed, step, place, lengths):
        first = 2 * (place[0] ^ hop if crossed else lax.rem(place[0] - hop + chips, chips))
        return (jnp.where(chunk_of(step) <= first, place[1], 1 - place[1]), 0, 0, 0)

    def block_map(step, place, lengths):
        chip, core = chunk_place(chunk_of(step), place, chips)
        return (chip, core, 0, 0, 0)

    def hops(lanes, crossed=False):
        block = (1, *shape[1:3], lanes)
        return [pl.BlockSpec(block, partial(hop_map, hop, crossed)) for hop in range(chips)]

    def block(lanes):
        return pl.BlockSpec((1, 1, *shape[1:3], lanes), block_map)

    return hops, block


def whole_spec(shape):
    return pl.BlockSpec(shape, lambda step, place, lengths: (0,) * len(shape))


def mixer_forward(
    pre_blocks, lengths, place, conv_weight, conv_bias, gate_weight, gate_bias, rate_scale, block_width
):
    chips = len(pre_blocks)
    _, seq_count, local_len, channels = pre_blocks[0].shape
    channels //= 2
    hops, block = mixer_specs(pre_blocks[0].shape, chips, lambda step: step)
    full = (chips, 2, seq_count, local_len, channels)
    params = (conv_weight, conv_bias, gate_weight, gate_bias, rate_scale)
    return pl.pallas_call(
        partial(mixer_forward_kernel, chips, block_width),
        grid_spec=pltpu.PrefetchScalarGridSpec(
            num_scalar_prefetch=2,
            grid=(2 * chips,),
            in_specs=hops(2 * channels) + [whole_spec(param.shape) for param in params],
            out_specs=[block(channels)] * 10
            + [whole_spec((seq_count, channels)), whole_spec((seq_count, 3, channels))],
            scratch_shapes=[
                pltpu.VMEM((seq_count, local_len, 2 * channels), f32),
                pltpu.VMEM((seq_count, 8, channels), f32),
                pltpu.VMEM((seq_count, 1, channels), f32),
            ],
        ),
        out_shape=[pltpu.HBM(full, bf16)]
        + [pltpu.HBM(full, f32)] * 8
        + [pltpu.HBM(full, bf16)]
        + [
            jax.ShapeDtypeStruct((seq_count, channels), f32),
            jax.ShapeDtypeStruct((seq_count, 3, channels), f32),
        ],
        compiler_params=pltpu.CompilerParams(vmem_limit_bytes=32 << 20),
        cost_estimate=kernel_cost,
        name="mixer_forward",
    )(place, lengths, *pre_blocks, *params)


def mixer_backward(
    back_blocks, crossed, saved, lengths, place, conv_weight, gate_back, block_width
):
    chips = len(back_blocks)
    _, seq_count, local_len, channels = back_blocks[0].shape
    hops, block = mixer_specs(back_blocks[0].shape, chips, lambda step: 2 * chips - 1 - step)
    full = (chips, 2, seq_count, local_len, channels)
    params = (conv_weight, gate_back)
    packed = gate_tiles(channels, block_width, 128)[-1]
    packed = packed[4] + packed[3] - packed[2]
    gate_shape = (channels // block_width, 2, block_width, block_width)
    return pl.pallas_call(
        partial(mixer_backward_kernel, chips, block_width, crossed),
        grid_spec=pltpu.PrefetchScalarGridSpec(
            num_scalar_prefetch=2,
            grid=(2 * chips,),
            in_specs=hops(channels, crossed)
            + [block(channels)] * 9
            + [whole_spec(param.shape) for param in params],
            out_specs=[block(2 * channels), whole_spec((8, channels)), whole_spec(gate_shape)],
            scratch_shapes=[
                pltpu.VMEM((seq_count, local_len, channels), f32),
                pltpu.VMEM((seq_count, 1, channels), f32),
                pltpu.VMEM((seq_count, 8, channels), f32),
                pltpu.VMEM((packed, 256), f32),
            ],
        ),
        out_shape=[
            pltpu.HBM((*full[:-1], 2 * channels), bf16),
            jax.ShapeDtypeStruct((8, channels), f32),
            jax.ShapeDtypeStruct(gate_shape, f32),
        ],
        compiler_params=pltpu.CompilerParams(vmem_limit_bytes=32 << 20),
        cost_estimate=kernel_cost,
        name="mixer_backward",
    )(place, lengths, *back_blocks, *saved, *params)


def mlp_kernel(tiles, rows, back, own_in, other_in, own_down, other_down, *refs):
    hidden, gate_grads, up_grads, middle, out, middle_sum, out_sum = refs
    step = pl.program_id(0)

    @pl.when(step == 0)
    def _():
        middle_sum[...] = jnp.zeros_like(middle_sum)
        out_sum[...] = jnp.zeros_like(out_sum)

    def units(weight_in, weight_down):
        gated, slope = gelu_pair(dot(rows[...], weight_in[0]))
        up_pre = dot(rows[...], weight_in[1])
        hidden_grad = dot_nt(back[...], weight_down[...])
        hidden_b = (gated * up_pre).astype(bf16)
        gate_b = (hidden_grad * up_pre * slope).astype(bf16)
        up_b = (hidden_grad * gated).astype(bf16)
        hidden[...] = hidden_b
        gate_grads[...] = gate_b
        up_grads[...] = up_b
        out_sum[...] += dot(hidden_b, weight_down[...])
        middle_sum[...] += dot_nt(gate_b, weight_in[0]) + dot_nt(up_b, weight_in[1])

    @pl.when(step < tiles)
    def _():
        units(own_in, own_down)

    @pl.when(step >= tiles)
    def _():
        units(other_in, other_down)

    @pl.when(step == 2 * tiles - 1)
    def _():
        middle[...] = middle_sum[...]
        out[...] = out_sum[...].astype(bf16)


def mlp_block(rows, back, own_in, other_in, own_down, other_down):
    count, width = rows.shape
    units = own_down.shape[0]
    tile = 256 if units % 256 == 0 else 128
    tiles = units // tile

    def own_tile(step):
        return jnp.minimum(step, tiles - 1)

    def other_tile(step):
        return jnp.maximum(step - tiles, 0)

    whole = pl.BlockSpec((count, width), lambda step: (0, 0))
    tiled = pl.BlockSpec((count, tile), lambda step: (0, step))
    return pl.pallas_call(
        partial(mlp_kernel, tiles),
        grid=(2 * tiles,),
        in_specs=[
            whole,
            whole,
            pl.BlockSpec((2, width, tile), lambda step: (0, 0, own_tile(step))),
            pl.BlockSpec((2, width, tile), lambda step: (0, 0, other_tile(step))),
            pl.BlockSpec((tile, width), lambda step: (own_tile(step), 0)),
            pl.BlockSpec((tile, width), lambda step: (other_tile(step), 0)),
        ],
        out_specs=[tiled] * 3 + [whole] * 2,
        out_shape=[pltpu.HBM((count, 2 * units), bf16)] * 3
        + [pltpu.HBM((count, width), f32), pltpu.HBM((count, width), bf16)],
        scratch_shapes=[pltpu.VMEM((count, width), f32)] * 2,
        compiler_params=pltpu.CompilerParams(vmem_limit_bytes=36 << 20),
        cost_estimate=kernel_cost,
        name="mlp_block",
    )(rows, back, own_in, other_in, own_down, other_down)


def weight_grad_kernel(count, kinds, weighted, *refs):
    lefts, rights = refs[:count], refs[count : 2 * count]
    outs = refs[2 * count + weighted :]
    total = dot_tn(lefts[0][...], rights[0][...])
    for left, right in zip(lefts[1:], rights[1:]):
        total = total + dot_tn(left[...], right[...])
    half = outs[0].shape[0]
    for kind in range(kinds):
        start = 2 * kind * half
        outs[kind][...] = total[start : start + half]
        outs[kinds + kind][...] = total[start + half : start + 2 * half].astype(bf16)
    if weighted:
        weight = refs[2 * count][...]
        outs[2 * kinds][...] = jnp.sum(total * weight.astype(f32), axis=0, keepdims=True)


def weight_grad(lefts, rights, kinds, weight=None):
    count = len(rights)
    rows, width = rights[0].shape
    columns = lefts[0].shape[1]
    half, tile = columns // kinds // 2, min(512, width)
    joined = len(lefts) == 1

    def left_spec(at):
        block = at if joined else 0
        return pl.BlockSpec((rows, columns), lambda step: (block, 0))

    lefts = list(lefts) * (count if joined else 1)
    weights = [] if weight is None else [weight]
    made = pl.pallas_call(
        partial(weight_grad_kernel, count, kinds, len(weights)),
        grid=(width // tile,),
        in_specs=[left_spec(at) for at in range(count)]
        + [pl.BlockSpec((rows, tile), lambda step: (0, step))] * count
        + [pl.BlockSpec((columns, tile), lambda step: (0, step))] * len(weights),
        out_specs=[pl.BlockSpec((half, tile), lambda step: (0, step))] * (2 * kinds)
        + [pl.BlockSpec((1, tile), lambda step: (0, step))] * len(weights),
        out_shape=[pltpu.HBM((half, width), f32)] * kinds
        + [pltpu.HBM((half, width), bf16)] * kinds
        + [jax.ShapeDtypeStruct((1, width), f32)] * len(weights),
        compiler_params=pltpu.CompilerParams(vmem_limit_bytes=28 << 20),
        cost_estimate=kernel_cost,
        name="weight_grad",
    )(*lefts, *rights, *weights)
    return list(zip(made[:kinds], made[kinds : 2 * kinds])), made[2 * kinds :]


def row_dot_kernel(rows, weight, *refs):
    total = dot(rows[...], weight[...])
    if len(refs) > 1:
        total = total + refs[0][...].astype(f32)
    refs[-1][...] = total.astype(refs[-1].dtype)


def row_dot(rows, weight, block, count, kind=f32, moving=()):
    depth, width = weight.shape
    size, tile = rows.shape[0] // count, min(512, width)
    return pl.pallas_call(
        row_dot_kernel,
        grid=(width // tile,),
        in_specs=[
            pl.BlockSpec((size, depth), lambda step: (block, 0)),
            pl.BlockSpec((depth, tile), lambda step: (0, step)),
        ]
        + [pl.BlockSpec((size, tile), lambda step: (0, step))] * len(moving),
        out_specs=pl.BlockSpec((size, tile), lambda step: (0, step)),
        out_shape=pltpu.HBM((size, width), kind),
        compiler_params=pltpu.CompilerParams(vmem_limit_bytes=10 << 20),
        cost_estimate=chain_cost if moving else kernel_cost,
        name="row_dot",
    )(rows, weight, *moving)


def join_kernel(count, tiles, *refs):
    out = refs[-1]
    for at in range(count):

        @pl.when(pl.program_id(0) // tiles == at)
        def _(at=at):
            out[...] = (refs[2 * at][...] + refs[2 * at + 1][...].astype(f32)).astype(bf16)


def join(*pairs, slots=1, slot=0, filled=(), tile=128):
    count = len(pairs)
    rows, width = pairs[0][0].shape
    tile = tile if rows % tile == 0 else rows // 2
    tiles = rows // tile

    def spec(at):
        return pl.BlockSpec((tile, width), lambda step: (jnp.clip(step - at * tiles, 0, tiles - 1), 0))

    return pl.pallas_call(
        partial(join_kernel, count, tiles),
        grid=(count * tiles,),
        in_specs=[spec(at) for at in range(count) for _ in range(2)]
        + [pl.BlockSpec(memory_space=pl.ANY)] * len(filled),
        out_specs=pl.BlockSpec((tile, width), lambda step: (slot * count * tiles + step, 0)),
        out_shape=pltpu.HBM((slots * count * rows, width), bf16),
        input_output_aliases={2 * count: 0} if filled else {},
        compiler_params=pltpu.CompilerParams(vmem_limit_bytes=16 << 20),
        cost_estimate=kernel_cost,
        name="join",
    )(*[value for pair in pairs for value in pair], *filled)


def block_diagonal(weight):
    count, width, _ = weight.shape
    rows = [
        jnp.pad(weight[at], ((0, 0), (at * width, (count - 1 - at) * width))) for at in range(count)
    ]
    return jnp.concatenate(rows, axis=0)


def pack_gates(rate, into, block_width):
    def padded(values, width):
        return jnp.pad(values, ((0, 0), (0, width - values.shape[1])))

    channels = rate.shape[0]
    forward, back = [], []
    for start, stop, low, high, _ in gate_tiles(channels, block_width, 128):
        forward.append(
            jnp.concatenate(
                (padded(rate[low:high, start:stop], 128), padded(into[low:high, start:stop], 128)), axis=1
            )
        )
    for start, stop, low, high, _ in gate_tiles(channels, block_width, 256):
        back.append(padded(rate.T[low:high, start:stop], 256))
        back.append(padded(into.T[low:high, start:stop], 256))
    return jnp.concatenate(forward, axis=0), jnp.concatenate(back, axis=0)


def narrow_whole(weight, dim):
    return lax.all_gather(weight, "narrow", axis=dim, tiled=True)


def narrow_sum(grad, dim):
    return lax.psum_scatter(grad, "narrow", scatter_dimension=dim, tiled=True)


class DirectSum:
    def __init__(self, grad):
        self.size = lax.axis_size("narrow")
        self.grad, self.got = grad, []

    def piece(self, flip):
        span = self.grad.shape[1] // self.size
        start = (lax.axis_index("narrow") ^ flip) * span
        return lax.dynamic_slice_in_dim(self.grad, start, span, axis=1)

    def send(self, flips):
        for flip in flips:
            pairs = [(at, at ^ flip) for at in range(self.size)]
            self.got.append(lax.ppermute(self.piece(flip), "narrow", pairs))

    def total(self):
        return plus(self.piece(0), *self.got)


def swap_cores(values, wide):
    return lax.ppermute(values, "wide", [(at, at ^ 1) for at in range(wide)])


def fence(*values):
    return lax.optimization_barrier(values)


class Chips:
    def __init__(self, wide, place):
        self.place, self.chip, self.count = place, place[0], wide // 2
        self.wide = wide

    def move(self, values, pairs):
        devices = [(2 * a + core, 2 * b + core) for a, b in pairs for core in range(2)]
        return lax.ppermute(values, "wide", devices)

    def ring(self, values):
        return self.move(values, [(at, (at + 1) % self.count) for at in range(self.count)])

    def gather_step(self, step, right, left):
        count = self.count
        to_right = [(at, at + 1) for at in range(step - 1, count - 1)]
        to_left = [(at, at - 1) for at in range(1, count - step + 1)]
        if 2 * step > count + 1:
            both = self.move(jnp.where(self.chip >= step - 1, right, left), to_right + to_left)
            return both, both
        return self.move(right, to_right), self.move(left, to_left)

    def gathered(self, hop, rights, lefts):
        return jnp.where(self.chip >= hop, rights[hop], lefts[self.count - hop])

    def sum_step(self, step, right, left):
        count = self.count
        to_right = [(at, at + 1) for at in range(step)]
        to_left = [(at, at - 1) for at in range(count - step, count)]
        if 2 * step < count - 1:
            both = self.move(jnp.where(self.chip < step, right, left), to_right + to_left)
            return both, both
        return self.move(right, to_right), self.move(left, to_left)


def advance_kernel(place, end_part, end_moved, mid_part, mid_moved, end, mid, *, inner):
    added = end_part[...].astype(f32) + end_moved[...].astype(f32)
    mid[...] = (mid_part[...].astype(f32) + mid_moved[...].astype(f32)).astype(bf16)
    if inner:
        edge = (place[0] == 0) | (place[0] == 3)

        @pl.when(edge)
        def _():
            end[...] = end_part[...].astype(bf16)

        @pl.when(jnp.logical_not(edge))
        def _():
            end[...] = end_moved[...]
    else:
        end[...] = added.astype(bf16)


def advance(place, end_part, end_moved, mid_part, mid_moved, inner):
    rows, width = end_moved.shape
    tile = min(64, rows)
    spec = pl.BlockSpec((tile, width), lambda step, place: (step, 0))
    return pl.pallas_call(
        partial(advance_kernel, inner=inner),
        grid_spec=pltpu.PrefetchScalarGridSpec(
            num_scalar_prefetch=1, grid=(rows // tile,), in_specs=[spec] * 4, out_specs=[spec] * 2
        ),
        out_shape=[pltpu.HBM((rows, width), bf16)] * 2,
        compiler_params=pltpu.CompilerParams(vmem_limit_bytes=8 << 20),
        cost_estimate=kernel_cost,
        name="advance",
    )(place, end_part, end_moved, mid_part, mid_moved)


class Exchange:
    def __init__(self, line, rows):
        self.line, self.own = line, rows
        self.packed = line.count == 4
        if self.packed:
            self.odd = line.chip % 2 == 1
            self.edge = (line.chip == 0) | (line.chip == 3)
        self.ends, self.mids, self.chosen = [], [], ()
        self.backs, self.moved = {0: (rows, rows)}, (0.0, 0.0)

    def pair(self, end, mid):
        self.ends.append(self.line.move(end, [(0, 1), (1, 0), (2, 3), (3, 2)]))
        self.mids.append(self.line.move(mid, [(1, 2), (2, 1)]))

    def first(self, choose):
        if self.packed:
            self.chosen = (choose(self.line.chip == 0, 1, 3),)

    def step(self, number, choose):
        line, count = self.line, self.line.count
        if not self.packed:
            if number < count:
                self.backs[number] = line.gather_step(number, *self.backs[number - 1])
            if number > 1:
                sent = [
                    plus(choose(True, hop, hop), self.moved[way]).astype(bf16)
                    for way, hop in enumerate((number - 1, count - number + 1))
                ]
                self.moved = line.sum_step(number - 1, *sent)
        elif number == 1:
            self.pair(self.own, self.own)
        elif number == 2:
            self.pair(jnp.where(self.edge, self.chosen[0], self.mids[0]), self.ends[0])
            self.chosen = (choose(self.odd, 1, 3), choose(line.chip == 1, 3, 1), choose(True, 2, 2))
        elif number == 3:
            end, mid, two = self.chosen
            self.pair(*advance(line.place, two, self.mids[1], two, self.ends[1], True))
        else:
            end, mid, _ = self.chosen
            self.pair(*advance(line.place, end, self.mids[2], mid, self.ends[2], False))

    def fence(self, *values):
        state = (self.ends, self.mids, self.chosen, self.backs, self.moved)
        state, values = fence(state, values)
        self.ends, self.mids, self.chosen, self.backs, self.moved = state
        return values

    def arrived(self, number):
        if self.packed:
            if number == 1:
                return self.ends[0]
            if number == 2:
                return jnp.where(self.edge, self.ends[1], self.mids[1])
            return jnp.where(self.edge, self.ends[2], self.mids[0])
        return self.rows()[number] if number < self.line.count else None

    def rows(self):
        if self.packed:
            near, two, far = (self.arrived(number) for number in (1, 2, 3))
            return [self.own, jnp.where(self.odd, near, far), two, jnp.where(self.odd, far, near)]
        rights, lefts = ({at: pair[way] for at, pair in self.backs.items()} for way in range(2))
        hops = range(1, self.line.count)
        return [self.own] + [self.line.gathered(hop, rights, lefts) for hop in hops]

    def total(self, part):
        if self.packed:
            return plus(part, self.ends[3], self.mids[3])
        return plus(part, *self.moved)


def plus(total, *moved):
    total = total.astype(f32)
    for values in moved:
        total = total + (values.astype(f32) if isinstance(values, jax.Array) else values)
    return total


def paired_step(values, axis, bit):
    size = lax.axis_size(axis)
    return values + lax.ppermute(values, axis, [(at, at ^ bit) for at in range(size)])


def direct_sum(values, axis, stride=1):
    size = lax.axis_size(axis)
    terms = [values] + [
        lax.ppermute(values, axis, [(at, at ^ flip) for at in range(size)])
        for flip in range(stride, size, stride)
    ]
    while len(terms) > 1:
        terms = [left + right for left, right in zip(terms[::2], terms[1::2])]
    return terms[0]


def norm_forward(values, gain):
    scale = lax.rsqrt(jnp.mean(values * values, axis=-1, keepdims=True) + norm_eps)
    return scale, (values * scale * gain).astype(bf16)


def norm_backward(values, scale, gain, grad):
    unit = values * scale
    scaled = grad * gain
    back = scale * (scaled - unit * jnp.mean(scaled * unit, axis=-1, keepdims=True))
    return back, jnp.sum(grad * unit, axis=0)


def dot(left, right):
    return jnp.dot(left, right, preferred_element_type=f32)


def dot_nt(left, right):
    return lax.dot_general(left, right, (((1,), (1,)), ((), ())), preferred_element_type=f32)


def dot_tn(left, right):
    return lax.dot_general(left, right, (((0,), (0,)), ((), ())), preferred_element_type=f32)


def body(
    tokens, lengths, cotangent, first_gain, proj_in, conv_weight, conv_bias, rate_weight, rate_bias,
    input_weight, input_bias, decay_param, proj_out, second_gain, mlp_in, mlp_down,
):
    seq_count, local_len, width = tokens.shape
    wide = lax.axis_size("wide")
    chips = wide // 2
    me = lax.axis_index("wide")
    chip, core = me // 2, me % 2
    place = jnp.stack((chip, core)).astype(jnp.int32)
    channels = proj_in.shape[2]
    block_width = rate_weight.shape[1]
    seq_half = seq_count // 2
    block_shape = (2, seq_half, local_len, 2 * channels)
    line = Chips(wide, place)
    last = chips - 1

    def swap(values):
        return swap_cores(values, wide)

    def by_sequence(values):
        parts = values.reshape(2, seq_half * local_len, width)
        mine = jnp.where(core == 0, parts[0], parts[1])
        return jnp.concatenate((mine, swap(jnp.where(core == 0, parts[1], parts[0]))), axis=0)

    def both_orders(mine, other):
        return jnp.where(core == 0, jnp.stack((mine, other)), jnp.stack((other, mine)))

    def by_position(rows):
        own, other = jnp.split(rows, 2, axis=0)
        return both_orders(own, swap(other)).reshape(tokens.shape)

    def by_channel(values):
        mine, other = values[..., :channels], values[..., channels:]
        both = both_orders(mine, swap(other))
        return both.reshape(seq_count, *both.shape[2:])

    lengths = lax.dynamic_slice_in_dim(lengths, core * seq_half, seq_half)
    chunk = 2 * chip + (jnp.arange(2, dtype=jnp.int32) ^ core)
    positions = chunk[:, None] * local_len + jnp.arange(local_len, dtype=jnp.int32)
    mask = (positions[:, None, :] < lengths[None, :, None]).astype(f32).reshape(-1, 1)

    def both_cores(own, dim):
        return jnp.concatenate((own, swap(own)), axis=dim)

    own_in = narrow_whole(jnp.swapaxes(proj_in, 1, 2), 2)
    own_out = narrow_whole(proj_out, 1)
    own_mlp_in = narrow_whole(mlp_in, 1)
    own_down = narrow_whole(mlp_down, 1)
    tokens_f = by_sequence(tokens).astype(f32)
    scale_one, norm_in = norm_forward(tokens_f, first_gain)

    params = jnp.concatenate(
        (conv_weight, conv_bias[None], rate_bias[None], input_bias[None], decay_param[None]), axis=0
    )
    norm_in, params, cotangent = fence(norm_in, params, cotangent)

    def project(rows):
        return dot_nt(rows, whole_in).reshape(2, seq_half, local_len, 4 * channels)

    rows_first = [norm_in]
    for hop in range(1, chips):
        moved = line.ring(rows_first[-1])
        if hop == 1:
            out_grad = by_sequence(cotangent).astype(f32) * mask
            out_grad_b = out_grad.astype(bf16)
            params = both_cores(params, 1)
            gates = both_cores(jnp.stack((rate_weight, input_weight)), 1)
            gate_weight, gate_back = pack_gates(
                block_diagonal(gates[0]), block_diagonal(gates[1]), block_width
            )
            rate_scale = decay_scale * jax.nn.softplus(-params[7:8])
            moved, out_grad_b, gate_weight = fence(moved, out_grad_b, gate_weight)
        if hop == last - 1:
            moved, own_in = fence(moved, own_in)
        if hop == last:
            whole_in = both_cores(own_in, 1).reshape(-1, width)
            pre_blocks = [project(rows) for rows in rows_first]
            moved, out_grad_b, own_out, pre_blocks = fence(moved, out_grad_b, own_out, pre_blocks)
        rows_first.append(moved)

    lanes = Exchange(line, out_grad_b)
    lanes.step(1, None)
    whole_out = both_cores(own_out, 0)
    pre_blocks.append(project(rows_first[last]))
    mixed, *saved, final_state, conv_state = mixer_forward(
        pre_blocks, lengths, place, params[:4], params[4:5], gate_weight, params[5:7],
        rate_scale, block_width,
    )

    def mixed_part(flag, left, right):
        rows = mixed_rows[left]
        if left != right:
            rows = jnp.where(flag, rows, mixed_rows[right])
        return dot(rows, whole_out).astype(bf16)

    mixed_rows = mixed.reshape(chips, -1, 2 * channels)
    lanes.first(mixed_part)
    mixed_rows, final_state, conv_state = lanes.fence(mixed_rows, final_state, conv_state)
    for step in range(2, chips + 1):
        lanes.step(step, mixed_part)
        if step == 2:
            own_part = dot(mixed_rows[0], whole_out)
            final_state, conv_state = by_channel(final_state), by_channel(conv_state)
            own_part, mixed_rows, final_state, conv_state = lanes.fence(
                own_part, mixed_rows, final_state, conv_state
            )
        elif step == chips - 1:
            own_part, own_mlp_in = lanes.fence(own_part, own_mlp_in)
            other_mlp_in = swap(own_mlp_in)
        elif step < chips:
            (own_part,) = lanes.fence(own_part)
    rows_back = lanes.rows()
    own_part, rows_back, own_down = lanes.fence(own_part, rows_back, own_down)
    resid = tokens_f + lanes.total(own_part)

    scale_two, norm_mid = norm_forward(resid, second_gain)
    norm_mid, own_down = fence(norm_mid, own_down)
    other_down = swap(own_down)
    rows_second = [norm_mid]
    hidden, gate_grads, up_grads, parts, outs = [], [], [], [], []
    sums = None
    for hop in range(chips):
        if hop < last:
            rows_second.append(line.ring(rows_second[hop]))
        if hop > 1:
            sums = line.ring(total_b)
        made = mlp_block(
            rows_second[hop], rows_back[hop], own_mlp_in, other_mlp_in, own_down, other_down
        )
        rows_second, made, sums = fence(rows_second, made, sums)
        for kept, value in zip((hidden, gate_grads, up_grads, parts, outs), made):
            kept.append(value)
        if hop:
            total = parts[hop] if sums is None else plus(parts[hop], sums)
            total_b = total.astype(bf16)
    sums = line.ring(total_b)
    [grads_gate], _ = weight_grad(gate_grads, rows_second, 1)
    [grads_down], _ = weight_grad(hidden, rows_back, 1)
    sums, grads_gate, grads_down, up_grads = fence(sums, grads_gate, grads_down, up_grads)
    mid_sum = plus(parts[0], sums)

    from_norm, gain_two = norm_backward(resid, scale_two, second_gain, mid_sum)
    resid_grad = out_grad + from_norm
    resid_grad_b = resid_grad.astype(bf16)
    resid_grad_b, up_grads, outs = fence(resid_grad_b, up_grads, outs)

    def back_block(rows):
        return dot_nt(rows, whole_out).reshape(2, seq_half, local_len, 2 * channels)

    def out_part(flag, left, right):
        return outs[left] if left == right else jnp.where(flag, outs[left], outs[right])

    lanes = Exchange(line, resid_grad_b)
    lanes.step(1, None)
    lanes.first(out_part)
    [grads_up], _ = weight_grad(up_grads, rows_second, 1)
    from_down, from_gate = swap(grads_down[1]), swap(grads_gate[1])
    grads_up, from_down, from_gate, outs = lanes.fence(grads_up, from_down, from_gate, outs)
    back_blocks = [back_block(resid_grad_b)]
    for step in range(2, chips + 1):
        lanes.step(step, out_part)
        if step == 2:
            part_down = join((grads_down[0], from_down))
            part_mlp_in = join((grads_gate[0], from_gate), slots=2)
            from_up = swap(grads_up[1])
            part_down, part_mlp_in, from_up, outs = lanes.fence(part_down, part_mlp_in, from_up, outs)
            grad_mlp_down = narrow_sum(part_down, 1)
        elif step == 3:
            part_mlp_in = join((grads_up[0], from_up), slots=2, slot=1, filled=(part_mlp_in,))
            if lanes.packed:
                back_blocks += [back_block(lanes.arrived(at)) for at in (1, 2)]
            part_mlp_in, back_blocks = lanes.fence(part_mlp_in, back_blocks)
            grad_mlp_in = narrow_sum(part_mlp_in, 1)
        elif step < chips:
            lanes.fence()
    if lanes.packed:
        back_blocks.append(back_block(lanes.arrived(3)))
    else:
        back_blocks += [back_block(rows) for rows in lanes.rows()[1:]]
    grads, small, gate_grads = mixer_backward(
        back_blocks, lanes.packed, saved, lengths, place, params[:4], gate_back, block_width
    )
    grad_rows = grads.reshape(-1, 4 * channels)
    part = row_dot(grad_rows, whole_in, 1, chips, bf16)
    part, grad_rows, small, gate_grads, mixed, grad_mlp_down = lanes.fence(
        part, grad_rows, small, gate_grads, mixed, grad_mlp_down
    )

    size = lax.axis_size("narrow")
    split = size // 2 + 1
    count = rate_weight.shape[0]

    def gate_rows(gates, sums):
        return jnp.concatenate((gates.reshape(-1, block_width), sums.reshape(-1, block_width)), axis=0)

    gate_mine = gate_rows(gate_grads[:count], small[:, :channels])
    gate_other = gate_rows(gate_grads[count:], small[:, channels:])
    moving = line.ring(part)
    grads_in, [gain_one] = weight_grad([grad_rows], rows_first, 2, weight=whole_in)
    [grads_out], _ = weight_grad([mixed.reshape(-1, 2 * channels)], lanes.rows(), 1)
    gate_sum = (gate_mine + swap(gate_other.astype(bf16)).astype(f32)).astype(bf16)
    gate_sum = paired_step(gate_sum, "narrow", 1)
    grads_in, grads_out, gain_one, moving, gate_sum, resid, grad_rows = fence(
        grads_in, grads_out, gain_one, moving, gate_sum, resid, grad_rows
    )
    for hop in range(2, chips):
        sent = row_dot(grad_rows, whole_in, hop, chips, bf16, (moving,))
        if hop == 2:
            sent, grads_in, grads_out, gain_one = fence(sent, grads_in, grads_out, gain_one)
        moving = line.ring(sent)
    part = row_dot(grad_rows, whole_in, 0, chips)
    parts = join(*[(own, swap(other)) for own, other in (*grads_in, grads_out)])
    gains = jnp.concatenate((gain_one / first_gain, gain_two[None]), axis=0)
    parts, gate_sum, gains = fence(parts, gate_sum, gains)
    gains = direct_sum(gains, "narrow")
    sum_proj = DirectSum(parts)
    sum_proj.send(range(1, split))
    part, parts, grad_mlp_in, gate_sum, resid, gains, sum_proj.got = fence(
        part, parts, grad_mlp_in, gate_sum, resid, gains, sum_proj.got
    )
    sum_proj.grad = parts
    sum_proj.send(range(split, size))
    output = by_position((resid + lanes.total(outs[0])).astype(bf16))
    gains = gains + swap(gains)
    moving, output, gains, sum_proj.got, gate_sum = fence(
        moving, output, gains, sum_proj.got, gate_sum
    )
    bit = 2
    while bit < size:
        gate_sum = paired_step(gate_sum, "narrow", bit)
        bit *= 2
    in_sum = plus(part, moving)
    from_norm, _ = norm_backward(tokens_f, scale_one, first_gain, in_sum)
    grad_tokens = (resid_grad + from_norm).astype(bf16)
    grad_tokens, gains, sum_proj.got = fence(grad_tokens, gains, sum_proj.got)
    gains = direct_sum(gains, "wide", 2)
    grad_proj = sum_proj.total()
    gate_sum = gate_sum.astype(f32)
    gate_grads = gate_sum[: count * 2 * block_width].reshape(count, 2, block_width, block_width)
    small = gate_sum[count * 2 * block_width :].reshape(8, channels)
    grad_mlp_in, grad_mlp_down = grad_mlp_in.astype(f32), grad_mlp_down.astype(f32)
    grad_proj_in = grad_proj[: 2 * channels].reshape(2, channels, -1)
    grad_proj_out = grad_proj[2 * channels :]
    grad_mlp_in = grad_mlp_in.reshape(2, mlp_in.shape[2], -1)
    return (
        output,
        by_position(grad_tokens),
        final_state,
        conv_state,
        gains[0],
        jnp.swapaxes(grad_proj_in, 1, 2),
        small[4:8],
        small[3],
        gate_grads[:, 0],
        small[0],
        gate_grads[:, 1],
        small[1],
        small[2] * decay_scale * jax.nn.sigmoid(-decay_param),
        grad_proj_out,
        gains[1],
        jnp.swapaxes(grad_mlp_in, 1, 2),
        grad_mlp_down,
    )


def solution(mesh):
    return jax.shard_map(
        body,
        mesh=mesh,
        in_specs=(
            P("narrow", "wide", None),
            P("narrow"),
            P("narrow", "wide", None),
            P(),
            P(None, "narrow", "wide"),
            P(None, "wide"),
            P("wide"),
            P("wide", None, None),
            P("wide"),
            P("wide", None, None),
            P("wide"),
            P("wide"),
            P("wide", "narrow"),
            P(),
            P(None, "narrow", "wide"),
            P("wide", "narrow"),
        ),
        out_specs=(
            P("narrow", "wide", None),
            P("narrow", "wide", None),
            P("narrow", "wide"),
            P("narrow", None, "wide"),
            P(),
            P(None, "narrow", "wide"),
            P(None, "wide"),
            P("wide"),
            P("wide", None, None),
            P("wide"),
            P("wide", None, None),
            P("wide"),
            P("wide"),
            P("wide", "narrow"),
            P(),
            P(None, "narrow", "wide"),
            P("wide", "narrow"),
        ),
        check_vma=False,
    )
```

```python
from functools import partial

import jax
import jax.numpy as jnp
from jax import lax
from jax.experimental import pallas as pl
from jax.experimental.pallas import tpu as pltpu
from jax.sharding import PartitionSpec as P

decay_scale = 8.0
norm_eps = 1e-06
gelu_in = 0.7978845608028654
gelu_cube = 0.044715
f32 = jnp.float32
bf16 = jnp.bfloat16
kernel_cost = pl.CostEstimate(flops=1, bytes_accessed=1, transcendentals=0)
chain_cost = pl.CostEstimate(flops=1, bytes_accessed=1 << 26, transcendentals=0)


def gelu_tanh(v):
    return jnp.tanh(gelu_in * (v + gelu_cube * v * v * v))


def gelu_pair(v):
    t = gelu_tanh(v)
    half = 0.5 * (1.0 + t)
    slope = half + 0.5 * v * (1.0 - t * t) * (gelu_in + (3.0 * gelu_in * gelu_cube) * v * v)
    return v * half, slope


def one_minus_exp(v, decay):
    series = 1.0 - v * (1.0 / 7.0)
    for order in (6.0, 5.0, 4.0, 3.0, 2.0):
        series = 1.0 - v * (1.0 / order) * series
    return jnp.where(v < 0.3, v * series, 1.0 - decay * decay)


def gate_tiles(channels, block_width, tile):
    tiles, offset = [], 0
    for start in range(0, channels, tile):
        stop = min(start + tile, channels)
        low = start // block_width * block_width // 128 * 128
        high = min(-(-((stop - 1) // block_width + 1) * block_width // 128) * 128, channels)
        tiles.append((start, stop, low, high, offset))
        offset += high - low
    return tiles


def split_rows(values):
    high = values.astype(bf16)
    return jnp.concatenate((high, (values - high.astype(f32)).astype(bf16)), axis=0)


def joined_dot(halves, weight):
    both = jnp.dot(halves, weight, preferred_element_type=f32)
    rows = both.shape[0] // 2
    return both[:rows] + both[rows:]


def tile_scan(decay, drive, backward):
    rows, channels = decay.shape
    a = decay.reshape(rows // 8, 8, channels)
    b = drive.reshape(rows // 8, 8, channels)
    row = lax.broadcasted_iota(jnp.int32, (1, 8, channels), 1)
    for step in (1, 2, 4):
        if backward:
            keep, shift = row < 8 - step, 8 - step
        else:
            keep, shift = row >= step, step
        a_moved = jnp.where(keep, pltpu.roll(a, shift, 1), 1.0)
        b_moved = jnp.where(keep, pltpu.roll(b, shift, 1), 0.0)
        b = b + a * b_moved
        a = a * a_moved
    return a, b


def mixer_forward_kernel(
    chips, block_width, place, lengths, *refs
):
    pre_refs, refs = refs[:chips], refs[chips:]
    conv_weight, conv_bias, gate_weight, gate_bias, rate_scale = refs[:5]
    mixed, *saved = refs[5:15]
    final_state, conv_state, pre_now, x_tail, carry = refs[15:]
    chunk = pl.program_id(0)
    seq_count, local_len, channels = pre_now.shape
    channels //= 2
    pick_block(chunk, place, chips, pre_refs, pre_now)

    @pl.when(chunk == 0)
    def _():
        x_tail[...] = jnp.zeros_like(x_tail)
        carry[...] = jnp.zeros_like(carry)

    convs = []
    for seq in range(seq_count):
        x = pre_now[seq, :, channels:]
        extended = jnp.concatenate((x_tail[seq], x), axis=0)
        conv = conv_bias[...] + conv_weight[0:1] * x
        for lag in range(1, 4):
            conv = conv + conv_weight[lag : lag + 1] * extended[8 - lag : 8 - lag + local_len]
        x_tail[seq] = x[local_len - 8 :]
        convs.append(conv)
        for tap in range(3):
            position = lengths[seq] - 3 + tap

            @pl.when(position // local_len == chunk)
            def _(seq=seq, tap=tap, position=position):
                conv_state[seq, tap : tap + 1] = pre_now[
                    seq, pl.ds(lax.rem(position, local_len), 1), channels:
                ]

    conv_all = jnp.concatenate(convs, axis=0)
    parted = split_rows(conv_all)
    rate_parts, in_parts = [], []
    for start, stop, low, high, at in gate_tiles(channels, block_width, 128):
        both = joined_dot(parted[:, low:high], gate_weight[at : at + high - low])
        rate_parts.append(both[:, : stop - start])
        in_parts.append(both[:, 128 : 128 + stop - start])
    rate_all = jax.nn.sigmoid(jnp.concatenate(rate_parts, axis=1) + gate_bias[0:1])
    in_all = jax.nn.sigmoid(jnp.concatenate(in_parts, axis=1) + gate_bias[1:2])
    for seq in range(seq_count):
        rows = slice(seq * local_len, (seq + 1) * local_len)
        conv = convs[seq]
        rate_gate = rate_all[rows]
        in_gate = in_all[rows]
        step_log = rate_scale[...] * rate_gate
        decay = jnp.exp(-step_log)
        square = jnp.maximum(one_minus_exp(2.0 * step_log, decay), 1e-36)
        inverse_root = lax.rsqrt(square)
        root = square * inverse_root
        position = chunk * local_len + lax.broadcasted_iota(jnp.int32, (local_len, 1), 0)
        live = position < lengths[seq]
        gated_conv = in_gate * conv
        driven = root * gated_conv
        kept_decay = jnp.where(live, decay, 1.0)
        a, b = tile_scan(kept_decay, jnp.where(live, driven, 0.0), False)
        last = carry[seq]
        tiles = []
        for tile in range(local_len // 8):
            tiles.append(b[tile] + a[tile] * last)
            last = tiles[-1][7:8]
        states = jnp.concatenate(tiles, axis=0)
        carry[seq] = last
        final_state[seq : seq + 1] = last
        gated, slope = gelu_pair(pre_now[seq, :, :channels])
        mixed[0, 0, seq] = (gated * states).astype(bf16)
        rate_factor = (states - driven - gated_conv * decay * decay * inverse_root) * rate_gate
        for out, value in zip(
            saved,
            (
                gated,
                slope * states,
                kept_decay,
                rate_factor,
                -rate_scale[...] * rate_factor * (1.0 - rate_gate),
                driven * (1.0 - in_gate),
                root * in_gate,
                pre_now[seq, :, channels:],
                conv.astype(bf16),
            ),
        ):
            out[0, 0, seq] = value


def mixer_backward_kernel(
    chips, block_width, crossed, place, lengths, *refs
):
    back_refs, refs = refs[:chips], refs[chips:]
    gated_in, y_in, decay_in, rate_in, rate_pre_in, in_pre_in, direct_in, x_in, conv_in = refs[:9]
    conv_weight, gate_back, grads, sums, gate_grads = refs[9:14]
    back_now, carry, grad_head, gate_sums = refs[14:]
    step = pl.program_id(0)
    chunk = pl.num_programs(0) - 1 - step
    seq_count, local_len, channels = back_now.shape
    pick_block(chunk, place, chips, back_refs, back_now, crossed)

    @pl.when(step == 0)
    def _():
        carry[...] = jnp.zeros_like(carry)
        grad_head[...] = jnp.zeros_like(grad_head)
        sums[...] = jnp.zeros_like(sums)
        gate_sums[...] = jnp.zeros_like(gate_sums)

    rate_pre, in_pre, direct = [], [], []
    decay_sum = jnp.zeros((1, channels), f32)
    for seq in range(seq_count):
        position = chunk * local_len + lax.broadcasted_iota(jnp.int32, (local_len, 1), 0)
        live = position < lengths[seq]
        mixer_grad = back_now[seq]
        grads[0, 0, seq, :, :channels] = (mixer_grad * y_in[0, 0, seq]).astype(bf16)
        source = mixer_grad * gated_in[0, 0, seq]
        decay = decay_in[0, 0, seq]
        a, b = tile_scan(decay, decay * source, True)
        following = carry[seq]
        tiles = []
        for tile in reversed(range(local_len // 8)):
            passed = b[tile] + a[tile] * following
            tiles.append(jnp.concatenate((passed[1:], following), axis=0))
            following = passed[0:1]
        carry[seq] = following
        adjoint = source + jnp.concatenate(tiles[::-1], axis=0)
        adjoint = jnp.where(live, adjoint, 0.0)
        decay_sum = decay_sum + jnp.sum(adjoint * rate_in[0, 0, seq], axis=0, keepdims=True)
        rate_pre.append(adjoint * rate_pre_in[0, 0, seq])
        in_pre.append(adjoint * in_pre_in[0, 0, seq])
        direct.append(adjoint * direct_in[0, 0, seq])
    rate_all = jnp.concatenate(rate_pre, axis=0)
    in_all = jnp.concatenate(in_pre, axis=0)
    conv_all = jnp.concatenate([conv_in[0, 0, seq] for seq in range(seq_count)], axis=0)
    rate_b, in_b = rate_all.astype(bf16), in_all.astype(bf16)
    for start, stop, low, high, at in gate_tiles(channels, block_width, 128):
        both = jnp.concatenate((rate_b[:, start:stop], in_b[:, start:stop]), axis=1)
        part = lax.dot_general(
            conv_all[:, low:high], both, (((0,), (0,)), ((), ())), preferred_element_type=f32
        )
        if stop - start == 128:
            gate_sums[at : at + high - low] += part
        else:
            gate_sums[at : at + high - low, : stop - start] += part[:, : stop - start]
            gate_sums[at : at + high - low, 128 : 128 + stop - start] += part[:, stop - start :]
    parts = []
    for start, stop, low, high, at in gate_tiles(channels, block_width, 256):
        both = jnp.concatenate((rate_b[:, low:high], in_b[:, low:high]), axis=1)
        parts.append(dot(both, gate_back[2 * at : 2 * (at + high - low)])[:, : stop - start])
    conv_grad = jnp.concatenate(direct, axis=0) + jnp.concatenate(parts, axis=1)
    tap_sums = [jnp.zeros((1, channels), f32) for _ in range(4)]
    for seq in range(seq_count):
        part = conv_grad[seq * local_len : (seq + 1) * local_len]
        extended = jnp.concatenate((part, grad_head[seq]), axis=0)
        x = x_in[0, 0, seq]
        total = conv_weight[0:1] * part
        tap_sums[0] = tap_sums[0] + jnp.sum(part * x, axis=0, keepdims=True)
        for lag in range(1, 4):
            moved = extended[lag : lag + local_len]
            total = total + conv_weight[lag : lag + 1] * moved
            tap_sums[lag] = tap_sums[lag] + jnp.sum(moved * x, axis=0, keepdims=True)
        grads[0, 0, seq, :, channels:] = total.astype(bf16)
        grad_head[seq] = part[:8]
    sums[0:1] += jnp.sum(rate_all, axis=0, keepdims=True)
    sums[1:2] += jnp.sum(in_all, axis=0, keepdims=True)
    sums[2:3] += decay_sum
    sums[3:4] += jnp.sum(conv_grad, axis=0, keepdims=True)
    for lag in range(4):
        sums[4 + lag : 5 + lag] += tap_sums[lag]

    @pl.when(chunk == 0)
    def _():
        tiles = gate_tiles(channels, block_width, 128)
        for kind, column in enumerate((0, 128)):
            for base in range(0, channels, block_width):
                pieces = []
                for start, stop, low, _, at in tiles:
                    left, right = max(start, base), min(stop, base + block_width)
                    if left < right:
                        row = at + base - low
                        span = gate_sums[row : row + block_width, column : column + 128]
                        pieces.append(span[:, left - start : right - start])
                gate_grads[base // block_width, kind] = jnp.concatenate(pieces, axis=1)


def chunk_place(chunk, place, chips):
    return lax.rem(place[0] - chunk // 2 + chips, chips), lax.rem(chunk + place[1], 2)


def pick_block(chunk, place, chips, refs, now, crossed=False):
    slot = (chunk // 2) ^ place[0] if crossed else chunk_place(chunk, place, chips)[0]
    for hop in range(chips):

        @pl.when(slot == hop)
        def _(hop=hop):
            now[...] = refs[hop][0]


def mixer_specs(shape, chips, chunk_of):
    def hop_map(hop, crossed, step, place, lengths):
        first = 2 * (place[0] ^ hop if crossed else lax.rem(place[0] - hop + chips, chips))
        return (jnp.where(chunk_of(step) <= first, place[1], 1 - place[1]), 0, 0, 0)

    def block_map(step, place, lengths):
        chip, core = chunk_place(chunk_of(step), place, chips)
        return (chip, core, 0, 0, 0)

    def hops(lanes, crossed=False):
        block = (1, *shape[1:3], lanes)
        return [pl.BlockSpec(block, partial(hop_map, hop, crossed)) for hop in range(chips)]

    def block(lanes):
        return pl.BlockSpec((1, 1, *shape[1:3], lanes), block_map)

    return hops, block


def whole_spec(shape):
    return pl.BlockSpec(shape, lambda step, place, lengths: (0,) * len(shape))


def mixer_forward(
    pre_blocks, lengths, place, conv_weight, conv_bias, gate_weight, gate_bias, rate_scale, block_width
):
    chips = len(pre_blocks)
    _, seq_count, local_len, channels = pre_blocks[0].shape
    channels //= 2
    hops, block = mixer_specs(pre_blocks[0].shape, chips, lambda step: step)
    full = (chips, 2, seq_count, local_len, channels)
    params = (conv_weight, conv_bias, gate_weight, gate_bias, rate_scale)
    return pl.pallas_call(
        partial(mixer_forward_kernel, chips, block_width),
        grid_spec=pltpu.PrefetchScalarGridSpec(
            num_scalar_prefetch=2,
            grid=(2 * chips,),
            in_specs=hops(2 * channels) + [whole_spec(param.shape) for param in params],
            out_specs=[block(channels)] * 10
            + [whole_spec((seq_count, channels)), whole_spec((seq_count, 3, channels))],
            scratch_shapes=[
                pltpu.VMEM((seq_count, local_len, 2 * channels), f32),
                pltpu.VMEM((seq_count, 8, channels), f32),
                pltpu.VMEM((seq_count, 1, channels), f32),
            ],
        ),
        out_shape=[pltpu.HBM(full, bf16)]
        + [pltpu.HBM(full, f32)] * 8
        + [pltpu.HBM(full, bf16)]
        + [
            jax.ShapeDtypeStruct((seq_count, channels), f32),
            jax.ShapeDtypeStruct((seq_count, 3, channels), f32),
        ],
        compiler_params=pltpu.CompilerParams(vmem_limit_bytes=32 << 20),
        cost_estimate=kernel_cost,
        name="mixer_forward",
    )(place, lengths, *pre_blocks, *params)


def mixer_backward(
    back_blocks, crossed, saved, lengths, place, conv_weight, gate_back, block_width
):
    chips = len(back_blocks)
    _, seq_count, local_len, channels = back_blocks[0].shape
    hops, block = mixer_specs(back_blocks[0].shape, chips, lambda step: 2 * chips - 1 - step)
    full = (chips, 2, seq_count, local_len, channels)
    params = (conv_weight, gate_back)
    packed = gate_tiles(channels, block_width, 128)[-1]
    packed = packed[4] + packed[3] - packed[2]
    gate_shape = (channels // block_width, 2, block_width, block_width)
    return pl.pallas_call(
        partial(mixer_backward_kernel, chips, block_width, crossed),
        grid_spec=pltpu.PrefetchScalarGridSpec(
            num_scalar_prefetch=2,
            grid=(2 * chips,),
            in_specs=hops(channels, crossed)
            + [block(channels)] * 9
            + [whole_spec(param.shape) for param in params],
            out_specs=[block(2 * channels), whole_spec((8, channels)), whole_spec(gate_shape)],
            scratch_shapes=[
                pltpu.VMEM((seq_count, local_len, channels), f32),
                pltpu.VMEM((seq_count, 1, channels), f32),
                pltpu.VMEM((seq_count, 8, channels), f32),
                pltpu.VMEM((packed, 256), f32),
            ],
        ),
        out_shape=[
            pltpu.HBM((*full[:-1], 2 * channels), bf16),
            jax.ShapeDtypeStruct((8, channels), f32),
            jax.ShapeDtypeStruct(gate_shape, f32),
        ],
        compiler_params=pltpu.CompilerParams(vmem_limit_bytes=32 << 20),
        cost_estimate=kernel_cost,
        name="mixer_backward",
    )(place, lengths, *back_blocks, *saved, *params)


def mlp_kernel(tiles, rows, back, own_in, other_in, own_down, other_down, *refs):
    hidden, gate_grads, up_grads, middle, out, middle_sum, out_sum = refs
    step = pl.program_id(0)

    @pl.when(step == 0)
    def _():
        middle_sum[...] = jnp.zeros_like(middle_sum)
        out_sum[...] = jnp.zeros_like(out_sum)

    def units(weight_in, weight_down):
        gated, slope = gelu_pair(dot(rows[...], weight_in[0]))
        up_pre = dot(rows[...], weight_in[1])
        hidden_grad = dot_nt(back[...], weight_down[...])
        hidden_b = (gated * up_pre).astype(bf16)
        gate_b = (hidden_grad * up_pre * slope).astype(bf16)
        up_b = (hidden_grad * gated).astype(bf16)
        hidden[...] = hidden_b
        gate_grads[...] = gate_b
        up_grads[...] = up_b
        out_sum[...] += dot(hidden_b, weight_down[...])
        middle_sum[...] += dot_nt(gate_b, weight_in[0]) + dot_nt(up_b, weight_in[1])

    @pl.when(step < tiles)
    def _():
        units(own_in, own_down)

    @pl.when(step >= tiles)
    def _():
        units(other_in, other_down)

    @pl.when(step == 2 * tiles - 1)
    def _():
        middle[...] = middle_sum[...]
        out[...] = out_sum[...].astype(bf16)


def mlp_block(rows, back, own_in, other_in, own_down, other_down):
    count, width = rows.shape
    units = own_down.shape[0]
    tile = 256 if units % 256 == 0 else 128
    tiles = units // tile

    def own_tile(step):
        return jnp.minimum(step, tiles - 1)

    def other_tile(step):
        return jnp.maximum(step - tiles, 0)

    whole = pl.BlockSpec((count, width), lambda step: (0, 0))
    tiled = pl.BlockSpec((count, tile), lambda step: (0, step))
    return pl.pallas_call(
        partial(mlp_kernel, tiles),
        grid=(2 * tiles,),
        in_specs=[
            whole,
            whole,
            pl.BlockSpec((2, width, tile), lambda step: (0, 0, own_tile(step))),
            pl.BlockSpec((2, width, tile), lambda step: (0, 0, other_tile(step))),
            pl.BlockSpec((tile, width), lambda step: (own_tile(step), 0)),
            pl.BlockSpec((tile, width), lambda step: (other_tile(step), 0)),
        ],
        out_specs=[tiled] * 3 + [whole] * 2,
        out_shape=[pltpu.HBM((count, 2 * units), bf16)] * 3
        + [pltpu.HBM((count, width), f32), pltpu.HBM((count, width), bf16)],
        scratch_shapes=[pltpu.VMEM((count, width), f32)] * 2,
        compiler_params=pltpu.CompilerParams(vmem_limit_bytes=36 << 20),
        cost_estimate=kernel_cost,
        name="mlp_block",
    )(rows, back, own_in, other_in, own_down, other_down)


def weight_grad_kernel(count, kinds, weighted, *refs):
    lefts, rights = refs[:count], refs[count : 2 * count]
    outs = refs[2 * count + weighted :]
    total = dot_tn(lefts[0][...], rights[0][...])
    for left, right in zip(lefts[1:], rights[1:]):
        total = total + dot_tn(left[...], right[...])
    half = outs[0].shape[0]
    for kind in range(kinds):
        start = 2 * kind * half
        outs[kind][...] = total[start : start + half]
        outs[kinds + kind][...] = total[start + half : start + 2 * half].astype(bf16)
    if weighted:
        weight = refs[2 * count][...]
        outs[2 * kinds][...] = jnp.sum(total * weight.astype(f32), axis=0, keepdims=True)


def weight_grad(lefts, rights, kinds, weight=None):
    count = len(rights)
    rows, width = rights[0].shape
    columns = lefts[0].shape[1]
    half, tile = columns // kinds // 2, min(512, width)
    joined = len(lefts) == 1

    def left_spec(at):
        block = at if joined else 0
        return pl.BlockSpec((rows, columns), lambda step: (block, 0))

    lefts = list(lefts) * (count if joined else 1)
    weights = [] if weight is None else [weight]
    made = pl.pallas_call(
        partial(weight_grad_kernel, count, kinds, len(weights)),
        grid=(width // tile,),
        in_specs=[left_spec(at) for at in range(count)]
        + [pl.BlockSpec((rows, tile), lambda step: (0, step))] * count
        + [pl.BlockSpec((columns, tile), lambda step: (0, step))] * len(weights),
        out_specs=[pl.BlockSpec((half, tile), lambda step: (0, step))] * (2 * kinds)
        + [pl.BlockSpec((1, tile), lambda step: (0, step))] * len(weights),
        out_shape=[pltpu.HBM((half, width), f32)] * kinds
        + [pltpu.HBM((half, width), bf16)] * kinds
        + [jax.ShapeDtypeStruct((1, width), f32)] * len(weights),
        compiler_params=pltpu.CompilerParams(vmem_limit_bytes=28 << 20),
        cost_estimate=kernel_cost,
        name="weight_grad",
    )(*lefts, *rights, *weights)
    return list(zip(made[:kinds], made[kinds : 2 * kinds])), made[2 * kinds :]


def row_dot_kernel(rows, weight, *refs):
    total = dot(rows[...], weight[...])
    if len(refs) > 1:
        total = total + refs[0][...].astype(f32)
    refs[-1][...] = total.astype(refs[-1].dtype)


def row_dot(rows, weight, block, count, kind=f32, moving=()):
    depth, width = weight.shape
    size, tile = rows.shape[0] // count, min(512, width)
    return pl.pallas_call(
        row_dot_kernel,
        grid=(width // tile,),
        in_specs=[
            pl.BlockSpec((size, depth), lambda step: (block, 0)),
            pl.BlockSpec((depth, tile), lambda step: (0, step)),
        ]
        + [pl.BlockSpec((size, tile), lambda step: (0, step))] * len(moving),
        out_specs=pl.BlockSpec((size, tile), lambda step: (0, step)),
        out_shape=pltpu.HBM((size, width), kind),
        compiler_params=pltpu.CompilerParams(vmem_limit_bytes=10 << 20),
        cost_estimate=chain_cost if moving else kernel_cost,
        name="row_dot",
    )(rows, weight, *moving)


def join_kernel(count, tiles, *refs):
    out = refs[-1]
    for at in range(count):

        @pl.when(pl.program_id(0) // tiles == at)
        def _(at=at):
            out[...] = (refs[2 * at][...] + refs[2 * at + 1][...].astype(f32)).astype(bf16)


def join(*pairs, slots=1, slot=0, filled=(), tile=128):
    count = len(pairs)
    rows, width = pairs[0][0].shape
    tile = tile if rows % tile == 0 else rows // 2
    tiles = rows // tile

    def spec(at):
        return pl.BlockSpec((tile, width), lambda step: (jnp.clip(step - at * tiles, 0, tiles - 1), 0))

    return pl.pallas_call(
        partial(join_kernel, count, tiles),
        grid=(count * tiles,),
        in_specs=[spec(at) for at in range(count) for _ in range(2)]
        + [pl.BlockSpec(memory_space=pl.ANY)] * len(filled),
        out_specs=pl.BlockSpec((tile, width), lambda step: (slot * count * tiles + step, 0)),
        out_shape=pltpu.HBM((slots * count * rows, width), bf16),
        input_output_aliases={2 * count: 0} if filled else {},
        compiler_params=pltpu.CompilerParams(vmem_limit_bytes=16 << 20),
        cost_estimate=kernel_cost,
        name="join",
    )(*[value for pair in pairs for value in pair], *filled)


def block_diagonal(weight):
    count, width, _ = weight.shape
    rows = [
        jnp.pad(weight[at], ((0, 0), (at * width, (count - 1 - at) * width))) for at in range(count)
    ]
    return jnp.concatenate(rows, axis=0)


def pack_gates(rate, into, block_width):
    def padded(values, width):
        return jnp.pad(values, ((0, 0), (0, width - values.shape[1])))

    channels = rate.shape[0]
    forward, back = [], []
    for start, stop, low, high, _ in gate_tiles(channels, block_width, 128):
        forward.append(
            jnp.concatenate(
                (padded(rate[low:high, start:stop], 128), padded(into[low:high, start:stop], 128)), axis=1
            )
        )
    for start, stop, low, high, _ in gate_tiles(channels, block_width, 256):
        back.append(padded(rate.T[low:high, start:stop], 256))
        back.append(padded(into.T[low:high, start:stop], 256))
    return jnp.concatenate(forward, axis=0), jnp.concatenate(back, axis=0)


def narrow_whole(weight, dim):
    return lax.all_gather(weight, "narrow", axis=dim, tiled=True)


def narrow_sum(grad, dim):
    return lax.psum_scatter(grad, "narrow", scatter_dimension=dim, tiled=True)


class DirectSum:
    def __init__(self, grad):
        self.size = lax.axis_size("narrow")
        self.grad, self.got = grad, []

    def piece(self, flip):
        span = self.grad.shape[1] // self.size
        start = (lax.axis_index("narrow") ^ flip) * span
        return lax.dynamic_slice_in_dim(self.grad, start, span, axis=1)

    def send(self, flips):
        for flip in flips:
            pairs = [(at, at ^ flip) for at in range(self.size)]
            self.got.append(lax.ppermute(self.piece(flip), "narrow", pairs))

    def total(self):
        return plus(self.piece(0), *self.got)


def swap_cores(values, wide):
    return lax.ppermute(values, "wide", [(at, at ^ 1) for at in range(wide)])


def fence(*values):
    return lax.optimization_barrier(values)


class Chips:
    def __init__(self, wide, place):
        self.place, self.chip, self.count = place, place[0], wide // 2
        self.wide = wide

    def move(self, values, pairs):
        devices = [(2 * a + core, 2 * b + core) for a, b in pairs for core in range(2)]
        return lax.ppermute(values, "wide", devices)

    def ring(self, values):
        return self.move(values, [(at, (at + 1) % self.count) for at in range(self.count)])

    def gather_step(self, step, right, left):
        count = self.count
        to_right = [(at, at + 1) for at in range(step - 1, count - 1)]
        to_left = [(at, at - 1) for at in range(1, count - step + 1)]
        if 2 * step > count + 1:
            both = self.move(jnp.where(self.chip >= step - 1, right, left), to_right + to_left)
            return both, both
        return self.move(right, to_right), self.move(left, to_left)

    def gathered(self, hop, rights, lefts):
        return jnp.where(self.chip >= hop, rights[hop], lefts[self.count - hop])

    def sum_step(self, step, right, left):
        count = self.count
        to_right = [(at, at + 1) for at in range(step)]
        to_left = [(at, at - 1) for at in range(count - step, count)]
        if 2 * step < count - 1:
            both = self.move(jnp.where(self.chip < step, right, left), to_right + to_left)
            return both, both
        return self.move(right, to_right), self.move(left, to_left)


def advance_kernel(place, end_part, end_moved, mid_part, mid_moved, end, mid, *, inner):
    added = end_part[...].astype(f32) + end_moved[...].astype(f32)
    mid[...] = (mid_part[...].astype(f32) + mid_moved[...].astype(f32)).astype(bf16)
    if inner:
        edge = (place[0] == 0) | (place[0] == 3)

        @pl.when(edge)
        def _():
            end[...] = end_part[...].astype(bf16)

        @pl.when(jnp.logical_not(edge))
        def _():
            end[...] = end_moved[...]
    else:
        end[...] = added.astype(bf16)


def advance(place, end_part, end_moved, mid_part, mid_moved, inner):
    rows, width = end_moved.shape
    tile = min(64, rows)
    spec = pl.BlockSpec((tile, width), lambda step, place: (step, 0))
    return pl.pallas_call(
        partial(advance_kernel, inner=inner),
        grid_spec=pltpu.PrefetchScalarGridSpec(
            num_scalar_prefetch=1, grid=(rows // tile,), in_specs=[spec] * 4, out_specs=[spec] * 2
        ),
        out_shape=[pltpu.HBM((rows, width), bf16)] * 2,
        compiler_params=pltpu.CompilerParams(vmem_limit_bytes=8 << 20),
        cost_estimate=kernel_cost,
        name="advance",
    )(place, end_part, end_moved, mid_part, mid_moved)


class Exchange:
    def __init__(self, line, rows):
        self.line, self.own = line, rows
        self.packed = line.count == 4
        if self.packed:
            self.odd = line.chip % 2 == 1
            self.edge = (line.chip == 0) | (line.chip == 3)
        self.ends, self.mids, self.chosen = [], [], ()
        self.backs, self.moved = {0: (rows, rows)}, (0.0, 0.0)

    def pair(self, end, mid):
        self.ends.append(self.line.move(end, [(0, 1), (1, 0), (2, 3), (3, 2)]))
        self.mids.append(self.line.move(mid, [(1, 2), (2, 1)]))

    def first(self, choose):
        if self.packed:
            self.chosen = (choose(self.line.chip == 0, 1, 3),)

    def step(self, number, choose):
        line, count = self.line, self.line.count
        if not self.packed:
            if number < count:
                self.backs[number] = line.gather_step(number, *self.backs[number - 1])
            if number > 1:
                sent = [
                    plus(choose(True, hop, hop), self.moved[way]).astype(bf16)
                    for way, hop in enumerate((number - 1, count - number + 1))
                ]
                self.moved = line.sum_step(number - 1, *sent)
        elif number == 1:
            self.pair(self.own, self.own)
        elif number == 2:
            self.pair(jnp.where(self.edge, self.chosen[0], self.mids[0]), self.ends[0])
            self.chosen = (choose(self.odd, 1, 3), choose(line.chip == 1, 3, 1), choose(True, 2, 2))
        elif number == 3:
            end, mid, two = self.chosen
            self.pair(*advance(line.place, two, self.mids[1], two, self.ends[1], True))
        else:
            end, mid, _ = self.chosen
            self.pair(*advance(line.place, end, self.mids[2], mid, self.ends[2], False))

    def fence(self, *values):
        state = (self.ends, self.mids, self.chosen, self.backs, self.moved)
        state, values = fence(state, values)
        self.ends, self.mids, self.chosen, self.backs, self.moved = state
        return values

    def arrived(self, number):
        if self.packed:
            if number == 1:
                return self.ends[0]
            if number == 2:
                return jnp.where(self.edge, self.ends[1], self.mids[1])
            return jnp.where(self.edge, self.ends[2], self.mids[0])
        return self.rows()[number] if number < self.line.count else None

    def rows(self):
        if self.packed:
            near, two, far = (self.arrived(number) for number in (1, 2, 3))
            return [self.own, jnp.where(self.odd, near, far), two, jnp.where(self.odd, far, near)]
        rights, lefts = ({at: pair[way] for at, pair in self.backs.items()} for way in range(2))
        hops = range(1, self.line.count)
        return [self.own] + [self.line.gathered(hop, rights, lefts) for hop in hops]

    def total(self, part):
        if self.packed:
            return plus(part, self.ends[3], self.mids[3])
        return plus(part, *self.moved)


def plus(total, *moved):
    total = total.astype(f32)
    for values in moved:
        total = total + (values.astype(f32) if isinstance(values, jax.Array) else values)
    return total


def paired_step(values, axis, bit):
    size = lax.axis_size(axis)
    return values + lax.ppermute(values, axis, [(at, at ^ bit) for at in range(size)])


def direct_sum(values, axis, stride=1):
    size = lax.axis_size(axis)
    terms = [values] + [
        lax.ppermute(values, axis, [(at, at ^ flip) for at in range(size)])
        for flip in range(stride, size, stride)
    ]
    while len(terms) > 1:
        terms = [left + right for left, right in zip(terms[::2], terms[1::2])]
    return terms[0]


def norm_forward(values, gain):
    scale = lax.rsqrt(jnp.mean(values * values, axis=-1, keepdims=True) + norm_eps)
    return scale, (values * scale * gain).astype(bf16)


def norm_backward(values, scale, gain, grad):
    unit = values * scale
    scaled = grad * gain
    back = scale * (scaled - unit * jnp.mean(scaled * unit, axis=-1, keepdims=True))
    return back, jnp.sum(grad * unit, axis=0)


def dot(left, right):
    return jnp.dot(left, right, preferred_element_type=f32)


def dot_nt(left, right):
    return lax.dot_general(left, right, (((1,), (1,)), ((), ())), preferred_element_type=f32)


def dot_tn(left, right):
    return lax.dot_general(left, right, (((0,), (0,)), ((), ())), preferred_element_type=f32)


def body(
    tokens, lengths, cotangent, first_gain, proj_in, conv_weight, conv_bias, rate_weight, rate_bias,
    input_weight, input_bias, decay_param, proj_out, second_gain, mlp_in, mlp_down,
):
    seq_count, local_len, width = tokens.shape
    wide = lax.axis_size("wide")
    chips = wide // 2
    me = lax.axis_index("wide")
    chip, core = me // 2, me % 2
    place = jnp.stack((chip, core)).astype(jnp.int32)
    channels = proj_in.shape[2]
    block_width = rate_weight.shape[1]
    seq_half = seq_count // 2
    block_shape = (2, seq_half, local_len, 2 * channels)
    line = Chips(wide, place)
    last = chips - 1

    def swap(values):
        return swap_cores(values, wide)

    def by_sequence(values):
        parts = values.reshape(2, seq_half * local_len, width)
        mine = jnp.where(core == 0, parts[0], parts[1])
        return jnp.concatenate((mine, swap(jnp.where(core == 0, parts[1], parts[0]))), axis=0)

    def both_orders(mine, other):
        return jnp.where(core == 0, jnp.stack((mine, other)), jnp.stack((other, mine)))

    def by_position(rows):
        own, other = jnp.split(rows, 2, axis=0)
        return both_orders(own, swap(other)).reshape(tokens.shape)

    def by_channel(values):
        mine, other = values[..., :channels], values[..., channels:]
        both = both_orders(mine, swap(other))
        return both.reshape(seq_count, *both.shape[2:])

    lengths = lax.dynamic_slice_in_dim(lengths, core * seq_half, seq_half)
    chunk = 2 * chip + (jnp.arange(2, dtype=jnp.int32) ^ core)
    positions = chunk[:, None] * local_len + jnp.arange(local_len, dtype=jnp.int32)
    mask = (positions[:, None, :] < lengths[None, :, None]).astype(f32).reshape(-1, 1)

    def both_cores(own, dim):
        return jnp.concatenate((own, swap(own)), axis=dim)

    own_in = narrow_whole(jnp.swapaxes(proj_in, 1, 2), 2)
    own_out = narrow_whole(proj_out, 1)
    own_mlp_in = narrow_whole(mlp_in, 1)
    own_down = narrow_whole(mlp_down, 1)
    tokens_f = by_sequence(tokens).astype(f32)
    scale_one, norm_in = norm_forward(tokens_f, first_gain)

    params = jnp.concatenate(
        (conv_weight, conv_bias[None], rate_bias[None], input_bias[None], decay_param[None]), axis=0
    )
    norm_in, params, cotangent = fence(norm_in, params, cotangent)

    def project(rows):
        return dot_nt(rows, whole_in).reshape(2, seq_half, local_len, 4 * channels)

    rows_first = [norm_in]
    for hop in range(1, chips):
        moved = line.ring(rows_first[-1])
        if hop == 1:
            out_grad = by_sequence(cotangent).astype(f32) * mask
            out_grad_b = out_grad.astype(bf16)
            params = both_cores(params, 1)
            gates = both_cores(jnp.stack((rate_weight, input_weight)), 1)
            gate_weight, gate_back = pack_gates(
                block_diagonal(gates[0]), block_diagonal(gates[1]), block_width
            )
            rate_scale = decay_scale * jax.nn.softplus(-params[7:8])
            moved, out_grad_b, gate_weight = fence(moved, out_grad_b, gate_weight)
        if hop == last - 1:
            moved, own_in = fence(moved, own_in)
        if hop == last:
            whole_in = both_cores(own_in, 1).reshape(-1, width)
            pre_blocks = [project(rows) for rows in rows_first]
            moved, out_grad_b, own_out, pre_blocks = fence(moved, out_grad_b, own_out, pre_blocks)
        rows_first.append(moved)

    lanes = Exchange(line, out_grad_b)
    lanes.step(1, None)
    whole_out = both_cores(own_out, 0)
    pre_blocks.append(project(rows_first[last]))
    mixed, *saved, final_state, conv_state = mixer_forward(
        pre_blocks, lengths, place, params[:4], params[4:5], gate_weight, params[5:7],
        rate_scale, block_width,
    )

    def mixed_part(flag, left, right):
        rows = mixed_rows[left]
        if left != right:
            rows = jnp.where(flag, rows, mixed_rows[right])
        return dot(rows, whole_out).astype(bf16)

    mixed_rows = mixed.reshape(chips, -1, 2 * channels)
    lanes.first(mixed_part)
    mixed_rows, final_state, conv_state = lanes.fence(mixed_rows, final_state, conv_state)
    for step in range(2, chips + 1):
        lanes.step(step, mixed_part)
        if step == 2:
            own_part = dot(mixed_rows[0], whole_out)
            final_state, conv_state = by_channel(final_state), by_channel(conv_state)
            own_part, mixed_rows, final_state, conv_state = lanes.fence(
                own_part, mixed_rows, final_state, conv_state
            )
        elif step == chips - 1:
            own_part, own_mlp_in = lanes.fence(own_part, own_mlp_in)
            other_mlp_in = swap(own_mlp_in)
        elif step < chips:
            (own_part,) = lanes.fence(own_part)
    rows_back = lanes.rows()
    own_part, rows_back, own_down = lanes.fence(own_part, rows_back, own_down)
    resid = tokens_f + lanes.total(own_part)

    scale_two, norm_mid = norm_forward(resid, second_gain)
    norm_mid, own_down = fence(norm_mid, own_down)
    other_down = swap(own_down)
    rows_second = [norm_mid]
    hidden, gate_grads, up_grads, parts, outs = [], [], [], [], []
    sums = None
    for hop in range(chips):
        if hop < last:
            rows_second.append(line.ring(rows_second[hop]))
        if hop > 1:
            sums = line.ring(total_b)
        made = mlp_block(
            rows_second[hop], rows_back[hop], own_mlp_in, other_mlp_in, own_down, other_down
        )
        rows_second, made, sums = fence(rows_second, made, sums)
        for kept, value in zip((hidden, gate_grads, up_grads, parts, outs), made):
            kept.append(value)
        if hop:
            total = parts[hop] if sums is None else plus(parts[hop], sums)
            total_b = total.astype(bf16)
    sums = line.ring(total_b)
    [grads_gate], _ = weight_grad(gate_grads, rows_second, 1)
    [grads_down], _ = weight_grad(hidden, rows_back, 1)
    sums, grads_gate, grads_down, up_grads = fence(sums, grads_gate, grads_down, up_grads)
    mid_sum = plus(parts[0], sums)

    from_norm, gain_two = norm_backward(resid, scale_two, second_gain, mid_sum)
    resid_grad = out_grad + from_norm
    resid_grad_b = resid_grad.astype(bf16)
    resid_grad_b, up_grads, outs = fence(resid_grad_b, up_grads, outs)

    def back_block(rows):
        return dot_nt(rows, whole_out).reshape(2, seq_half, local_len, 2 * channels)

    def out_part(flag, left, right):
        return outs[left] if left == right else jnp.where(flag, outs[left], outs[right])

    lanes = Exchange(line, resid_grad_b)
    lanes.step(1, None)
    lanes.first(out_part)
    [grads_up], _ = weight_grad(up_grads, rows_second, 1)
    from_down, from_gate = swap(grads_down[1]), swap(grads_gate[1])
    grads_up, from_down, from_gate, outs = lanes.fence(grads_up, from_down, from_gate, outs)
    back_blocks = [back_block(resid_grad_b)]
    for step in range(2, chips + 1):
        lanes.step(step, out_part)
        if step == 2:
            part_down = join((grads_down[0], from_down))
            part_mlp_in = join((grads_gate[0], from_gate), slots=2)
            from_up = swap(grads_up[1])
            part_down, part_mlp_in, from_up, outs = lanes.fence(part_down, part_mlp_in, from_up, outs)
            grad_mlp_down = narrow_sum(part_down, 1)
        elif step == 3:
            part_mlp_in = join((grads_up[0], from_up), slots=2, slot=1, filled=(part_mlp_in,))
            if lanes.packed:
                back_blocks += [back_block(lanes.arrived(at)) for at in (1, 2)]
            part_mlp_in, back_blocks = lanes.fence(part_mlp_in, back_blocks)
            grad_mlp_in = narrow_sum(part_mlp_in, 1)
        elif step < chips:
            lanes.fence()
    if lanes.packed:
        back_blocks.append(back_block(lanes.arrived(3)))
    else:
        back_blocks += [back_block(rows) for rows in lanes.rows()[1:]]
    grads, small, gate_grads = mixer_backward(
        back_blocks, lanes.packed, saved, lengths, place, params[:4], gate_back, block_width
    )
    grad_rows = grads.reshape(-1, 4 * channels)
    part = row_dot(grad_rows, whole_in, 1, chips, bf16)
    part, grad_rows, small, gate_grads, mixed, grad_mlp_down = lanes.fence(
        part, grad_rows, small, gate_grads, mixed, grad_mlp_down
    )

    size = lax.axis_size("narrow")
    split = size // 2 + 1
    count = rate_weight.shape[0]

    def gate_rows(gates, sums):
        return jnp.concatenate((gates.reshape(-1, block_width), sums.reshape(-1, block_width)), axis=0)

    gate_mine = gate_rows(gate_grads[:count], small[:, :channels])
    gate_other = gate_rows(gate_grads[count:], small[:, channels:])
    moving = line.ring(part)
    grads_in, [gain_one] = weight_grad([grad_rows], rows_first, 2, weight=whole_in)
    [grads_out], _ = weight_grad([mixed.reshape(-1, 2 * channels)], lanes.rows(), 1)
    gate_sum = (gate_mine + swap(gate_other.astype(bf16)).astype(f32)).astype(bf16)
    gate_sum = paired_step(gate_sum, "narrow", 1)
    grads_in, grads_out, gain_one, moving, gate_sum, resid, grad_rows = fence(
        grads_in, grads_out, gain_one, moving, gate_sum, resid, grad_rows
    )
    for hop in range(2, chips):
        sent = row_dot(grad_rows, whole_in, hop, chips, bf16, (moving,))
        if hop == 2:
            sent, grads_in, grads_out, gain_one = fence(sent, grads_in, grads_out, gain_one)
        moving = line.ring(sent)
    part = row_dot(grad_rows, whole_in, 0, chips)
    parts = join(*[(own, swap(other)) for own, other in (*grads_in, grads_out)])
    gains = jnp.concatenate((gain_one / first_gain, gain_two[None]), axis=0)
    parts, gate_sum, gains = fence(parts, gate_sum, gains)
    gains = direct_sum(gains, "narrow")
    sum_proj = DirectSum(parts)
    sum_proj.send(range(1, split))
    part, parts, grad_mlp_in, gate_sum, resid, gains, sum_proj.got = fence(
        part, parts, grad_mlp_in, gate_sum, resid, gains, sum_proj.got
    )
    sum_proj.grad = parts
    sum_proj.send(range(split, size))
    output = by_position((resid + lanes.total(outs[0])).astype(bf16))
    gains = gains + swap(gains)
    moving, output, gains, sum_proj.got, gate_sum = fence(
        moving, output, gains, sum_proj.got, gate_sum
    )
    bit = 2
    while bit < size:
        gate_sum = paired_step(gate_sum, "narrow", bit)
        bit *= 2
    in_sum = plus(part, moving)
    from_norm, _ = norm_backward(tokens_f, scale_one, first_gain, in_sum)
    grad_tokens = (resid_grad + from_norm).astype(bf16)
    grad_tokens, gains, sum_proj.got = fence(grad_tokens, gains, sum_proj.got)
    gains = direct_sum(gains, "wide", 2)
    grad_proj = sum_proj.total()
    gate_sum = gate_sum.astype(f32)
    gate_grads = gate_sum[: count * 2 * block_width].reshape(count, 2, block_width, block_width)
    small = gate_sum[count * 2 * block_width :].reshape(8, channels)
    grad_mlp_in, grad_mlp_down = grad_mlp_in.astype(f32), grad_mlp_down.astype(f32)
    grad_proj_in = grad_proj[: 2 * channels].reshape(2, channels, -1)
    grad_proj_out = grad_proj[2 * channels :]
    grad_mlp_in = grad_mlp_in.reshape(2, mlp_in.shape[2], -1)
    return (
        output,
        by_position(grad_tokens),
        final_state,
        conv_state,
        gains[0],
        jnp.swapaxes(grad_proj_in, 1, 2),
        small[4:8],
        small[3],
        gate_grads[:, 0],
        small[0],
        gate_grads[:, 1],
        small[1],
        small[2] * decay_scale * jax.nn.sigmoid(-decay_param),
        grad_proj_out,
        gains[1],
        jnp.swapaxes(grad_mlp_in, 1, 2),
        grad_mlp_down,
    )


def solution(mesh):
    return jax.shard_map(
        body,
        mesh=mesh,
        in_specs=(
            P("narrow", "wide", None),
            P("narrow"),
            P("narrow", "wide", None),
            P(),
            P(None, "narrow", "wide"),
            P(None, "wide"),
            P("wide"),
            P("wide", None, None),
            P("wide"),
            P("wide", None, None),
            P("wide"),
            P("wide"),
            P("wide", "narrow"),
            P(),
            P(None, "narrow", "wide"),
            P("wide", "narrow"),
        ),
        out_specs=(
            P("narrow", "wide", None),
            P("narrow", "wide", None),
            P("narrow", "wide"),
            P("narrow", None, "wide"),
            P(),
            P(None, "narrow", "wide"),
            P(None, "wide"),
            P("wide"),
            P("wide", None, None),
            P("wide"),
            P("wide", None, None),
            P("wide"),
            P("wide"),
            P("wide", "narrow"),
            P(),
            P(None, "narrow", "wide"),
            P("wide", "narrow"),
        ),
        check_vma=False,
    )
```
